32 devices in a mesh: dp: 8 (over y, x, core), mp: 4 (over z).
Axes of the slice: x: 2, y: 2, z: 4, core: 2. Of those that a mesh axis runs over, the one named last changes fastest.
Arguments:
- tokens: bfloat16 [16384, 768], P(('dp', 'mp')), may hold values from -6 to 6
- segments: int32 [8, 2048], P('dp'), may hold values from -1 to 2048, as said below
- out_grad: bfloat16 [16384, 768], P(('dp', 'mp')), may hold values from -6 to 6
- align_grad: bfloat16 [16384, 1024], P(('dp', 'mp')), may hold values from -6 to 6
- first_gain: bfloat16 [768], P(('dp', 'mp')), may hold values from 0.5 to 1.5
- first_shift: bfloat16 [768], P(('dp', 'mp')), may hold values from -1.75 to 1.75
- joint_weight: bfloat16 [768, 2304], P(('dp', 'mp')), may hold values from -0.21875 to 0.21875
- query_bias: bfloat16 [768], P(('dp', 'mp')), may hold values from -3 to 3
- value_bias: bfloat16 [768], P(('dp', 'mp')), may hold values from -3 to 3
- output_weight: bfloat16 [768, 768], P(('dp', 'mp')), may hold values from -0.875 to 0.875
- output_bias: bfloat16 [768], P(('dp', 'mp')), may hold values from -1.75 to 1.75
- second_gain: bfloat16 [768], P(('dp', 'mp')), may hold values from 0.5 to 1.5
- second_shift: bfloat16 [768], P(('dp', 'mp')), may hold values from -1.75 to 1.75
- expand_bias: bfloat16 [3072], P(('dp', 'mp')), may hold values from -3 to 3
- reduce_bias: bfloat16 [768], P(('dp', 'mp')), may hold values from -1.75 to 1.75
- head_gain: bfloat16 [768], P(('dp', 'mp')), may hold values from 0.5 to 1.5
- head_shift: bfloat16 [768], P(('dp', 'mp')), may hold values from -1.75 to 1.75
- align_weight: bfloat16 [768, 1024], P(('dp', 'mp')), may hold values from -0.21875 to 0.21875
- align_bias: bfloat16 [1024], P(('dp', 'mp')), may hold values from -3 to 3
- expand_weight: bfloat16 [768, 3072], P('dp', 'mp'), may hold values from -0.21875 to 0.21875
- reduce_weight: bfloat16 [3072, 768], P('mp', 'dp'), may hold values from -0.109375 to 0.109375
Outputs:
- block_out: bfloat16 [16384, 768], P(('dp', 'mp'))
- align_out: bfloat16 [16384, 1024], P(('dp', 'mp'))
- tokens_grad: float32 [16384, 768], P(('dp', 'mp'))
- first_gain_grad: float32 [768], P(('dp', 'mp'))
- first_shift_grad: float32 [768], P(('dp', 'mp'))
- joint_weight_grad: float32 [768, 2304], P(('dp', 'mp'))
- query_bias_grad: float32 [768], P(('dp', 'mp'))
- value_bias_grad: float32 [768], P(('dp', 'mp'))
- output_weight_grad: float32 [768, 768], P(('dp', 'mp'))
- output_bias_grad: float32 [768], P(('dp', 'mp'))
- second_gain_grad: float32 [768], P(('dp', 'mp'))
- second_shift_grad: float32 [768], P(('dp', 'mp'))
- expand_bias_grad: float32 [3072], P(('dp', 'mp'))
- reduce_bias_grad: float32 [768], P(('dp', 'mp'))
- head_gain_grad: float32 [768], P(('dp', 'mp'))
- head_shift_grad: float32 [768], P(('dp', 'mp'))
- align_weight_grad: float32 [768, 1024], P(('dp', 'mp'))
- align_bias_grad: float32 [1024], P(('dp', 'mp'))
- expand_weight_grad: float32 [768, 3072], P('dp', 'mp')
- reduce_weight_grad: float32 [3072, 768], P('mp', 'dp')
The draws below stay inside these ranges and needn't reach their ends.
Inputs may be any that keep to these rules, and one draw needn't show every extreme that they name: `segments`: segment numbers never fall along a row; padding slots carry -1 and stand at the end of a row, every row having some; the last segment before the padding is numbered 2048 in every row; in every row one segment starts within the first 256 slots and ends after slot 1536.
All inputs are finite; a program needn't handle non-finite values.
Results may differ from the reference program's by a relative error of at most 0.014.
Values may be sent and summed in bfloat16 or wider, within the bound.
A program may use at most 192 MiB of HBM per device.

```python
import jax
import jax.numpy as jnp
from jax import lax

D = 768
H = 12
HD = 64
FF = 3072
AL = 1024
SEQ = 2048
SEQS = 8
TOKENS = 16384


def draw_segments(key, part):
    key = jax.random.fold_in(key, 11)
    key_pad, key_start, key_tail, key_break = jax.random.split(key, 4)
    padding = jax.random.randint(key_pad, (SEQS, 1), 1, max(2, SEQ // 8))
    start = jax.random.randint(key_start, (SEQS, 1), 0, max(1, SEQ // 8))
    tail = jax.random.randint(key_tail, (SEQS, 1), 0, max(1, SEQ // 16))
    finish = SEQ - padding - tail
    position = jnp.arange(SEQ, dtype=jnp.int32)[None, :]
    breaks = jax.random.randint(key_break, (SEQS, SEQ), 0, 16) == 0
    outside = (position < start) | (position > finish)
    heads = (position == 0) | (position == start) | (position == finish) | breaks & outside
    live = position < SEQ - padding
    numbers = jnp.cumsum(heads.astype(jnp.int32), axis=1) - 1
    last_number = jnp.max(jnp.where(live, numbers, 0), axis=1, keepdims=True)
    numbers = numbers + (SEQ - last_number)
    return jnp.where(live, numbers, -1).astype(jnp.int32)


def block_scale(key, dims, pieces, low, high):
    loudness, own = 1.0, jax.random.fold_in(key, 6)
    for dim, blocks in pieces:
        steps = jnp.exp(jax.random.uniform(jax.random.fold_in(own, dim), (blocks,), jnp.float32, low / len(pieces), high / len(pieces)))
        loudness = loudness * jnp.repeat(steps, dims[dim] // blocks).reshape([-1 if axis == dim else 1 for axis in range(len(dims))])
    return loudness


def noise(rng, shape, scale, bound, shards=(), held_as=jnp.bfloat16):
    result = jax.random.normal(rng, shape, jnp.float32) * scale
    if len(shards) > 0:
        result = block_scale(rng, shape, shards, -0.22, 0.18) * result
    return jnp.clip(result, min=-bound, max=bound).astype(held_as)


def setup_inputs(seed: int = 0) -> dict:
    key_list = jax.random.split(jax.random.key(seed), 22)
    tokens = noise(key_list[0], (TOKENS, D), 1.0, 6.0, ((0, 32),))
    segments = draw_segments(jax.random.fold_in(key_list[21], 71), 0)
    out_grad = noise(key_list[2], (TOKENS, D), 1.0, 6.0, ((0, 32),))
    align_grad = noise(key_list[3], (TOKENS, AL), 1.0, 6.0, ((0, 32),))
    first_gain = jnp.clip(1.0 + 0.1 * jax.random.normal(key_list[4], (D,), jnp.float32), 0.5, 1.5).astype(jnp.bfloat16)
    first_shift = noise(key_list[5], (D,), 0.3, 1.75, ((0, 32),))
    joint_weight = noise(key_list[6], (D, 3 * D), D ** -0.5, 0.21875, ((0, 32),))
    query_bias = noise(key_list[7], (D,), 0.5, 3.0, ((0, 32),))
    value_bias = noise(key_list[8], (D,), 0.5, 3.0, ((0, 32),))
    output_weight = noise(key_list[9], (D, D), (D // 16) ** -0.5, 0.875, ((0, 32),))
    output_bias = noise(key_list[10], (D,), 0.3, 1.75, ((0, 32),))
    second_gain = jnp.clip(1.0 + 0.1 * jax.random.normal(key_list[11], (D,), jnp.float32), 0.5, 1.5).astype(jnp.bfloat16)
    second_shift = noise(key_list[12], (D,), 0.3, 1.75, ((0, 32),))
    expand_bias = noise(key_list[13], (FF,), 0.5, 3.0, ((0, 32),))
    reduce_bias = noise(key_list[14], (D,), 0.3, 1.75, ((0, 32),))
    head_gain = jnp.clip(1.0 + 0.1 * jax.random.normal(key_list[15], (D,), jnp.float32), 0.5, 1.5).astype(jnp.bfloat16)
    head_shift = noise(key_list[16], (D,), 0.3, 1.75, ((0, 32),))
    align_weight = noise(key_list[17], (D, AL), D ** -0.5, 0.21875, ((0, 32),))
    align_bias = noise(key_list[18], (AL,), 0.5, 3.0, ((0, 32),))
    expand_weight = noise(key_list[19], (D, FF), D ** -0.5, 0.21875, ((0, 8), (1, 4)))
    reduce_weight = noise(key_list[20], (FF, D), FF ** -0.5, 0.109375, ((0, 4), (1, 8)))
    return dict(tokens=tokens, segments=segments, out_grad=out_grad, align_grad=align_grad, first_gain=first_gain, first_shift=first_shift, joint_weight=joint_weight, query_bias=query_bias, value_bias=value_bias, output_weight=output_weight, output_bias=output_bias, second_gain=second_gain, second_shift=second_shift, expand_bias=expand_bias, reduce_bias=reduce_bias, head_gain=head_gain, head_shift=head_shift, align_weight=align_weight, align_bias=align_bias, expand_weight=expand_weight, reduce_weight=reduce_weight)


EPSILON = 1e-06
NEG_FILL = -1000000000.0

@jax.custom_vjp
def low(v):
    return lax.optimization_barrier(v.astype(jnp.bfloat16)).astype(jnp.float32)

@jax.custom_vjp
def low_back(v):
    return v

def low_keep(v):
    return (low(v), None)

def low_pass(kept, grad):
    return (grad,)

def back_keep(v):
    return (v, None)

def back_low(kept, grad):
    return (low(grad),)
low.defvjp(low_keep, low_pass)
low_back.defvjp(back_keep, back_low)

def layer_norm(values, gain, shift):
    centre = values - lax.optimization_barrier(jnp.mean(values, axis=-1, keepdims=True))
    spread = lax.optimization_barrier(jnp.mean(centre * centre, axis=-1, keepdims=True))
    return centre * lax.rsqrt(spread + EPSILON) * gain + shift

def matmul(left, right):
    return jnp.dot(left, right, precision=lax.Precision.HIGHEST, preferred_element_type=jnp.float32)

def attention(queries, keys, values, segment_row):
    block_len = min(512, SEQ)
    query_blocks = queries.reshape(SEQ // block_len, block_len, H, HD)
    segment_blocks = segment_row.reshape(SEQ // block_len, block_len)
    scale = 1.0 / jnp.sqrt(jnp.float32(HD))

    @jax.checkpoint
    def one_block(item):
        block_queries, block_segments = item
        logits = jnp.einsum('qhd,khd->hqk', block_queries, keys, precision=lax.Precision.HIGHEST) * scale
        logits = low_back(logits)
        allowed = (block_segments[:, None] == segment_row[None, :])[None]
        logits = jnp.where(allowed, logits, NEG_FILL)
        weights = low(jax.nn.softmax(logits, axis=-1))
        return jnp.einsum('hqk,khd->qhd', weights, values, precision=lax.Precision.HIGHEST)
    attended = lax.map(one_block, (query_blocks, segment_blocks))
    return attended.reshape(SEQ, D)

def layer_forward(resid, segment_row, weights):
    first_gain, first_shift, joint_weight, query_bias, value_bias, output_weight, output_bias, second_gain, second_shift, expand_bias, reduce_bias, head_gain, head_shift, align_weight, align_bias, expand_weight, reduce_weight = weights
    normed_one = low(layer_norm(resid, first_gain, first_shift))
    joint_bias = jnp.concatenate([query_bias, jnp.zeros_like(query_bias), value_bias])
    projected = low(low_back(matmul(normed_one, joint_weight) + joint_bias))
    queries = projected[:, :D].reshape(SEQ, H, HD)
    keys = projected[:, D:2 * D].reshape(SEQ, H, HD)
    values = projected[:, 2 * D:].reshape(SEQ, H, HD)
    attended = low(low_back(attention(queries, keys, values, segment_row)))
    middle = resid + low_back(matmul(attended, output_weight) + output_bias)
    normed_two = low(layer_norm(middle, second_gain, second_shift))
    preactivation = low_back(matmul(normed_two, expand_weight) + expand_bias)
    activated = low(jax.nn.gelu(preactivation, approximate=False))
    block_out = middle + low_back(matmul(activated, reduce_weight) + reduce_bias)
    normed_three = low(layer_norm(block_out, head_gain, head_shift))
    align_out = low_back(matmul(normed_three, align_weight) + align_bias)
    return (block_out, align_out)

def reference(tokens, segments, out_grad, align_grad, first_gain, first_shift, joint_weight, query_bias, value_bias, output_weight, output_bias, second_gain, second_shift, expand_bias, reduce_bias, head_gain, head_shift, align_weight, align_bias, expand_weight, reduce_weight):
    params = tuple((weight.astype(jnp.float32) for weight in (first_gain, first_shift, joint_weight, query_bias, value_bias, output_weight, output_bias, second_gain, second_shift, expand_bias, reduce_bias, head_gain, head_shift, align_weight, align_bias, expand_weight, reduce_weight)))
    inputs_seq = tokens.astype(jnp.float32).reshape(SEQS, SEQ, D)
    outs_seq = out_grad.astype(jnp.float32).reshape(SEQS, SEQ, D)
    aligns_seq = align_grad.astype(jnp.float32).reshape(SEQS, SEQ, AL)

    def one_sequence(carry, item):
        resid, segment_row, cot_out, cot_align = item

        def forward(values, weights):
            return layer_forward(values, segment_row, weights)
        outputs, pullback = jax.vjp(forward, resid, params)
        back_in, back_weights = pullback((cot_out, cot_align))
        carry = tuple((total + grad for total, grad in zip(carry, back_weights)))
        return (carry, (outputs[0], outputs[1], back_in))
    starts = tuple((jnp.zeros_like(weight) for weight in params))
    totals, (blocks, aligns, inputs_grad) = lax.scan(one_sequence, starts, (inputs_seq, segments, outs_seq, aligns_seq))
    g_first_gain, g_first_shift, g_joint, g_query, g_value, g_output_w, g_output_b, g_second_gain, g_second_shift, g_expand_b, g_reduce_b, g_head_gain, g_head_shift, g_align_w, g_align_b, g_expand_w, g_reduce_w = totals
    return (blocks.reshape(TOKENS, D).astype(jnp.bfloat16), aligns.reshape(TOKENS, AL).astype(jnp.bfloat16), inputs_grad.reshape(TOKENS, D), g_first_gain, g_first_shift, g_joint, g_query, g_value, g_output_w, g_output_b, g_second_gain, g_second_shift, g_expand_b, g_reduce_b, g_head_gain, g_head_shift, g_align_w, g_align_b, g_expand_w, g_reduce_w)
```

```python
import functools

import jax
import jax.numpy as jnp
from jax import lax
from jax.experimental import pallas as pl
from jax.experimental.pallas import tpu as pltpu
from jax.sharding import PartitionSpec as P

H = 12
HD = 64
EPSILON = 1e-06
NEG_FILL = -1000000000.0
MESH = pl.DeviceIdType.MESH
VMEM_LIMIT = 56 << 20


def layer_norm(values, gain, shift):
    centre = values - jnp.mean(values, axis=-1, keepdims=True)
    spread = jnp.mean(centre * centre, axis=-1, keepdims=True)
    return centre * lax.rsqrt(spread + EPSILON) * gain + shift


def exact_gelu(values):
    return jax.nn.gelu(values, approximate=False)


def matmul(left, right):
    return jnp.dot(left, right, preferred_element_type=jnp.float32)


def left_product(left, right):
    return jnp.einsum("ti,to->io", left, right, preferred_element_type=jnp.float32)


def right_product(left, right):
    return jnp.einsum("to,io->ti", left, right, preferred_element_type=jnp.float32)


def column_sums(values):
    return jnp.sum(values.astype(jnp.float32), axis=0)


def nn(left, right):
    return lax.dot_general(
        left, right, (((1,), (0,)), ((), ())), preferred_element_type=jnp.float32
    )


def nt(left, right):
    return lax.dot_general(
        left, right, (((1,), (1,)), ((), ())), preferred_element_type=jnp.float32
    )


ANY = pl.BlockSpec(memory_space=pl.ANY)
VM = pl.BlockSpec(memory_space=pltpu.VMEM)


def line_gather_kernel(nz, own, out, send_right, send_left, recv, local_sem):
    dp, z = lax.axis_index("dp"), lax.axis_index("mp")
    has_left, has_right = z > 0, z < nz - 1
    left, right = jnp.maximum(z - 1, 0), jnp.minimum(z + 1, nz - 1)
    barrier = pltpu.get_barrier_semaphore()

    for off in range(1, nz):
        pl.semaphore_signal(
            barrier, inc=1, device_id=(dp, lax.rem(z + off, nz)), device_id_type=MESH
        )
    keep = pltpu.make_async_copy(own, out.at[z], local_sem)
    keep.start()

    pl.semaphore_wait(barrier, nz - 1)

    def to_right(step):
        chunk = jnp.maximum(z - step, 0)
        return pltpu.make_async_remote_copy(
            src_ref=own if step == 0 else out.at[chunk],
            dst_ref=out.at[chunk],
            send_sem=send_right.at[step],
            recv_sem=recv.at[chunk],
            device_id=(dp, right),
            device_id_type=MESH,
        )

    def to_left(step):
        chunk = jnp.minimum(z + step, nz - 1)
        return pltpu.make_async_remote_copy(
            src_ref=own if step == 0 else out.at[chunk],
            dst_ref=out.at[chunk],
            send_sem=send_left.at[step],
            recv_sem=recv.at[chunk],
            device_id=(dp, left),
            device_id_type=MESH,
        )

    for step in range(nz):
        if step > 0:

            @pl.when(z - step >= 0)
            def _():
                to_right(step).wait_recv()

            @pl.when(z + step <= nz - 1)
            def _():
                to_left(step).wait_recv()

        if step < nz - 1:

            @pl.when(has_right & (z - step >= 0))
            def _():
                to_right(step).start()

            @pl.when(has_left & (z + step <= nz - 1))
            def _():
                to_left(step).start()

    for step in range(nz - 1):

        @pl.when(has_right & (z - step >= 0))
        def _():
            to_right(step).wait_send()

        @pl.when(has_left & (z + step <= nz - 1))
        def _():
            to_left(step).wait_send()

    keep.wait()


def line_gather(own, nz, cid):
    return pl.pallas_call(
        functools.partial(line_gather_kernel, nz),
        out_shape=jax.ShapeDtypeStruct((nz,) + own.shape, own.dtype),
        in_specs=[ANY],
        out_specs=ANY,
        scratch_shapes=[
            pltpu.SemaphoreType.DMA((nz,)),
            pltpu.SemaphoreType.DMA((nz,)),
            pltpu.SemaphoreType.DMA((nz,)),
            pltpu.SemaphoreType.DMA,
        ],
        compiler_params=pltpu.CompilerParams(collective_id=cid, has_side_effects=True),
    )(own)


def line_exchange_kernel(nz, parts, out, send, recv, local_sem):
    dp, z = lax.axis_index("dp"), lax.axis_index("mp")
    barrier = pltpu.get_barrier_semaphore()
    for off in range(1, nz):
        pl.semaphore_signal(
            barrier, inc=1, device_id=(dp, lax.rem(z + off, nz)), device_id_type=MESH
        )
    keep = pltpu.make_async_copy(parts.at[z], out.at[z], local_sem)
    keep.start()
    pl.semaphore_wait(barrier, nz - 1)
    copies = []
    for off in range(1, nz):
        peer = lax.rem(z + off, nz)
        copy = pltpu.make_async_remote_copy(
            src_ref=parts.at[peer],
            dst_ref=out.at[z],
            send_sem=send.at[off],
            recv_sem=recv.at[off],
            device_id=(dp, peer),
            device_id_type=MESH,
        )
        copy.start()
        copies.append(copy)
    for copy in copies:
        copy.wait()
    keep.wait()


def line_exchange(parts, nz, cid):
    return pl.pallas_call(
        functools.partial(line_exchange_kernel, nz),
        out_shape=jax.ShapeDtypeStruct(parts.shape, parts.dtype),
        in_specs=[ANY],
        out_specs=ANY,
        scratch_shapes=[
            pltpu.SemaphoreType.DMA((nz,)),
            pltpu.SemaphoreType.DMA((nz,)),
            pltpu.SemaphoreType.DMA,
        ],
        compiler_params=pltpu.CompilerParams(collective_id=cid, has_side_effects=True),
    )(parts)


def joint_scatter_kernel(nd, nz, joint_cols, parts, out, vec, land, stage, zland, send, recv, zsend, zrecv):
    dp, z = lax.axis_index("dp"), lax.axis_index("mp")
    barrier = pltpu.get_barrier_semaphore()
    for off in range(1, nd):
        pl.semaphore_signal(
            barrier, inc=1, device_id=(lax.rem(dp + off, nd), z), device_id_type=MESH
        )
    for off in range(1, nz):
        pl.semaphore_signal(
            barrier, inc=1, device_id=(dp, lax.rem(z + off, nz)), device_id_type=MESH
        )
    pl.semaphore_wait(barrier, nd - 1 + nz - 1)
    copies = []
    for off in range(1, nd):
        peer = lax.rem(dp + off, nd)
        copy = pltpu.make_async_remote_copy(
            src_ref=parts.at[peer],
            dst_ref=land.at[off],
            send_sem=send.at[off],
            recv_sem=recv.at[off],
            device_id=(peer, z),
            device_id_type=MESH,
        )
        copy.start()
        copies.append(copy)
    total = parts[dp].astype(jnp.float32)
    for off, copy in zip(range(1, nd), copies):
        copy.wait_recv()
        total = total + land[off].astype(jnp.float32)
    rows = total.shape[0] // nz
    for j in range(nz):
        stage[j] = total[j * rows : (j + 1) * rows]
    zcopies = []
    for off in range(1, nz):
        peer = lax.rem(z + off, nz)
        copy = pltpu.make_async_remote_copy(
            src_ref=stage.at[peer],
            dst_ref=zland.at[z],
            send_sem=zsend.at[off],
            recv_sem=zrecv.at[off],
            device_id=(dp, peer),
            device_id_type=MESH,
        )
        copy.start()
        zcopies.append(copy)
    zland[z] = stage[z]
    for copy in zcopies:
        copy.wait_recv()
    sums = zland[0, :, joint_cols:]
    for j in range(1, nz):
        sums = sums + zland[j, :, joint_cols:]
    vec[...] = sums
    for j in range(nz):
        out[j] = zland[j, :, :joint_cols]
    for copy in copies:
        copy.wait_send()
    for copy in zcopies:
        copy.wait_send()


def joint_scatter(parts, joint_cols, nd, nz, cid):
    rows, cols = parts.shape[1:]
    own = rows // nz
    return pl.pallas_call(
        functools.partial(joint_scatter_kernel, nd, nz, joint_cols),
        out_shape=(
            jax.ShapeDtypeStruct((nz, own, joint_cols), jnp.float32),
            jax.ShapeDtypeStruct((own, cols - joint_cols), jnp.float32),
        ),
        in_specs=[VM],
        out_specs=(VM, VM),
        scratch_shapes=[
            pltpu.VMEM((nd, rows, cols), jnp.bfloat16),
            pltpu.VMEM((nz, own, cols), jnp.float32),
            pltpu.VMEM((nz, own, cols), jnp.float32),
            pltpu.SemaphoreType.DMA((nd,)),
            pltpu.SemaphoreType.DMA((nd,)),
            pltpu.SemaphoreType.DMA((nz,)),
            pltpu.SemaphoreType.DMA((nz,)),
        ],
        compiler_params=pltpu.CompilerParams(
            collective_id=cid, has_side_effects=True, vmem_limit_bytes=VMEM_LIMIT
        ),
    )(parts)


def attention_forward_kernel(qb, kc, nh, qkv, seg_row, seg_col, out, lse, bias, keys):
    seq = qkv.shape[1]
    for h in range(nh):
        keys[h] = qkv[(nh + h) * HD : (nh + h + 1) * HD, :].T

    def block(i, carry):
        start = pl.multiple_of(i * qb, qb)
        own_seg = seg_row[0:1, pl.ds(start, qb)]
        for c in range(0, seq, kc):
            bias[c : c + kc, :] = jnp.where(
                seg_col[c : c + kc, 0:1] == own_seg, 0.0, NEG_FILL
            )
        for h in range(nh):
            query = qkv[h * HD : (h + 1) * HD, pl.ds(start, qb)] * jnp.bfloat16(0.125)
            top = jnp.full((1, qb), -jnp.inf, jnp.float32)
            total = jnp.zeros((1, qb), jnp.float32)
            acc = jnp.zeros((HD, qb), jnp.float32)
            for c in range(0, seq, kc):
                score = nn(keys[h, c : c + kc, :], query) + bias[c : c + kc, :]
                new_top = jnp.maximum(top, jnp.max(score, axis=0, keepdims=True))
                weight = jnp.exp(score - new_top)
                fade = jnp.exp(top - new_top)
                total = total * fade + jnp.sum(weight, axis=0, keepdims=True)
                value = qkv[(2 * nh + h) * HD : (2 * nh + h + 1) * HD, c : c + kc]
                acc = acc * fade + nn(value, weight.astype(jnp.bfloat16))
                top = new_top
            out[h * HD : (h + 1) * HD, pl.ds(start, qb)] = acc / total
            lse[h : h + 1, pl.ds(start, qb)] = top + jnp.log(total)
        return carry

    lax.fori_loop(0, seq // qb, block, 0)


def attention_forward(qkv, seg_row, seg_col, nh):
    seq = qkv.shape[1]
    qb, kc = min(512, seq), min(1024, seq)
    return pl.pallas_call(
        functools.partial(attention_forward_kernel, qb, kc, nh),
        out_shape=(
            jax.ShapeDtypeStruct((nh * HD, seq), jnp.float32),
            jax.ShapeDtypeStruct((8, seq), jnp.float32),
        ),
        in_specs=[VM] * 3,
        out_specs=(VM, VM),
        scratch_shapes=[
            pltpu.VMEM((seq, qb), jnp.float32),
            pltpu.VMEM((nh, seq, HD), jnp.bfloat16),
        ],
        compiler_params=pltpu.CompilerParams(vmem_limit_bytes=VMEM_LIMIT),
    )(qkv, seg_row, seg_col)


def attention_backward_kernel(
    qb, kc, nh, qkv, grad, att, lse, seg_row, seg_col, out, bias, keys, values, key_grad, value_grad
):
    seq = qkv.shape[1]
    for h in range(nh):
        keys[h] = qkv[(nh + h) * HD : (nh + h + 1) * HD, :].T
        values[h] = qkv[(2 * nh + h) * HD : (2 * nh + h + 1) * HD, :].T
    key_grad[...] = jnp.zeros_like(key_grad)
    value_grad[...] = jnp.zeros_like(value_grad)

    def block(i, carry):
        start = pl.multiple_of(i * qb, qb)
        own_seg = seg_row[0:1, pl.ds(start, qb)]
        for c in range(0, seq, kc):
            bias[c : c + kc, :] = jnp.where(
                seg_col[c : c + kc, 0:1] == own_seg, 0.0, NEG_FILL
            )
        for h in range(nh):
            query = qkv[h * HD : (h + 1) * HD, pl.ds(start, qb)] * jnp.bfloat16(0.125)
            back = grad[h * HD : (h + 1) * HD, pl.ds(start, qb)]
            row_term = jnp.sum(
                back.astype(jnp.float32) * att[h * HD : (h + 1) * HD, pl.ds(start, qb)],
                axis=0,
                keepdims=True,
            )
            log_total = lse[h : h + 1, pl.ds(start, qb)]
            query_grad = jnp.zeros((HD, qb), jnp.float32)
            for c in range(0, seq, kc):
                chunk = slice(c, c + kc)
                score = nn(keys[h, chunk, :], query) + bias[chunk, :]
                weight = jnp.exp(score - log_total)
                value_grad[h, chunk, :] += nt(weight.astype(jnp.bfloat16), back)
                weight_grad = nn(values[h, chunk, :], back)
                score_grad = (weight * (weight_grad - row_term)).astype(jnp.bfloat16)
                key_grad[h, chunk, :] += nt(score_grad, query)
                query_grad = query_grad + nn(
                    qkv[(nh + h) * HD : (nh + h + 1) * HD, chunk], score_grad
                )
            out[h * HD : (h + 1) * HD, pl.ds(start, qb)] = (query_grad * 0.125).astype(
                jnp.bfloat16
            )
        return carry

    lax.fori_loop(0, seq // qb, block, 0)
    for h in range(nh):
        out[(nh + h) * HD : (nh + h + 1) * HD, :] = key_grad[h].T.astype(jnp.bfloat16)
        out[(2 * nh + h) * HD : (2 * nh + h + 1) * HD, :] = value_grad[h].T.astype(jnp.bfloat16)


def attention_backward(qkv, grad, att, lse, seg_row, seg_col, nh):
    seq = qkv.shape[1]
    qb, kc = min(512, seq), min(512, seq)
    return pl.pallas_call(
        functools.partial(attention_backward_kernel, qb, kc, nh),
        out_shape=jax.ShapeDtypeStruct((3 * nh * HD, seq), jnp.bfloat16),
        in_specs=[VM] * 6,
        out_specs=VM,
        scratch_shapes=[
            pltpu.VMEM((seq, qb), jnp.float32),
            pltpu.VMEM((nh, seq, HD), jnp.bfloat16),
            pltpu.VMEM((nh, seq, HD), jnp.bfloat16),
            pltpu.VMEM((nh, seq, HD), jnp.float32),
            pltpu.VMEM((nh, seq, HD), jnp.float32),
        ],
        compiler_params=pltpu.CompilerParams(vmem_limit_bytes=VMEM_LIMIT),
    )(qkv, grad, att, lse, seg_row, seg_col)


def local(
    tokens,
    segments,
    out_grad,
    align_grad,
    first_gain,
    first_shift,
    joint_weight,
    query_bias,
    value_bias,
    output_weight,
    output_bias,
    second_gain,
    second_shift,
    expand_bias,
    reduce_bias,
    head_gain,
    head_shift,
    align_weight,
    align_bias,
    expand_weight,
    reduce_weight,
):
    nd, nz = lax.axis_size("dp"), lax.axis_size("mp")
    n = nd * nz
    z = lax.axis_index("mp")
    rows, width = tokens.shape
    seq = rows * nz
    nh = H // nz
    own_cols = nh * HD
    f32, b16 = jnp.float32, jnp.bfloat16

    shards = [
        joint_weight,
        output_weight,
        align_weight,
        expand_weight,
        reduce_weight.T,
        first_gain,
        first_shift,
        query_bias,
        value_bias,
        output_bias,
        second_gain,
        second_shift,
        reduce_bias,
        head_gain,
        head_shift,
        expand_bias,
        align_bias,
    ]
    own_size = sum(s.size for s in shards)
    lines = -(-own_size // (16 * width)) * 16
    filler = jnp.zeros((lines * width - own_size,), b16)
    packed = jnp.concatenate([s.reshape(-1) for s in shards] + [filler])
    packed = lax.all_gather(packed.reshape(lines, width), ("dp", "mp"), axis=0, tiled=True)
    packed = packed.reshape(n, lines * width)
    full, at = [], 0
    for s in shards:
        full.append(packed[:, at : at + s.size].reshape((n,) + s.shape))
        at += s.size
    joint_full = full[0].reshape(width, 3 * width)
    output_full = full[1].reshape(width, width)
    align_full = full[2].reshape(width, -1)

    def spread(parts):
        a, b = parts.shape[1:]
        return parts.reshape(nd, nz, a, b).transpose(0, 2, 1, 3).reshape(nd * a, nz * b)

    expand_full = spread(full[3])
    reduce_full = spread(full[4])
    (
        gain_one,
        shift_one,
        bias_query,
        bias_value,
        bias_output,
        gain_two,
        shift_two,
        bias_reduce,
        gain_head,
        shift_head,
        bias_expand,
        bias_align,
    ) = (v.reshape(-1).astype(f32) for v in full[5:])

    x_all = line_gather(tokens, nz, 1).reshape(seq, width)
    normed_all = layer_norm(x_all.astype(f32), gain_one, shift_one).astype(b16)
    joint_own = lax.dynamic_slice_in_dim(
        joint_full.reshape(width, 3, width), z * own_cols, own_cols, axis=2
    ).reshape(width, 3 * own_cols)
    joint_bias = jnp.stack([bias_query, jnp.zeros_like(bias_query), bias_value])
    bias_own = lax.dynamic_slice_in_dim(joint_bias, z * own_cols, own_cols, axis=1).reshape(-1)
    qkv = (
        jnp.einsum("ic,ri->cr", joint_own, normed_all, preferred_element_type=f32)
        + bias_own[:, None]
    ).astype(b16)
    seg_row, seg_col = segments.reshape(1, seq), segments.reshape(seq, 1)
    att, lse = attention_forward(qkv, seg_row, seg_col, nh)
    att_parts = att.astype(b16).reshape(own_cols, nz, rows).transpose(1, 0, 2)
    attended = line_exchange(att_parts, nz, 2).reshape(width, rows)

    resid = tokens.astype(f32)
    middle = (
        resid
        + jnp.einsum("ir,io->ro", attended, output_full, preferred_element_type=f32)
        + bias_output
    )
    normed_two = layer_norm(middle, gain_two, shift_two).astype(b16)
    preactivation = matmul(normed_two, expand_full) + bias_expand
    activated = exact_gelu(preactivation).astype(b16)
    block_out = middle + right_product(activated, reduce_full) + bias_reduce
    normed_three = layer_norm(block_out, gain_head, shift_head).astype(b16)
    align_out = matmul(normed_three, align_full) + bias_align
    grad_align_w = left_product(normed_three, align_grad)
    grad_align_b = column_sums(align_grad)
    back_three = right_product(align_grad, align_full)
    _, norm_pull = jax.vjp(layer_norm, block_out, gain_head, shift_head)
    back_extra, grad_head_gain, grad_head_shift = norm_pull(back_three)
    back_block = out_grad.astype(f32) + back_extra
    back_feed = back_block.astype(b16)
    grad_reduce_b = column_sums(back_feed)
    grad_reduce_w = left_product(back_feed, activated)
    back_active = matmul(back_feed, reduce_full)
    _, gelu_pull = jax.vjp(exact_gelu, preactivation)
    back_pre = gelu_pull(back_active)[0].astype(b16)
    grad_expand_w = left_product(normed_two, back_pre)
    grad_expand_b = column_sums(back_pre)
    back_two = right_product(back_pre, expand_full)
    _, norm_pull = jax.vjp(layer_norm, middle, gain_two, shift_two)
    middle_extra, grad_second_gain, grad_second_shift = norm_pull(back_two)
    back_middle = back_block + middle_extra
    back_output = back_middle.astype(b16)
    grad_output_b = column_sums(back_output)
    grad_output_w = jnp.einsum("ir,ro->io", attended, back_output, preferred_element_type=f32)
    back_att = jnp.einsum(
        "io,ro->ir", output_full, back_output, preferred_element_type=f32
    ).astype(b16)

    def gather_order(grad, a, b):
        return grad.reshape(nd, a, nz, b).transpose(0, 2, 1, 3).reshape(n, a * b)

    pieces = [
        grad_output_w.reshape(n, -1),
        grad_align_w.reshape(n, -1),
        gather_order(grad_expand_w, *expand_weight.shape),
        gather_order(grad_reduce_w, *reduce_weight.shape[::-1]),
        grad_output_b.reshape(n, -1),
        grad_second_gain.reshape(n, -1),
        grad_second_shift.reshape(n, -1),
        grad_reduce_b.reshape(n, -1),
        grad_head_gain.reshape(n, -1),
        grad_head_shift.reshape(n, -1),
        grad_expand_b.reshape(n, -1),
        grad_align_b.reshape(n, -1),
    ]
    own_size = sum(p.shape[1] for p in pieces)
    lines = -(-own_size // (16 * width)) * 16
    pieces.append(jnp.zeros((n, lines * width - own_size), f32))
    scattered = lax.psum_scatter(
        jnp.concatenate([p.astype(b16) for p in pieces], axis=1).reshape(n * lines, width),
        ("dp", "mp"),
        scatter_dimension=0,
        tiled=True,
    ).reshape(-1)
    got, at = [], 0
    for p in pieces:
        got.append(scattered[at : at + p.shape[1]].astype(f32))
        at += p.shape[1]

    grad_att = line_exchange(back_att.reshape(nz, own_cols, rows), nz, 3)
    grad_att = grad_att.transpose(1, 0, 2).reshape(own_cols, seq)
    back_joint = attention_backward(qkv, grad_att, att, lse, seg_row, seg_col, nh)
    joint_parts = back_joint.reshape(3 * own_cols, nz, rows).transpose(1, 0, 2)
    back_rows = line_exchange(joint_parts, nz, 4)
    back_rows = (
        back_rows.reshape(nz, 3, own_cols, rows).transpose(1, 0, 2, 3).reshape(3 * width, rows)
    )
    back_one = jnp.einsum("cr,ic->ri", back_rows, joint_full, preferred_element_type=f32)
    _, norm_pull = jax.vjp(layer_norm, resid, gain_one, shift_one)
    input_extra, grad_first_gain, grad_first_shift = norm_pull(back_one)
    tokens_grad = back_middle + input_extra
    grad_joint = jnp.einsum("ri,cr->ic", normed_all, back_joint, preferred_element_type=f32)
    sums = jnp.sum(back_joint.astype(f32), axis=1).reshape(3, own_cols)
    zero = jnp.zeros((width,), f32)
    grad_query_b = lax.dynamic_update_slice_in_dim(zero, sums[0], z * own_cols, 0)
    grad_value_b = lax.dynamic_update_slice_in_dim(zero, sums[2], z * own_cols, 0)
    vectors = jnp.stack([grad_first_gain, grad_first_shift, grad_query_b, grad_value_b], axis=1)
    pad = -(3 * own_cols + 4) % 128
    parts = jnp.concatenate(
        [grad_joint, vectors, jnp.zeros((width, pad), f32)], axis=1
    ).astype(b16)
    joint_mine, vec_mine = joint_scatter(
        parts.reshape(nd, width // nd, -1), 3 * own_cols, nd, nz, 5
    )
    g_joint = (
        joint_mine.reshape(nz, -1, 3, own_cols).transpose(1, 2, 0, 3).reshape(-1, 3 * width)
    )
    return (
        block_out.astype(b16),
        align_out.astype(b16),
        tokens_grad,
        vec_mine[:, 0],
        vec_mine[:, 1],
        g_joint,
        vec_mine[:, 2],
        vec_mine[:, 3],
        got[0].reshape(output_weight.shape),
        got[4],
        got[5],
        got[6],
        got[10],
        got[7],
        got[8],
        got[9],
        got[1].reshape(align_weight.shape),
        got[11],
        got[2].reshape(expand_weight.shape),
        got[3].reshape(reduce_weight.shape[::-1]).T,
    )


def solution(mesh):
    both = P(("dp", "mp"))
    rows = P(("dp", "mp"), None)
    in_specs = (
        (rows, P("dp", None), rows, rows, both, both, rows, both, both, rows)
        + (both,) * 7
        + (rows, both, P("dp", "mp"), P("mp", "dp"))
    )
    out_specs = (
        (rows, rows, rows, both, both, rows, both, both, rows)
        + (both,) * 7
        + (rows, both, P("dp", "mp"), P("mp", "dp"))
    )
    return jax.shard_map(local, mesh=mesh, in_specs=in_specs, out_specs=out_specs, check_vma=False)
```

```python
import functools

import jax
import jax.numpy as jnp
from jax import lax
from jax.experimental import pallas as pl
from jax.experimental.pallas import tpu as pltpu
from jax.sharding import PartitionSpec as P

H = 12
HD = 64
EPSILON = 1e-06
NEG_FILL = -1000000000.0
MESH = pl.DeviceIdType.MESH
VMEM_LIMIT = 56 << 20


def layer_norm(values, gain, shift):
    centre = values - jnp.mean(values, axis=-1, keepdims=True)
    spread = jnp.mean(centre * centre, axis=-1, keepdims=True)
    return centre * lax.rsqrt(spread + EPSILON) * gain + shift


def exact_gelu(values):
    return jax.nn.gelu(values, approximate=False)


def matmul(left, right):
    return jnp.dot(left, right, preferred_element_type=jnp.float32)


def left_product(left, right):
    return jnp.einsum("ti,to->io", left, right, preferred_element_type=jnp.float32)


def right_product(left, right):
    return jnp.einsum("to,io->ti", left, right, preferred_element_type=jnp.float32)


def column_sums(values):
    return jnp.sum(values.astype(jnp.float32), axis=0)


def nn(left, right):
    return lax.dot_general(
        left, right, (((1,), (0,)), ((), ())), preferred_element_type=jnp.float32
    )


def nt(left, right):
    return lax.dot_general(
        left, right, (((1,), (1,)), ((), ())), preferred_element_type=jnp.float32
    )


ANY = pl.BlockSpec(memory_space=pl.ANY)
VM = pl.BlockSpec(memory_space=pltpu.VMEM)


def peer_flip(index, bit):
    return index + bit * (1 - 2 * (index // bit % 2))


def mask_flip(index, mask):
    bit = 1
    while bit <= mask:
        if mask & bit:
            index = peer_flip(index, bit)
        bit *= 2
    return index


def plane_masks(order, step):
    masks = [0]
    for bit in order[:step]:
        masks += [m ^ bit for m in masks]
    return masks


class Spread:
    def __init__(self, slot, own, full, wide, nd, nz, dp, z, sems):
        self.slot, self.own, self.full, self.wide = slot, own, full, wide
        self.nd, self.nz, self.dp, self.z = nd, nz, dp, z
        self.keep_sem, self.right_sem, self.left_sem, self.line_sem, self.send_sem, self.recv_sem = sems
        self.bits = [1 << b for b in range(1, nd.bit_length() - 1)]
        self.cut = nz // 2

    def order(self, half):
        return self.bits if half == 0 else self.bits[::-1]

    def chunk(self, j):
        if self.wide:
            cols = self.own.shape[1]
            return self.full.at[self.dp, :, pl.ds(pl.multiple_of(j * cols, 128), cols)]
        return self.full.at[self.dp, j]

    def block(self, half, mask):
        d = mask_flip(self.dp, mask)
        lo, hi = (0, self.cut) if half == 0 else (self.cut, self.nz)
        if self.wide:
            cols = self.own.shape[1]
            return self.full.at[d, :, pl.ds(lo * cols, (hi - lo) * cols)]
        return self.full.at[d, pl.ds(lo, hi - lo)]

    def keep(self):
        return pltpu.make_async_copy(self.own, self.chunk(self.z), self.keep_sem.at[self.slot])

    def _right(self, step):
        j = jnp.maximum(self.z - step, 0)
        return pltpu.make_async_remote_copy(
            src_ref=self.own if step == 0 else self.chunk(j),
            dst_ref=self.chunk(j),
            send_sem=self.right_sem.at[self.slot, step],
            recv_sem=self.line_sem.at[self.slot, j],
            device_id=(self.dp, jnp.minimum(self.z + 1, self.nz - 1)),
            device_id_type=MESH,
        )

    def _left(self, step):
        j = jnp.minimum(self.z + step, self.nz - 1)
        return pltpu.make_async_remote_copy(
            src_ref=self.own if step == 0 else self.chunk(j),
            dst_ref=self.chunk(j),
            send_sem=self.left_sem.at[self.slot, step],
            recv_sem=self.line_sem.at[self.slot, j],
            device_id=(self.dp, jnp.maximum(self.z - 1, 0)),
            device_id_type=MESH,
        )

    def line_start(self, step):
        if step >= self.nz - 1:
            return

        @pl.when((self.z < self.nz - 1) & (self.z - step >= 0))
        def _():
            self._right(step).start()

        @pl.when((self.z > 0) & (self.z + step <= self.nz - 1))
        def _():
            self._left(step).start()

    def line_wait(self, step):
        @pl.when(self.z - step >= 0)
        def _():
            self._right(step).wait_recv()

        @pl.when(self.z + step <= self.nz - 1)
        def _():
            self._left(step).wait_recv()

    def _plane(self, half, mask, bit):
        return pltpu.make_async_remote_copy(
            src_ref=self.block(half, mask),
            dst_ref=self.block(half, mask),
            send_sem=self.send_sem.at[self.slot, half, mask ^ bit],
            recv_sem=self.recv_sem.at[self.slot, half, mask ^ bit],
            device_id=(peer_flip(self.dp, bit), self.z),
            device_id_type=MESH,
        )

    def _arrival(self, half, mask, bit):
        return pltpu.make_async_remote_copy(
            src_ref=self.block(half, mask),
            dst_ref=self.block(half, mask),
            send_sem=self.send_sem.at[self.slot, half, mask],
            recv_sem=self.recv_sem.at[self.slot, half, mask],
            device_id=(peer_flip(self.dp, bit), self.z),
            device_id_type=MESH,
        )

    def plane_start(self, step):
        if step >= len(self.bits):
            return
        for half in range(2):
            order = self.order(half)
            for mask in plane_masks(order, step):
                self._plane(half, mask, order[step]).start()

    def plane_wait(self, step):
        for half in range(2):
            order = self.order(half)
            for mask in plane_masks(order, step):
                self._arrival(half, mask ^ order[step], order[step]).wait_recv()

    def _new_masks(self, half, step):
        order = self.order(half)
        return [0] if step < 0 else [m ^ order[step] for m in plane_masks(order, step)]

    def core_start(self, step):
        for half in range(2):
            for mask in self._new_masks(half, step):
                self._plane(half, mask, 1).start()

    def core_wait(self):
        for half in range(2):
            for mask in plane_masks(self.bits, len(self.bits)):
                self._arrival(half, mask ^ 1, 1).wait_recv()

    def sends_wait(self):
        for step in range(self.nz - 1):

            @pl.when((self.z < self.nz - 1) & (self.z - step >= 0))
            def _():
                self._right(step).wait_send()

            @pl.when((self.z > 0) & (self.z + step <= self.nz - 1))
            def _():
                self._left(step).wait_send()

        for half in range(2):
            order = self.order(half)
            for step in range(len(self.bits)):
                for mask in plane_masks(order, step):
                    self._plane(half, mask, order[step]).wait_send()
            for mask in plane_masks(order, len(self.bits)):
                self._plane(half, mask, 1).wait_send()


def greet(nd, nz, dp, z, line=True, plane=True):
    barrier = pltpu.get_barrier_semaphore()
    count = 0
    if line:
        for off in range(1, nz):
            pl.semaphore_signal(
                barrier, inc=1, device_id=(dp, lax.rem(z + off, nz)), device_id_type=MESH
            )
            count += 1
    if plane:
        bit = 1
        while bit < nd:
            pl.semaphore_signal(
                barrier, inc=1, device_id=(peer_flip(dp, bit), z), device_id_type=MESH
            )
            count += 1
            bit *= 2
    pl.semaphore_wait(barrier, count)


def forward_kernel(
    nd,
    nz,
    nh,
    x_own,
    vec_own,
    joint_own,
    wo_own,
    wa_own,
    w1_own,
    w2_own,
    seg_row,
    seg_col,
    vec_rows,
    joint,
    wo,
    wa,
    w1,
    w2,
    normed,
    qkv,
    att,
    lse,
    att_land,
    x_land,
    vec,
    window,
    vec_cols,
    weights,
    weights_t,
    wide,
    keys,
    bias,
    att_out,
    keep_sem,
    right_sem,
    left_sem,
    line_sem,
    send_sem,
    recv_sem,
    x_sem,
    x_right,
    x_left,
    x_recv,
    win_sem,
    att_send,
    att_recv,
):
    dp, z = lax.axis_index("dp"), lax.axis_index("mp")
    rows, width = x_own.shape
    seq = rows * nz
    n = nd * nz
    own_cols = nh * HD
    win_cols = window.shape[-1] // 3
    win = z * own_cols // 128 * 128
    shift = pl.multiple_of(z * own_cols - win, HD)
    win = pl.multiple_of(win, 128)
    f32, b16 = jnp.float32, jnp.bfloat16
    sems = (keep_sem, right_sem, left_sem, line_sem, send_sem, recv_sem)
    specs = [
        (vec_own, vec, False),
        (joint_own, joint, False),
        (wo_own, wo, False),
        (w1_own, w1, True),
        (wa_own, wa, False),
        (w2_own, w2, True),
    ]
    spreads = [Spread(i, *spec, nd, nz, dp, z, sems) for i, spec in enumerate(specs)]
    first, second, third = spreads[:2], spreads[2:4], spreads[4:]
    steps = len(spreads[0].bits)

    greet(nd, nz, dp, z)
    for s in spreads:
        s.keep().start()
    x_keep = pltpu.make_async_copy(x_own, x_land.at[z], x_sem)
    x_keep.start()
    for s in first + second:
        s.line_start(0)
    for step in range(1, nz):
        for s in first:
            s.line_wait(step)
            s.line_start(step)
    for s in first:
        s.keep().wait()
        s.plane_start(0)
        s.core_start(-1)

    def x_to_right(step):
        j = jnp.maximum(z - step, 0)
        return pltpu.make_async_remote_copy(
            src_ref=x_land.at[j],
            dst_ref=x_land.at[j],
            send_sem=x_right.at[step],
            recv_sem=x_recv.at[j],
            device_id=(dp, jnp.minimum(z + 1, nz - 1)),
            device_id_type=MESH,
        )

    def x_to_left(step):
        j = jnp.minimum(z + step, nz - 1)
        return pltpu.make_async_remote_copy(
            src_ref=x_land.at[j],
            dst_ref=x_land.at[j],
            send_sem=x_left.at[step],
            recv_sem=x_recv.at[j],
            device_id=(dp, jnp.maximum(z - 1, 0)),
            device_id_type=MESH,
        )

    def x_start(step):
        @pl.when((z < nz - 1) & (z - step >= 0))
        def _():
            x_to_right(step).start()

        @pl.when((z > 0) & (z + step <= nz - 1))
        def _():
            x_to_left(step).start()

    x_keep.wait()
    x_start(0)
    for step in range(1, nz):
        for s in second:
            s.line_wait(step)
            s.line_start(step)
    for s in second:
        s.keep().wait()
        s.plane_start(0)
        s.core_start(-1)
    for t in range(steps):
        for s in first:
            s.plane_wait(t)
            s.plane_start(t + 1)
            s.core_start(t)
    for s in first:
        s.core_wait()

    loads = []
    for p in range(3):
        load = pltpu.make_async_copy(
            joint.at[:, :, :, pl.ds(pl.multiple_of(p * width + win, 128), win_cols)],
            window.at[:, :, :, pl.ds(p * win_cols, win_cols)],
            win_sem.at[p],
        )
        load.start()
        loads.append(load)
    own = vec.shape[2]
    for d in range(nd):
        for j in range(nz):
            at = (d * nz + j) * own
            vec_cols[at : at + own, :] = vec[d, j].astype(f32)
    vec_t = vec_cols[...].T
    vec_rows[...] = vec_t[: vec_rows.shape[0]]
    for load in loads:
        load.wait()
    for d in range(nd):
        for j in range(nz):
            at = (d * nz + j) * own
            weights[at : at + own, :] = window[d, j].astype(f32)
    for p in range(3):
        cols = slice(p * win_cols, (p + 1) * win_cols)
        weights_t[cols, :] = weights[:, cols].T.astype(b16)
    gain, offset = vec_rows[0:1, :], vec_rows[1:2, :]
    bias_q = vec_cols[pl.ds(win, win_cols), 2:3]
    bias_v = vec_cols[pl.ds(win, win_cols), 3:4]

    def project(j):
        at = pl.multiple_of(j * rows, rows)
        chunk = layer_norm(x_land[j].astype(f32), gain, offset).astype(b16)
        normed[pl.ds(at, rows), :] = chunk
        for p in range(3):
            part = nt(weights_t[p * win_cols : (p + 1) * win_cols, :], chunk)
            if p == 0:
                part = part + bias_q
            if p == 2:
                part = part + bias_v
            wide[p * win_cols : (p + 1) * win_cols, pl.ds(at, rows)] = part.astype(b16)

    project(z)
    for s in second:
        s.plane_wait(0)
        s.plane_start(1)
        s.core_start(0)

    def arrivals(step, carry):
        @pl.when(z - step >= 0)
        def _():
            x_to_right(step).wait_recv()

        @pl.when(z + step <= nz - 1)
        def _():
            x_to_left(step).wait_recv()

        @pl.when(step < nz - 1)
        def _():
            x_start(step)

        @pl.when(step == nz - 2)
        def _():
            for s in third:
                s.line_start(0)

        @pl.when(z - step >= 0)
        def _():
            project(z - step)

        @pl.when(z + step <= nz - 1)
        def _():
            project(z + step)

        return carry

    lax.fori_loop(1, nz, arrivals, 0)
    for t in range(1, steps):
        for s in second:
            s.plane_wait(t)
            s.plane_start(t + 1)
            s.core_start(t)
    for h in range(nh):
        keys[h] = wide[pl.ds(win_cols + shift + h * HD, HD), :].T
    for p in range(3):
        qkv[p * own_cols : (p + 1) * own_cols, :] = wide[pl.ds(p * win_cols + shift, own_cols), :]
    kc = min(1024, seq)

    def att_copy(to, slot):
        return pltpu.make_async_remote_copy(
            src_ref=att_out.at[to],
            dst_ref=att_land.at[z],
            send_sem=att_send.at[slot],
            recv_sem=att_recv.at[slot],
            device_id=(dp, to),
            device_id_type=MESH,
        )

    def block(k, carry):
        to = lax.rem(z + 1 + k, nz)
        start = pl.multiple_of(to * rows, rows)
        own_seg = seg_row[0:1, pl.ds(start, rows)]
        for c in range(0, seq, kc):
            bias[c : c + kc, :] = jnp.where(
                seg_col[c : c + kc, 0:1] == own_seg, 0.0, NEG_FILL
            )
        for h in range(nh):
            query = qkv[h * HD : (h + 1) * HD, pl.ds(start, rows)] * jnp.bfloat16(0.125)
            top = jnp.full((1, rows), -jnp.inf, f32)
            total = jnp.zeros((1, rows), f32)
            acc = jnp.zeros((HD, rows), f32)
            for c in range(0, seq, kc):
                score = nn(keys[h, c : c + kc, :], query) + bias[c : c + kc, :]
                new_top = jnp.maximum(top, jnp.max(score, axis=0, keepdims=True))
                weight = jnp.exp(score - new_top)
                fade = jnp.exp(top - new_top)
                total = total * fade + jnp.sum(weight, axis=0, keepdims=True)
                value = qkv[2 * own_cols + h * HD : 2 * own_cols + (h + 1) * HD, c : c + kc]
                acc = acc * fade + nn(value, weight.astype(b16))
                top = new_top
            acc = acc / total
            att[h * HD : (h + 1) * HD, pl.ds(start, rows)] = acc
            att_out[to, h * HD : (h + 1) * HD, :] = acc.astype(b16)
            lse[h : h + 1, pl.ds(start, rows)] = top + jnp.log(total)

        @pl.when(k < nz - 1)
        def _():
            att_copy(to, k).start()

        for step in range(1, nz):

            @pl.when(k == step - 1)
            def _():
                for s in third:
                    s.line_wait(step)
                    s.line_start(step)
                    if step == nz - 1:
                        s.keep().wait()
                        s.plane_start(0)
                        s.core_start(-1)

        return carry

    lax.fori_loop(0, nz, block, 0)
    att_keep = pltpu.make_async_copy(att_out.at[z], att_land.at[z], x_sem)
    att_keep.start()
    for t in range(steps):
        for s in third:
            s.plane_wait(t)
            s.plane_start(t + 1)
            s.core_start(t)
    for s in second + third:
        s.core_wait()
    att_keep.wait()
    for k in range(nz - 1):
        att_copy(lax.rem(z + 1 + k, nz), k).wait()
    for step in range(nz - 1):

        @pl.when((z < nz - 1) & (z - step >= 0))
        def _():
            x_to_right(step).wait_send()

        @pl.when((z > 0) & (z + step <= nz - 1))
        def _():
            x_to_left(step).wait_send()

    for s in spreads:
        s.sends_wait()


def forward_call(x, vec, joint, wo, wa, w1, w2, seg_row, seg_col, nd, nz, nh, cid):
    rows, width = x.shape
    seq, own_cols = rows * nz, nh * HD
    win_cols = -(-(own_cols + HD) // 128) * 128
    own = joint.shape[0]
    f32, b16 = jnp.float32, jnp.bfloat16
    S = jax.ShapeDtypeStruct
    na = 6
    return pl.pallas_call(
        functools.partial(forward_kernel, nd, nz, nh),
        out_shape=(
            S((16, width), f32),
            S((nd, nz) + joint.shape, b16),
            S((nd, nz) + wo.shape, b16),
            S((nd, nz) + wa.shape, b16),
            S((nd, w1.shape[0], nz * w1.shape[1]), b16),
            S((nd, w2.shape[0], nz * w2.shape[1]), b16),
            S((seq, width), b16),
            S((3 * own_cols, seq), b16),
            S((own_cols, seq), f32),
            S((8, seq), f32),
            S((nz, own_cols, rows), b16),
        ),
        in_specs=[ANY] * 7 + [VM] * 2,
        out_specs=(VM, ANY, ANY, ANY, ANY, ANY, VM, VM, VM, VM, ANY),
        scratch_shapes=[
            pltpu.VMEM((nz, rows, width), b16),
            pltpu.VMEM((nd, nz) + vec.shape, b16),
            pltpu.VMEM((nd, nz, own, 3 * win_cols), b16),
            pltpu.VMEM((width, vec.shape[1]), f32),
            pltpu.VMEM((width, 3 * win_cols), f32),
            pltpu.VMEM((3 * win_cols, width), b16),
            pltpu.VMEM((3 * win_cols, seq), b16),
            pltpu.VMEM((nh, seq, HD), b16),
            pltpu.VMEM((seq, rows), f32),
            pltpu.VMEM((nz, own_cols, rows), b16),
            pltpu.SemaphoreType.DMA((na,)),
            pltpu.SemaphoreType.DMA((na, nz)),
            pltpu.SemaphoreType.DMA((na, nz)),
            pltpu.SemaphoreType.DMA((na, nz)),
            pltpu.SemaphoreType.DMA((na, 2, nd)),
            pltpu.SemaphoreType.DMA((na, 2, nd)),
            pltpu.SemaphoreType.DMA,
            pltpu.SemaphoreType.DMA((nz,)),
            pltpu.SemaphoreType.DMA((nz,)),
            pltpu.SemaphoreType.DMA((nz,)),
            pltpu.SemaphoreType.DMA((3,)),
            pltpu.SemaphoreType.DMA((nz,)),
            pltpu.SemaphoreType.DMA((nz,)),
        ],
        compiler_params=pltpu.CompilerParams(
            collective_id=cid, has_side_effects=True, vmem_limit_bytes=VMEM_LIMIT
        ),
    )(x, vec, joint, wo, wa, w1, w2, seg_row, seg_col)


class Reduce:
    def __init__(self, slot, part, acc, land, plane, line, wide, nd, nz, dp, z, sems):
        self.slot, self.part, self.acc, self.land, self.plane, self.line = slot, part, acc, land, plane, line
        self.wide, self.nd, self.nz, self.dp, self.z = wide, nd, nz, dp, z
        self.load_sem, self.core_out, self.core_in, self.plane_out, self.plane_in, self.line_out, self.line_in = sems
        self.bits = [1 << b for b in range(1, nd.bit_length() - 1)]
        self.masks = plane_masks(self.bits, len(self.bits))
        self.cut = nz // 2
        self.cols = acc.shape[-1] // nz if wide else acc.shape[-1]

    def order(self, half):
        return self.bits if half == 0 else self.bits[::-1]

    def span(self, half):
        return (0, self.cut) if half == 0 else (self.cut, self.nz)

    def region(self, ref, i, half):
        lo, hi = self.span(half)
        if self.wide:
            return ref.at[i, :, pl.ds(lo * self.cols, (hi - lo) * self.cols)]
        return ref.at[i, pl.ds(lo, hi - lo)]

    def chunk(self, ref, i, j):
        if self.wide:
            at = j * self.cols
            at = at if isinstance(at, int) else pl.multiple_of(at, 128)
            return ref.at[i, :, pl.ds(at, self.cols)]
        return ref.at[i, j]

    def slots(self, half, step):
        order, base = self.order(half), 0
        for t in range(step):
            base += 1 << (len(order) - 1 - t)
        rest = plane_masks(order[step + 1 :], len(order) - step - 1)
        return [(m, base + k) for k, m in enumerate(rest)]

    def _load(self, m):
        return pltpu.make_async_copy(
            self.part.at[mask_flip(self.dp, m)], self.acc.at[m >> 1], self.load_sem.at[self.slot, m >> 1]
        )

    def _core(self, m):
        return pltpu.make_async_remote_copy(
            src_ref=self.part.at[mask_flip(self.dp, m ^ 1)],
            dst_ref=self.land.at[m >> 1],
            send_sem=self.core_out.at[self.slot, m >> 1],
            recv_sem=self.core_in.at[self.slot, m >> 1],
            device_id=(peer_flip(self.dp, 1), self.z),
            device_id_type=MESH,
        )

    def core_start(self):
        for m in self.masks:
            self._core(m).start()
        for m in self.masks:
            self._load(m).start()

    def _add(self, i, source, k, half):
        lo, hi = self.span(half)

        def step(j, carry):
            to, more = self.chunk(self.acc, i, j), self.chunk(source, k, j)
            to[...] = (to[...].astype(jnp.float32) + more[...].astype(jnp.float32)).astype(to.dtype)
            return carry

        lax.fori_loop(lo, hi, step, 0)

    def core_add(self):
        for m in self.masks:
            self._load(m).wait()
            self._core(m).wait_recv()
            for half in range(2):
                self._add(m >> 1, self.land, m >> 1, half)

    def _plane(self, half, step, m, place):
        bit = self.order(half)[step]
        return pltpu.make_async_remote_copy(
            src_ref=self.region(self.acc, (m ^ bit) >> 1, half),
            dst_ref=self.region(self.plane, place, half),
            send_sem=self.plane_out.at[self.slot, half, place],
            recv_sem=self.plane_in.at[self.slot, half, place],
            device_id=(peer_flip(self.dp, bit), self.z),
            device_id_type=MESH,
        )

    def plane_start(self, step):
        if step < len(self.bits):
            for half in range(2):
                for m, place in self.slots(half, step):
                    self._plane(half, step, m, place).start()

    def plane_add(self, step):
        for half in range(2):
            for m, place in self.slots(half, step):
                self._plane(half, step, m, place).wait_recv()
                self._add(m >> 1, self.plane, place, half)

    def _line(self, off):
        to = lax.rem(self.z + off, self.nz)
        return pltpu.make_async_remote_copy(
            src_ref=self.chunk(self.acc, 0, to),
            dst_ref=self.line.at[off],
            send_sem=self.line_out.at[self.slot, off],
            recv_sem=self.line_in.at[self.slot, off],
            device_id=(self.dp, to),
            device_id_type=MESH,
        )

    def line_start(self):
        for off in range(1, self.nz):
            self._line(off).start()

    def line_wait(self):
        for off in range(1, self.nz):
            self._line(off).wait_recv()

    def line_sum(self):
        self.line_wait()
        total = self.chunk(self.acc, 0, self.z)[...].astype(jnp.float32)
        for off in range(1, self.nz):
            total = total + self.line[off].astype(jnp.float32)
        return total

    def sends_wait(self):
        for m in self.masks:
            self._core(m).wait_send()
        for half in range(2):
            for step in range(len(self.bits)):
                for m, place in self.slots(half, step):
                    self._plane(half, step, m, place).wait_send()
        for off in range(1, self.nz):
            self._line(off).wait_send()


def backward_kernel(
    nd,
    nz,
    nh,
    grad_parts,
    part_wo,
    part_wa,
    part_w1,
    part_w2,
    qkv,
    att,
    lse,
    seg_row,
    seg_lanes,
    normed,
    joint_full,
    x_own,
    base,
    vec_in,
    tokens_grad,
    out_joint,
    out_wo,
    out_wa,
    out_w1,
    out_w2,
    out_vec,
    grad_land,
    keys,
    values,
    key_grad,
    value_grad,
    turned,
    staged,
    rows_land,
    part_joint,
    bias_cols,
    vec_stage,
    vec_land,
    vec_line,
    *rest,
):
    na = 5
    buffers = [rest[4 * a : 4 * a + 4] for a in range(na)]
    (
        load_sem,
        core_out,
        core_in,
        plane_out,
        plane_in,
        line_out,
        line_in,
        grad_out,
        grad_in,
        row_out,
        row_in,
        vec_out,
        vec_in_sem,
        own_sem,
    ) = rest[4 * na :]
    dp, z = lax.axis_index("dp"), lax.axis_index("mp")
    rows, width = x_own.shape
    seq = rows * nz
    own_cols = nh * HD
    f32, b16 = jnp.float32, jnp.bfloat16
    sems = (load_sem, core_out, core_in, plane_out, plane_in, line_out, line_in)
    parts = [(part_w2, True), (part_w1, True), (part_wa, False), (part_wo, False), (part_joint, False)]
    reduces = [
        Reduce(a, part, *buffers[a], wide, nd, nz, dp, z, sems) for a, (part, wide) in enumerate(parts)
    ]
    big, joint = reduces[:4], reduces[4]
    steps = len(joint.bits)

    greet(nd, nz, dp, z)

    def grad_copy(h, off):
        to = lax.rem(z + off, nz)
        return pltpu.make_async_remote_copy(
            src_ref=grad_parts.at[to, pl.ds(h * HD, HD)],
            dst_ref=grad_land.at[z, pl.ds(h * HD, HD)],
            send_sem=grad_out.at[h, off],
            recv_sem=grad_in.at[h, off],
            device_id=(dp, to),
            device_id_type=MESH,
        )

    grad_own = pltpu.make_async_copy(grad_parts.at[z], grad_land.at[z], own_sem)
    grad_own.start()
    for h in range(nh):
        for off in range(1, nz):
            grad_copy(h, off).start()
    for r in big:
        r.core_start()
    for h in range(nh):
        keys[h] = qkv[own_cols + h * HD : own_cols + (h + 1) * HD, :].T
        values[h] = qkv[2 * own_cols + h * HD : 2 * own_cols + (h + 1) * HD, :].T
    bias_cols[...] = jnp.zeros_like(bias_cols)
    kc = min(512, seq)

    def row_copy(h, off):
        to = lax.rem(z + off, nz)
        return pltpu.make_async_remote_copy(
            src_ref=staged.at[to, :, pl.ds(h * HD, HD)],
            dst_ref=rows_land.at[:, z, pl.ds(h * HD, HD)],
            send_sem=row_out.at[h, off],
            recv_sem=row_in.at[h, off],
            device_id=(dp, to),
            device_id_type=MESH,
        )

    def chores(u):
        if u == 1:
            big[0].core_add()
            big[0].plane_start(0)
        if u == 2:
            big[1].core_add()
            big[1].plane_start(0)
        if u == 3:
            for r in big[2:]:
                r.core_add()
                r.plane_start(0)
        if u == 5:
            big[0].plane_add(0)
            big[0].plane_start(1)
        if u == 8:
            big[1].plane_add(0)
            big[1].plane_start(1)
        if u == 10:
            for r in big[2:]:
                r.plane_add(0)
                r.plane_start(1)

    grad_own.wait()
    for h in range(nh):
        for off in range(1, nz):
            grad_copy(h, off).wait_recv()
        key_grad[...] = jnp.zeros_like(key_grad)
        value_grad[...] = jnp.zeros_like(value_grad)

        def block(i, carry):
            start = pl.multiple_of(i * rows, rows)
            own_seg = seg_row[0:1, pl.ds(start, rows)]
            query = qkv[h * HD : (h + 1) * HD, pl.ds(start, rows)] * jnp.bfloat16(0.125)
            back = grad_land[i, h * HD : (h + 1) * HD, :]
            row_term = jnp.sum(
                back.astype(f32) * att[h * HD : (h + 1) * HD, pl.ds(start, rows)],
                axis=0,
                keepdims=True,
            )
            log_total = lse[h : h + 1, pl.ds(start, rows)]
            query_grad = jnp.zeros((HD, rows), f32)
            for c in range(0, seq, kc):
                chunk = slice(c, c + kc)
                lanes = seg_lanes[chunk, :]
                allowed = jnp.concatenate(
                    [lanes == own_seg[:, k : k + 128] for k in range(0, rows, 128)], axis=1
                )
                score = nn(keys[h, chunk, :], query)
                weight = jnp.where(allowed, jnp.exp(score - log_total), 0.0)
                value_grad[chunk, :] += nt(weight.astype(b16), back)
                weight_grad = nn(values[h, chunk, :], back)
                score_grad = (weight * (weight_grad - row_term)).astype(b16)
                key_grad[chunk, :] += nt(score_grad, query)
                query_grad = query_grad + nn(
                    qkv[own_cols + h * HD : own_cols + (h + 1) * HD, chunk], score_grad
                )
            staged[i, 0, h * HD : (h + 1) * HD, :] = (query_grad * 0.125).astype(b16)
            for b in range(nz):
                u = h * nz + b

                @pl.when(i == b)
                def _():
                    chores(u)

            return carry

        lax.fori_loop(0, nz, block, 0)
        for p, source in ((1, key_grad), (2, value_grad)):
            turned[...] = source[...].T
            for j in range(nz):
                staged[j, p, h * HD : (h + 1) * HD, :] = turned[:, j * rows : (j + 1) * rows].astype(b16)
        for off in range(1, nz):
            row_copy(h, off).start()
        rows_land[:, z, h * HD : (h + 1) * HD, :] = staged[z, :, h * HD : (h + 1) * HD, :]
        at = pl.ds(pl.multiple_of(z * own_cols + h * HD, HD), HD)
        for col, p in ((0, 0), (1, 2)):
            total = jnp.zeros((HD, 1), f32)
            for j in range(nz):
                total = total + jnp.sum(
                    staged[j, p, h * HD : (h + 1) * HD, :].astype(f32), axis=1, keepdims=True
                )
            bias_cols[at, col : col + 1] = total

    grad_t = jnp.zeros((3 * own_cols, width), f32)
    for j in range(nz):
        grad_t = grad_t + nn(
            staged[j].reshape(3 * own_cols, rows), normed[j * rows : (j + 1) * rows, :]
        )
    grad_joint = grad_t.T
    own = part_joint.shape[2]
    for d in range(nd):
        for j in range(nz):
            at = (d * nz + j) * own
            part_joint[d, j] = grad_joint[at : at + own, :].astype(b16)
    joint.core_start()
    for t in range(1, steps):
        for r in big:
            r.plane_add(t)
            r.plane_start(t + 1)
    for r in big:
        r.line_start()
    joint.core_add()
    joint.plane_start(0)
    for t in range(steps):
        joint.plane_add(t)
        joint.plane_start(t + 1)
    joint.line_start()

    for h in range(nh):
        for off in range(1, nz):
            row_copy(h, off).wait_recv()
    back_t = nn(joint_full[...], rows_land[...].reshape(3 * width, rows))
    back = back_t.T
    gain = vec_in[0:1, :]
    x = x_own[...].astype(f32)
    centre = x - jnp.mean(x, axis=-1, keepdims=True)
    inverse = lax.rsqrt(jnp.mean(centre * centre, axis=-1, keepdims=True) + EPSILON)
    unit = centre * inverse
    scaled = back * gain
    tokens_grad[...] = base[...] + inverse * (
        scaled
        - jnp.mean(scaled, axis=-1, keepdims=True)
        - unit * jnp.mean(scaled * unit, axis=-1, keepdims=True)
    )
    bias_rows = bias_cols[...].T
    vec_stage[0] = vec_in[...]
    vec_stage[0, 0:1, :] = jnp.sum(back * unit, axis=0, keepdims=True)
    vec_stage[0, 1:2, :] = jnp.sum(back, axis=0, keepdims=True)
    vec_stage[0, 2:4, :] = bias_rows[0:2, :]
    bits = [1] + joint.bits

    def vec_copy(t):
        return pltpu.make_async_remote_copy(
            src_ref=vec_stage.at[t],
            dst_ref=vec_land.at[t],
            send_sem=vec_out.at[t],
            recv_sem=vec_in_sem.at[t],
            device_id=(peer_flip(dp, bits[t]), z),
            device_id_type=MESH,
        )

    def vec_line_copy(off):
        return pltpu.make_async_remote_copy(
            src_ref=vec_stage.at[len(bits)],
            dst_ref=vec_line.at[off],
            send_sem=vec_out.at[len(bits) + off],
            recv_sem=vec_in_sem.at[len(bits) + off],
            device_id=(dp, lax.rem(z + off, nz)),
            device_id_type=MESH,
        )

    for t in range(len(bits)):
        vec_copy(t).start()
        vec_copy(t).wait_recv()
        vec_stage[t + 1] = vec_stage[t] + vec_land[t]
    for off in range(1, nz):
        vec_line_copy(off).start()
    for r, out in zip(big, (out_w2, out_w1, out_wa, out_wo)):
        out[...] = r.line_sum()
    joint.line_wait()
    out_joint[z] = joint.acc[0, z].astype(f32)
    for off in range(1, nz):
        out_joint[lax.rem(z - off + nz, nz)] = joint.line[off].astype(f32)
    total = vec_stage[len(bits)]
    for off in range(1, nz):
        vec_line_copy(off).wait_recv()
        total = total + vec_line[off]
    out_vec[...] = total
    for t in range(len(bits)):
        vec_copy(t).wait_send()
    for off in range(1, nz):
        vec_line_copy(off).wait_send()
        for h in range(nh):
            grad_copy(h, off).wait_send()
            row_copy(h, off).wait_send()
    for r in reduces:
        r.sends_wait()


def backward_call(
    grad_parts, wo, wa, w1, w2, qkv, att, lse, seg_row, seg_lanes, normed, joint_full, x_own, base, vec_in, nd, nz, nh, cid
):
    rows, width = x_own.shape
    seq, own_cols = rows * nz, nh * HD
    own = width // (nd * nz)
    f32, b16 = jnp.float32, jnp.bfloat16
    S, D = jax.ShapeDtypeStruct, pltpu.SemaphoreType.DMA
    joint_shape = (nd, nz, own, 3 * own_cols)
    held = []
    for shape, wide in ((w2.shape, True), (w1.shape, True), (wa.shape, False), (wo.shape, False), (joint_shape, False)):
        piece = shape[1:]
        line = (nz, piece[0], piece[1] // nz) if wide else piece
        held += [
            pltpu.VMEM((nd // 2,) + piece, b16),
            pltpu.VMEM((nd // 2,) + piece, b16),
            pltpu.VMEM((max(nd // 2 - 1, 1),) + piece, b16),
            pltpu.VMEM(line, b16),
        ]
    na, nb = 5, nd.bit_length() - 1
    return pl.pallas_call(
        functools.partial(backward_kernel, nd, nz, nh),
        out_shape=(
            S((rows, width), f32),
            S((nz, own, 3 * own_cols), f32),
            S(wo.shape[2:], f32),
            S(wa.shape[2:], f32),
            S((w1.shape[1], w1.shape[2] // nz), f32),
            S((w2.shape[1], w2.shape[2] // nz), f32),
            S(vec_in.shape, f32),
        ),
        in_specs=[ANY] * 5 + [VM] * 10,
        out_specs=(VM,) * 7,
        scratch_shapes=[
            pltpu.VMEM((nz, own_cols, rows), b16),
            pltpu.VMEM((nh, seq, HD), b16),
            pltpu.VMEM((nh, seq, HD), b16),
            pltpu.VMEM((seq, HD), f32),
            pltpu.VMEM((seq, HD), f32),
            pltpu.VMEM((HD, seq), f32),
            pltpu.VMEM((nz, 3, own_cols, rows), b16),
            pltpu.VMEM((3, nz, own_cols, rows), b16),
            pltpu.VMEM(joint_shape, b16),
            pltpu.VMEM((width, 128), f32),
            pltpu.VMEM((nb + 1,) + vec_in.shape, f32),
            pltpu.VMEM((nb,) + vec_in.shape, f32),
            pltpu.VMEM((nz,) + vec_in.shape, f32),
        ]
        + held
        + [
            D((na, nd // 2)),
            D((na, nd // 2)),
            D((na, nd // 2)),
            D((na, 2, nd // 2)),
            D((na, 2, nd // 2)),
            D((na, nz)),
            D((na, nz)),
            D((nh, nz)),
            D((nh, nz)),
            D((nh, nz)),
            D((nh, nz)),
            D((nb + nz,)),
            D((nb + nz,)),
            D,
        ],
        compiler_params=pltpu.CompilerParams(
            collective_id=cid, has_side_effects=True, vmem_limit_bytes=60 << 20
        ),
    )(grad_parts, wo, wa, w1, w2, qkv, att, lse, seg_row, seg_lanes, normed, joint_full, x_own, base, vec_in)


def local(
    tokens,
    segments,
    out_grad,
    align_grad,
    first_gain,
    first_shift,
    joint_weight,
    query_bias,
    value_bias,
    output_weight,
    output_bias,
    second_gain,
    second_shift,
    expand_bias,
    reduce_bias,
    head_gain,
    head_shift,
    align_weight,
    align_bias,
    expand_weight,
    reduce_weight,
):
    nd, nz = lax.axis_size("dp"), lax.axis_size("mp")
    n = nd * nz
    z = lax.axis_index("mp")
    rows, width = tokens.shape
    seq = rows * nz
    nh = H // nz
    own_cols = nh * HD
    f32, b16 = jnp.float32, jnp.bfloat16

    own = first_gain.shape[0]

    def columns(vector):
        count = -(-vector.shape[0] // own)
        padded = jnp.zeros((count * own,), b16).at[: vector.shape[0]].set(vector)
        return padded.reshape(count, own)

    vec = jnp.concatenate(
        [
            columns(v)
            for v in (
                first_gain,
                first_shift,
                query_bias,
                value_bias,
                output_bias,
                second_gain,
                second_shift,
                reduce_bias,
                head_gain,
                head_shift,
                expand_bias,
                align_bias,
            )
        ]
    )
    vec = jnp.zeros((own, 128), b16).at[:, : vec.shape[0]].set(vec.T)
    seg_row, seg_col = segments.reshape(1, seq), segments.reshape(seq, 1)
    vectors, joint_full, wo, wa, w1, w2, normed_all, qkv, att, lse, attended = forward_call(
        tokens,
        vec,
        joint_weight,
        output_weight,
        align_weight,
        expand_weight,
        reduce_weight.T,
        seg_row,
        seg_col,
        nd,
        nz,
        nh,
        1,
    )
    joint_full = joint_full.reshape(width, 3 * width)
    output_full = wo.reshape(width, width)
    align_full = wa.reshape(width, -1)
    expand_full = w1.reshape(width, -1)
    reduce_full = w2.reshape(width, -1)
    attended = attended.reshape(width, rows)
    (
        gain_one,
        shift_one,
        _,
        _,
        bias_output,
        gain_two,
        shift_two,
        bias_reduce,
        gain_head,
        shift_head,
    ) = (vectors[i] for i in range(10))
    count = -(-expand_bias.shape[0] // own)
    bias_expand = (
        vectors[10 : 10 + count].reshape(count, n, own).transpose(1, 0, 2).reshape(n, count * own)
    )[:, : expand_bias.shape[0]].reshape(-1)
    count_align = -(-align_bias.shape[0] // own)
    bias_align = (
        vectors[10 + count : 10 + count + count_align]
        .reshape(count_align, n, own)
        .transpose(1, 0, 2)
        .reshape(n, count_align * own)
    )[:, : align_bias.shape[0]].reshape(-1)

    resid = tokens.astype(f32)
    middle = (
        resid
        + jnp.einsum("ir,io->ro", attended, output_full, preferred_element_type=f32)
        + bias_output
    )
    normed_two = layer_norm(middle, gain_two, shift_two).astype(b16)
    preactivation = matmul(normed_two, expand_full) + bias_expand
    activated = exact_gelu(preactivation).astype(b16)
    block_out = middle + right_product(activated, reduce_full) + bias_reduce
    normed_three = layer_norm(block_out, gain_head, shift_head).astype(b16)
    align_out = matmul(normed_three, align_full) + bias_align
    grad_align_w = left_product(normed_three, align_grad)
    grad_align_b = column_sums(align_grad)
    back_three = right_product(align_grad, align_full)
    _, norm_pull = jax.vjp(layer_norm, block_out, gain_head, shift_head)
    back_extra, grad_head_gain, grad_head_shift = norm_pull(back_three)
    back_block = out_grad.astype(f32) + back_extra
    back_feed = back_block.astype(b16)
    grad_reduce_b = column_sums(back_feed)
    grad_reduce_w = left_product(back_feed, activated)
    back_active = matmul(back_feed, reduce_full)
    _, gelu_pull = jax.vjp(exact_gelu, preactivation)
    back_pre = gelu_pull(back_active)[0].astype(b16)
    grad_expand_w = left_product(normed_two, back_pre)
    grad_expand_b = column_sums(back_pre)
    back_two = right_product(back_pre, expand_full)
    _, norm_pull = jax.vjp(layer_norm, middle, gain_two, shift_two)
    middle_extra, grad_second_gain, grad_second_shift = norm_pull(back_two)
    back_middle = back_block + middle_extra
    back_output = back_middle.astype(b16)
    grad_output_b = column_sums(back_output)
    grad_output_w = jnp.einsum("ir,ro->io", attended, back_output, preferred_element_type=f32)
    back_att = jnp.einsum(
        "io,ro->ir", output_full, back_output, preferred_element_type=f32
    ).astype(b16)

    zero = jnp.zeros((width,), f32)
    lines = [
        gain_one,
        zero,
        zero,
        zero,
        grad_output_b,
        grad_second_gain,
        grad_second_shift,
        grad_reduce_b,
        grad_head_gain,
        grad_head_shift,
    ]
    hidden, aligned = grad_expand_b.shape[0], grad_align_b.shape[0]
    more = -(-aligned // width) * width
    vec_in = jnp.concatenate(
        lines + [grad_expand_b, jnp.zeros((more,), f32).at[:aligned].set(grad_align_b)]
    ).reshape(-1, width)
    tokens_grad, joint_mine, g_wo, g_wa, g_w1, g_w2, sums = backward_call(
        back_att.reshape(nz, own_cols, rows),
        grad_output_w.astype(b16).reshape(nd, nz, own, width),
        grad_align_w.astype(b16).reshape(nd, nz, own, -1),
        grad_expand_w.astype(b16).reshape(nd, width // nd, hidden),
        grad_reduce_w.astype(b16).reshape(nd, width // nd, hidden),
        qkv,
        att,
        lse,
        seg_row,
        jnp.broadcast_to(seg_col, (seq, 128)),
        normed_all,
        joint_full,
        tokens,
        back_middle,
        vec_in,
        nd,
        nz,
        nh,
        2,
    )
    g_joint = (
        joint_mine.reshape(nz, own, 3, own_cols).transpose(1, 2, 0, 3).reshape(own, 3 * width)
    )
    me = lax.axis_index("dp") * nz + z
    mine = lax.dynamic_slice_in_dim(sums[:10], me * own, own, axis=1)
    flat = sums[10:].reshape(-1)
    size_e, size_a = expand_bias.shape[0], align_bias.shape[0]
    g_expand_b = lax.dynamic_slice_in_dim(flat, me * size_e, size_e)
    g_align_b = lax.dynamic_slice_in_dim(flat, hidden + me * size_a, size_a)
    return (
        block_out.astype(b16),
        align_out.astype(b16),
        tokens_grad,
        mine[0],
        mine[1],
        g_joint,
        mine[2],
        mine[3],
        g_wo,
        mine[4],
        mine[5],
        mine[6],
        g_expand_b,
        mine[7],
        mine[8],
        mine[9],
        g_wa,
        g_align_b,
        g_w1,
        g_w2.T,
    )


def solution(mesh):
    both = P(("dp", "mp"))
    rows = P(("dp", "mp"), None)
    in_specs = (
        (rows, P("dp", None), rows, rows, both, both, rows, both, both, rows)
        + (both,) * 7
        + (rows, both, P("dp", "mp"), P("mp", "dp"))
    )
    out_specs = (
        (rows, rows, rows, both, both, rows, both, both, rows)
        + (both,) * 7
        + (rows, both, P("dp", "mp"), P("mp", "dp"))
    )
    return jax.shard_map(local, mesh=mesh, in_specs=in_specs, out_specs=out_specs, check_vma=False)
```

```python
import functools

import jax
import jax.numpy as jnp
from jax import lax
from jax.experimental import pallas as pl
from jax.experimental.pallas import tpu as pltpu
from jax.sharding import PartitionSpec as P

H = 12
HD = 64
EPSILON = 1e-06
NEG_FILL = -1000000000.0
MESH = pl.DeviceIdType.MESH
VMEM_LIMIT = 56 << 20


def layer_norm(values, gain, shift):
    centre = values - jnp.mean(values, axis=-1, keepdims=True)
    spread = jnp.mean(centre * centre, axis=-1, keepdims=True)
    return centre * lax.rsqrt(spread + EPSILON) * gain + shift


def nn(left, right):
    return lax.dot_general(
        left, right, (((1,), (0,)), ((), ())), preferred_element_type=jnp.float32
    )


def nt(left, right):
    return lax.dot_general(
        left, right, (((1,), (1,)), ((), ())), preferred_element_type=jnp.float32
    )


ANY = pl.BlockSpec(memory_space=pl.ANY)
VM = pl.BlockSpec(memory_space=pltpu.VMEM)


def peer_flip(index, bit):
    return index + bit * (1 - 2 * (index // bit % 2))


def mask_flip(index, mask):
    bit = 1
    while bit <= mask:
        if mask & bit:
            index = peer_flip(index, bit)
        bit *= 2
    return index


def plane_masks(order, step):
    masks = [0]
    for bit in order[:step]:
        masks += [m ^ bit for m in masks]
    return masks


class Spread:
    def __init__(self, slot, own, full, wide, nd, nz, dp, z, sems):
        self.slot, self.own, self.full, self.wide = slot, own, full, wide
        self.nd, self.nz, self.dp, self.z = nd, nz, dp, z
        self.keep_sem, self.right_sem, self.left_sem, self.line_sem, self.send_sem, self.recv_sem = sems
        self.bits = [1 << b for b in range(1, nd.bit_length() - 1)]
        self.cut = nz // 2

    def order(self, half):
        return self.bits if half == 0 else self.bits[::-1]

    def chunk(self, j):
        if self.wide:
            cols = self.own.shape[1]
            return self.full.at[self.dp, :, pl.ds(pl.multiple_of(j * cols, 128), cols)]
        return self.full.at[self.dp, j]

    def block(self, half, mask):
        d = mask_flip(self.dp, mask)
        lo, hi = (0, self.cut) if half == 0 else (self.cut, self.nz)
        if self.wide:
            cols = self.own.shape[1]
            return self.full.at[d, :, pl.ds(lo * cols, (hi - lo) * cols)]
        return self.full.at[d, pl.ds(lo, hi - lo)]

    def keep(self):
        return pltpu.make_async_copy(self.own, self.chunk(self.z), self.keep_sem.at[self.slot])

    def _right(self, step):
        j = jnp.maximum(self.z - step, 0)
        return pltpu.make_async_remote_copy(
            src_ref=self.own if step == 0 else self.chunk(j),
            dst_ref=self.chunk(j),
            send_sem=self.right_sem.at[self.slot, step],
            recv_sem=self.line_sem.at[self.slot, j],
            device_id=(self.dp, jnp.minimum(self.z + 1, self.nz - 1)),
            device_id_type=MESH,
        )

    def _left(self, step):
        j = jnp.minimum(self.z + step, self.nz - 1)
        return pltpu.make_async_remote_copy(
            src_ref=self.own if step == 0 else self.chunk(j),
            dst_ref=self.chunk(j),
            send_sem=self.left_sem.at[self.slot, step],
            recv_sem=self.line_sem.at[self.slot, j],
            device_id=(self.dp, jnp.maximum(self.z - 1, 0)),
            device_id_type=MESH,
        )

    def line_start(self, step):
        if step >= self.nz - 1:
            return

        @pl.when((self.z < self.nz - 1) & (self.z - step >= 0))
        def _():
            self._right(step).start()

        @pl.when((self.z > 0) & (self.z + step <= self.nz - 1))
        def _():
            self._left(step).start()

    def line_wait(self, step):
        @pl.when(self.z - step >= 0)
        def _():
            self._right(step).wait_recv()

        @pl.when(self.z + step <= self.nz - 1)
        def _():
            self._left(step).wait_recv()

    def _plane(self, half, mask, bit):
        return pltpu.make_async_remote_copy(
            src_ref=self.block(half, mask),
            dst_ref=self.block(half, mask),
            send_sem=self.send_sem.at[self.slot, half, mask ^ bit],
            recv_sem=self.recv_sem.at[self.slot, half, mask ^ bit],
            device_id=(peer_flip(self.dp, bit), self.z),
            device_id_type=MESH,
        )

    def _arrival(self, half, mask, bit):
        return pltpu.make_async_remote_copy(
            src_ref=self.block(half, mask),
            dst_ref=self.block(half, mask),
            send_sem=self.send_sem.at[self.slot, half, mask],
            recv_sem=self.recv_sem.at[self.slot, half, mask],
            device_id=(peer_flip(self.dp, bit), self.z),
            device_id_type=MESH,
        )

    def plane_start(self, step):
        if step >= len(self.bits):
            return
        for half in range(2):
            order = self.order(half)
            for mask in plane_masks(order, step):
                self._plane(half, mask, order[step]).start()

    def plane_wait(self, step):
        for half in range(2):
            order = self.order(half)
            for mask in plane_masks(order, step):
                self._arrival(half, mask ^ order[step], order[step]).wait_recv()

    def _new_masks(self, half, step):
        order = self.order(half)
        return [0] if step < 0 else [m ^ order[step] for m in plane_masks(order, step)]

    def core_start(self, step):
        for half in range(2):
            for mask in self._new_masks(half, step):
                self._plane(half, mask, 1).start()

    def core_wait(self):
        for half in range(2):
            for mask in plane_masks(self.bits, len(self.bits)):
                self._arrival(half, mask ^ 1, 1).wait_recv()

    def sends_wait(self):
        for step in range(self.nz - 1):

            @pl.when((self.z < self.nz - 1) & (self.z - step >= 0))
            def _():
                self._right(step).wait_send()

            @pl.when((self.z > 0) & (self.z + step <= self.nz - 1))
            def _():
                self._left(step).wait_send()

        for half in range(2):
            order = self.order(half)
            for step in range(len(self.bits)):
                for mask in plane_masks(order, step):
                    self._plane(half, mask, order[step]).wait_send()
            for mask in plane_masks(order, len(self.bits)):
                self._plane(half, mask, 1).wait_send()


def greet(nd, nz, dp, z, line=True, plane=True):
    barrier = pltpu.get_barrier_semaphore()
    count = 0
    if line:
        for off in range(1, nz):
            pl.semaphore_signal(
                barrier, inc=1, device_id=(dp, lax.rem(z + off, nz)), device_id_type=MESH
            )
            count += 1
    if plane:
        bit = 1
        while bit < nd:
            pl.semaphore_signal(
                barrier, inc=1, device_id=(peer_flip(dp, bit), z), device_id_type=MESH
            )
            count += 1
            bit *= 2
    pl.semaphore_wait(barrier, count)


def lane_copies(seg_row):
    return jnp.broadcast_to(seg_row[...], (128, seg_row.shape[1])).T


def forward_kernel(
    nd,
    nz,
    nh,
    x_own,
    vec_own,
    joint_own,
    wo_own,
    wa_own,
    w1_own,
    w2_own,
    seg_row,
    vec_rows,
    joint,
    wo,
    wa,
    w1,
    w2,
    normed_out,
    qkv_out,
    att_out,
    lse,
    att_land,
    x_land,
    vec,
    window,
    vec_cols,
    weights,
    weights_t,
    wide,
    normed,
    qkv,
    att,
    keys,
    bias,
    seg_lanes,
    tops,
    totals,
    att_send,
    keep_sem,
    right_sem,
    left_sem,
    line_sem,
    send_sem,
    recv_sem,
    x_sem,
    x_right,
    x_left,
    x_recv,
    win_sem,
    att_send_sem,
    att_recv_sem,
    out_sem,
):
    dp, z = lax.axis_index("dp"), lax.axis_index("mp")
    rows, width = x_own.shape
    seq = rows * nz
    own_cols = nh * HD
    win_cols = window.shape[-1] // 3
    win = z * own_cols // 128 * 128
    shift = pl.multiple_of(z * own_cols - win, HD)
    win = pl.multiple_of(win, 128)
    f32, b16 = jnp.float32, jnp.bfloat16
    sems = (keep_sem, right_sem, left_sem, line_sem, send_sem, recv_sem)
    specs = [
        (vec_own, vec, False),
        (joint_own, joint, False),
        (wo_own, wo, False),
        (w1_own, w1, True),
        (wa_own, wa, False),
        (w2_own, w2, True),
    ]
    spreads = [Spread(i, *spec, nd, nz, dp, z, sems) for i, spec in enumerate(specs)]
    first, second, third = spreads[:2], spreads[2:4], spreads[4:]
    steps = len(spreads[0].bits)

    def line_step(group, step):
        for s in group:
            s.line_wait(step)
            s.line_start(step)

    def plane_open(group):
        for s in group:
            s.keep().wait()
            s.plane_start(0)
            s.core_start(-1)

    def plane_step(group, step):
        for s in group:
            s.plane_wait(step)
            s.plane_start(step + 1)
            s.core_start(step)

    def x_to_right(step):
        j = jnp.maximum(z - step, 0)
        return pltpu.make_async_remote_copy(
            src_ref=x_land.at[j],
            dst_ref=x_land.at[j],
            send_sem=x_right.at[step],
            recv_sem=x_recv.at[j],
            device_id=(dp, jnp.minimum(z + 1, nz - 1)),
            device_id_type=MESH,
        )

    def x_to_left(step):
        j = jnp.minimum(z + step, nz - 1)
        return pltpu.make_async_remote_copy(
            src_ref=x_land.at[j],
            dst_ref=x_land.at[j],
            send_sem=x_left.at[step],
            recv_sem=x_recv.at[j],
            device_id=(dp, jnp.maximum(z - 1, 0)),
            device_id_type=MESH,
        )

    def x_start(step):
        @pl.when((z < nz - 1) & (z - step >= 0))
        def _():
            x_to_right(step).start()

        @pl.when((z > 0) & (z + step <= nz - 1))
        def _():
            x_to_left(step).start()

    greet(nd, nz, dp, z)
    for s in spreads:
        s.keep().start()
    x_keep = pltpu.make_async_copy(x_own, x_land.at[z], x_sem)
    x_keep.start()
    for s in first:
        s.line_start(0)
    for step in range(1, nz - 1):
        line_step(first, step)
    for s in second:
        s.line_start(0)
    seg_lanes[...] = lane_copies(seg_row)
    line_step(first, nz - 1)
    plane_open(first)
    line_step(second, 1)
    plane_step(first, 0)
    for step in range(2, nz - 1):
        line_step(second, step)
    for s in third:
        s.line_start(0)
    line_step(second, nz - 1)
    plane_open(second)
    line_step(third, 1)
    for t in range(1, steps):
        plane_step(first, t)
    for step in range(2, nz - 1):
        line_step(third, step)
    x_keep.wait()
    x_start(0)
    line_step(third, nz - 1)
    plane_open(third)
    plane_step(second, 0)
    for s in first:
        s.core_wait()

    loads = []
    for p in range(3):
        load = pltpu.make_async_copy(
            joint.at[:, :, :, pl.ds(pl.multiple_of(p * width + win, 128), win_cols)],
            window.at[:, :, :, pl.ds(p * win_cols, win_cols)],
            win_sem.at[p],
        )
        load.start()
        loads.append(load)
    own = vec.shape[2]
    for d in range(nd):
        for j in range(nz):
            at = (d * nz + j) * own
            vec_cols[at : at + own, :] = vec[d, j].astype(f32)
    vec_t = vec_cols[...].T
    vec_rows[...] = vec_t[: vec_rows.shape[0]]
    for load in loads:
        load.wait()
    for d in range(nd):
        for j in range(nz):
            at = (d * nz + j) * own
            weights[at : at + own, :] = window[d, j].astype(f32)
    for p in range(3):
        cols = slice(p * win_cols, (p + 1) * win_cols)
        weights_t[cols, :] = weights[:, cols].T.astype(b16)
    gain, offset = vec_rows[0:1, :], vec_rows[1:2, :]
    bias_q = vec_cols[pl.ds(win, win_cols), 2:3]
    bias_v = vec_cols[pl.ds(win, win_cols), 3:4]

    def normed_copy(j):
        at = pl.ds(pl.multiple_of(j * rows, rows), rows)
        return pltpu.make_async_copy(normed.at[at], normed_out.at[at], out_sem.at[0, j])

    def qkv_copy(j):
        at = pl.ds(pl.multiple_of(j * rows, rows), rows)
        return pltpu.make_async_copy(qkv.at[:, at], qkv_out.at[:, at], out_sem.at[1, j])

    def att_keep(j):
        at = pl.ds(pl.multiple_of(j * rows, rows), rows)
        return pltpu.make_async_copy(att.at[:, at], att_out.at[:, at], out_sem.at[2, j])

    def att_copy(to):
        return pltpu.make_async_remote_copy(
            src_ref=att_send.at[to],
            dst_ref=att_land.at[z],
            send_sem=att_send_sem.at[lax.rem(to - z + nz, nz)],
            recv_sem=att_recv_sem.at[lax.rem(to - z + nz, nz)],
            device_id=(dp, to),
            device_id_type=MESH,
        )

    def project(j):
        at = pl.ds(pl.multiple_of(j * rows, rows), rows)
        normed[at, :] = layer_norm(x_land[j].astype(f32), gain, offset).astype(b16)
        for p in range(3):
            part = nt(weights_t[p * win_cols : (p + 1) * win_cols, :], normed[at, :])
            if p == 0:
                part = part + bias_q
            if p == 2:
                part = part + bias_v
            wide[p * win_cols : (p + 1) * win_cols, :] = part.astype(b16)
            qkv[p * own_cols : (p + 1) * own_cols, at] = wide[
                pl.ds(p * win_cols + shift, own_cols), :
            ]
        for h in range(nh):
            keys[h, at, :] = wide[pl.ds(win_cols + shift + h * HD, HD), :].T
        tops[:, at] = jnp.full((tops.shape[0], rows), -jnp.inf, f32)
        totals[:, at] = jnp.zeros((totals.shape[0], rows), f32)
        att[:, at] = jnp.zeros((own_cols, rows), f32)
        normed_copy(j).start()
        qkv_copy(j).start()

    def pair(i, j):
        to = pl.ds(pl.multiple_of(i * rows, rows), rows)
        of = pl.ds(pl.multiple_of(j * rows, rows), rows)
        own_seg, lanes = seg_row[0:1, to], seg_lanes[of, :]
        bias[...] = jnp.concatenate(
            [
                jnp.where(lanes == own_seg[:, k : k + 128], 0.0, NEG_FILL)
                for k in range(0, rows, 128)
            ],
            axis=1,
        )
        for h in range(nh):
            query = qkv[h * HD : (h + 1) * HD, to] * jnp.bfloat16(0.125)
            score = nn(keys[h, of, :], query) + bias[...]
            top = tops[h : h + 1, to]
            new_top = jnp.maximum(top, jnp.max(score, axis=0, keepdims=True))
            weight = jnp.exp(score - new_top)
            fade = jnp.exp(top - new_top)
            tops[h : h + 1, to] = new_top
            totals[h : h + 1, to] = totals[h : h + 1, to] * fade + jnp.sum(
                weight, axis=0, keepdims=True
            )
            value = qkv[2 * own_cols + h * HD : 2 * own_cols + (h + 1) * HD, of]
            att[h * HD : (h + 1) * HD, to] = att[h * HD : (h + 1) * HD, to] * fade + nn(
                value, weight.astype(b16)
            )

    def finish(i):
        to = pl.ds(pl.multiple_of(i * rows, rows), rows)
        for h in range(nh):
            total = totals[h : h + 1, to]
            result = att[h * HD : (h + 1) * HD, to] / total
            att[h * HD : (h + 1) * HD, to] = result
            att_send[i, h * HD : (h + 1) * HD, :] = result.astype(b16)
            lse[h : h + 1, to] = tops[h : h + 1, to] + jnp.log(total)
        att_keep(i).start()

        @pl.when(i != z)
        def _():
            att_copy(i).start()

    def take(c, low, high, last):
        project(c)

        def old_queries(f, carry):
            pair(f, c)

            @pl.when(last)
            def _():
                finish(f)

            return carry

        def new_queries(f, carry):
            pair(c, f)
            return carry

        lax.fori_loop(low, high, old_queries, 0)
        lax.fori_loop(low, high, new_queries, 0)
        pair(c, c)

        @pl.when(last)
        def _():
            finish(c)

    project(z)
    pair(z, z)
    final = jnp.maximum(z, nz - 1 - z)

    def arrivals(step, carry):
        @pl.when(z - step >= 0)
        def _():
            x_to_right(step).wait_recv()

        @pl.when(z + step <= nz - 1)
        def _():
            x_to_left(step).wait_recv()

        @pl.when(step < nz - 1)
        def _():
            x_start(step)

        high = jnp.minimum(z + step, nz)

        @pl.when(z - step >= 0)
        def _():
            take(z - step, z - step + 1, high, (step == final) & (z + step > nz - 1))

        @pl.when(z + step <= nz - 1)
        def _():
            take(z + step, jnp.maximum(z - step, 0), high, step == final)

        @pl.when(step == 1)
        def _():
            plane_step(third, 0)
            for t in range(1, steps):
                plane_step(second, t)

        @pl.when(step == 2)
        def _():
            for t in range(1, steps):
                plane_step(third, t)

        return carry

    lax.fori_loop(1, nz, arrivals, 0)
    own_keep = pltpu.make_async_copy(att_send.at[z], att_land.at[z], x_sem)
    own_keep.start()
    for s in second + third:
        s.core_wait()
    own_keep.wait()
    for off in range(1, nz):
        att_copy(lax.rem(z + off, nz)).wait()
    for j in range(nz):
        normed_copy(j).wait()
        qkv_copy(j).wait()
        att_keep(j).wait()
    for step in range(nz - 1):

        @pl.when((z < nz - 1) & (z - step >= 0))
        def _():
            x_to_right(step).wait_send()

        @pl.when((z > 0) & (z + step <= nz - 1))
        def _():
            x_to_left(step).wait_send()

    for s in spreads:
        s.sends_wait()


def forward_call(x, vec, joint, wo, wa, w1, w2, seg_row, nd, nz, nh, cid):
    rows, width = x.shape
    seq, own_cols = rows * nz, nh * HD
    win_cols = -(-(own_cols + HD) // 128) * 128
    own = joint.shape[0]
    f32, b16 = jnp.float32, jnp.bfloat16
    S = jax.ShapeDtypeStruct
    na = 6
    return pl.pallas_call(
        functools.partial(forward_kernel, nd, nz, nh),
        out_shape=(
            S((16, width), f32),
            S((nd, nz) + joint.shape, b16),
            S((nd, nz) + wo.shape, b16),
            S((nd, nz) + wa.shape, b16),
            S((nd, w1.shape[0], nz * w1.shape[1]), b16),
            S((nd, w2.shape[0], nz * w2.shape[1]), b16),
            S((seq, width), b16),
            S((3 * own_cols, seq), b16),
            S((own_cols, seq), f32),
            S((8, seq), f32),
            S((nz, own_cols, rows), b16),
        ),
        in_specs=[ANY] + [VM] * 7,
        out_specs=(VM,) + (ANY,) * 8 + (VM, ANY),
        scratch_shapes=[
            pltpu.VMEM((nz, rows, width), b16),
            pltpu.VMEM((nd, nz) + vec.shape, b16),
            pltpu.VMEM((nd, nz, own, 3 * win_cols), b16),
            pltpu.VMEM((width, vec.shape[1]), f32),
            pltpu.VMEM((width, 3 * win_cols), f32),
            pltpu.VMEM((3 * win_cols, width), b16),
            pltpu.VMEM((3 * win_cols, rows), b16),
            pltpu.VMEM((seq, width), b16),
            pltpu.VMEM((3 * own_cols, seq), b16),
            pltpu.VMEM((own_cols, seq), f32),
            pltpu.VMEM((nh, seq, HD), b16),
            pltpu.VMEM((rows, rows), f32),
            pltpu.VMEM((seq, 128), jnp.int32),
            pltpu.VMEM((8, seq), f32),
            pltpu.VMEM((8, seq), f32),
            pltpu.VMEM((nz, own_cols, rows), b16),
            pltpu.SemaphoreType.DMA((na,)),
            pltpu.SemaphoreType.DMA((na, nz)),
            pltpu.SemaphoreType.DMA((na, nz)),
            pltpu.SemaphoreType.DMA((na, nz)),
            pltpu.SemaphoreType.DMA((na, 2, nd)),
            pltpu.SemaphoreType.DMA((na, 2, nd)),
            pltpu.SemaphoreType.DMA,
            pltpu.SemaphoreType.DMA((nz,)),
            pltpu.SemaphoreType.DMA((nz,)),
            pltpu.SemaphoreType.DMA((nz,)),
            pltpu.SemaphoreType.DMA((3,)),
            pltpu.SemaphoreType.DMA((nz,)),
            pltpu.SemaphoreType.DMA((nz,)),
            pltpu.SemaphoreType.DMA((3, nz)),
        ],
        compiler_params=pltpu.CompilerParams(
            collective_id=cid, has_side_effects=True, vmem_limit_bytes=VMEM_LIMIT
        ),
    )(x, vec, joint, wo, wa, w1, w2, seg_row)


class Reduce:
    def __init__(self, slot, part, acc, land, plane, line, wide, nd, nz, dp, z, sems):
        self.slot, self.part, self.acc, self.land, self.plane, self.line = slot, part, acc, land, plane, line
        self.wide, self.nd, self.nz, self.dp, self.z = wide, nd, nz, dp, z
        self.load_sem, self.core_out, self.core_in, self.plane_out, self.plane_in, self.line_out, self.line_in = sems
        self.bits = [1 << b for b in range(1, nd.bit_length() - 1)]
        self.masks = plane_masks(self.bits, len(self.bits))
        self.cut = nz // 2
        self.cols = acc.shape[-1] // nz if wide else acc.shape[-1]

    def order(self, half):
        return self.bits if half == 0 else self.bits[::-1]

    def span(self, half):
        return (0, self.cut) if half == 0 else (self.cut, self.nz)

    def region(self, ref, i, half):
        lo, hi = self.span(half)
        if self.wide:
            return ref.at[i, :, pl.ds(lo * self.cols, (hi - lo) * self.cols)]
        return ref.at[i, pl.ds(lo, hi - lo)]

    def chunk(self, ref, i, j):
        if self.wide:
            at = j * self.cols
            at = at if isinstance(at, int) else pl.multiple_of(at, 128)
            return ref.at[i, :, pl.ds(at, self.cols)]
        return ref.at[i, j]

    def slots(self, half, step):
        order, base = self.order(half), 0
        for t in range(step):
            base += 1 << (len(order) - 1 - t)
        rest = plane_masks(order[step + 1 :], len(order) - step - 1)
        return [(m, base + k) for k, m in enumerate(rest)]

    def _load(self, m):
        return pltpu.make_async_copy(
            self.part.at[mask_flip(self.dp, m)], self.acc.at[m >> 1], self.load_sem.at[self.slot, m >> 1]
        )

    def _core(self, m):
        return pltpu.make_async_remote_copy(
            src_ref=self.part.at[mask_flip(self.dp, m ^ 1)],
            dst_ref=self.land.at[m >> 1],
            send_sem=self.core_out.at[self.slot, m >> 1],
            recv_sem=self.core_in.at[self.slot, m >> 1],
            device_id=(peer_flip(self.dp, 1), self.z),
            device_id_type=MESH,
        )

    def core_start(self):
        for m in self.masks:
            self._core(m).start()
        for m in self.masks:
            self._load(m).start()

    def _add(self, i, source, k, half):
        lo, hi = self.span(half)

        def step(j, carry):
            to, more = self.chunk(self.acc, i, j), self.chunk(source, k, j)
            to[...] = (to[...].astype(jnp.float32) + more[...].astype(jnp.float32)).astype(to.dtype)
            return carry

        lax.fori_loop(lo, hi, step, 0)

    def core_add(self):
        for m in self.masks:
            self._load(m).wait()
            self._core(m).wait_recv()
            for half in range(2):
                self._add(m >> 1, self.land, m >> 1, half)

    def _plane(self, half, step, m, place):
        bit = self.order(half)[step]
        return pltpu.make_async_remote_copy(
            src_ref=self.region(self.acc, (m ^ bit) >> 1, half),
            dst_ref=self.region(self.plane, place, half),
            send_sem=self.plane_out.at[self.slot, half, place],
            recv_sem=self.plane_in.at[self.slot, half, place],
            device_id=(peer_flip(self.dp, bit), self.z),
            device_id_type=MESH,
        )

    def plane_start(self, step):
        if step < len(self.bits):
            for half in range(2):
                for m, place in self.slots(half, step):
                    self._plane(half, step, m, place).start()

    def plane_add(self, step):
        for half in range(2):
            for m, place in self.slots(half, step):
                self._plane(half, step, m, place).wait_recv()
                self._add(m >> 1, self.plane, place, half)

    def _line(self, off):
        to = lax.rem(self.z + off, self.nz)
        return pltpu.make_async_remote_copy(
            src_ref=self.chunk(self.acc, 0, to),
            dst_ref=self.line.at[off],
            send_sem=self.line_out.at[self.slot, off],
            recv_sem=self.line_in.at[self.slot, off],
            device_id=(self.dp, to),
            device_id_type=MESH,
        )

    def line_start(self):
        for off in range(1, self.nz):
            self._line(off).start()

    def line_wait(self):
        for off in range(1, self.nz):
            self._line(off).wait_recv()

    def line_sum(self):
        self.line_wait()
        total = self.chunk(self.acc, 0, self.z)[...].astype(jnp.float32)
        for off in range(1, self.nz):
            total = total + self.line[off].astype(jnp.float32)
        return total

    def sends_wait(self):
        for m in self.masks:
            self._core(m).wait_send()
        for half in range(2):
            for step in range(len(self.bits)):
                for m, place in self.slots(half, step):
                    self._plane(half, step, m, place).wait_send()
        for off in range(1, self.nz):
            self._line(off).wait_send()


def backward_kernel(
    nd,
    nz,
    nh,
    grad_parts,
    part_wo,
    part_wa,
    part_w1,
    part_w2,
    qkv,
    att,
    lse,
    seg_row,
    normed,
    joint_full,
    x_own,
    base,
    vec_in,
    tokens_grad,
    out_joint,
    out_wo,
    out_wa,
    out_w1,
    out_w2,
    out_vec,
    grad_land,
    keys,
    values,
    key_grad,
    value_grad,
    turned,
    staged,
    rows_land,
    part_joint,
    bias_cols,
    seg_lanes,
    vec_stage,
    vec_land,
    vec_line,
    *rest,
):
    na = 5
    buffers = [rest[4 * a : 4 * a + 4] for a in range(na)]
    (
        load_sem,
        core_out,
        core_in,
        plane_out,
        plane_in,
        line_out,
        line_in,
        grad_out,
        grad_in,
        row_out,
        row_in,
        vec_out,
        vec_in_sem,
        own_sem,
    ) = rest[4 * na :]
    dp, z = lax.axis_index("dp"), lax.axis_index("mp")
    rows, width = x_own.shape
    seq = rows * nz
    own_cols = nh * HD
    f32, b16 = jnp.float32, jnp.bfloat16
    sems = (load_sem, core_out, core_in, plane_out, plane_in, line_out, line_in)
    parts = [(part_w2, True), (part_w1, True), (part_wa, False), (part_wo, False), (part_joint, False)]
    reduces = [
        Reduce(a, part, *buffers[a], wide, nd, nz, dp, z, sems) for a, (part, wide) in enumerate(parts)
    ]
    big, joint = reduces[:4], reduces[4]
    steps = len(joint.bits)

    greet(nd, nz, dp, z)

    def grad_copy(h, off):
        to = lax.rem(z + off, nz)
        return pltpu.make_async_remote_copy(
            src_ref=grad_parts.at[to, pl.ds(h * HD, HD)],
            dst_ref=grad_land.at[z, pl.ds(h * HD, HD)],
            send_sem=grad_out.at[h, off],
            recv_sem=grad_in.at[h, off],
            device_id=(dp, to),
            device_id_type=MESH,
        )

    grad_own = pltpu.make_async_copy(grad_parts.at[z], grad_land.at[z], own_sem)
    grad_own.start()
    for h in range(nh):
        for off in range(1, nz):
            grad_copy(h, off).start()
    for r in big:
        r.core_start()
    for h in range(nh):
        keys[h] = qkv[own_cols + h * HD : own_cols + (h + 1) * HD, :].T
        values[h] = qkv[2 * own_cols + h * HD : 2 * own_cols + (h + 1) * HD, :].T
    bias_cols[...] = jnp.zeros_like(bias_cols)
    seg_lanes[...] = lane_copies(seg_row)
    kc = min(512, seq)

    def row_copy(h, off):
        to = lax.rem(z + off, nz)
        return pltpu.make_async_remote_copy(
            src_ref=staged.at[to, :, pl.ds(h * HD, HD)],
            dst_ref=rows_land.at[:, z, pl.ds(h * HD, HD)],
            send_sem=row_out.at[h, off],
            recv_sem=row_in.at[h, off],
            device_id=(dp, to),
            device_id_type=MESH,
        )

    def chores(u):
        if u == 1:
            big[0].core_add()
            big[0].plane_start(0)
        if u == 2:
            big[1].core_add()
            big[1].plane_start(0)
        if u == 3:
            for r in big[2:]:
                r.core_add()
                r.plane_start(0)
        if u == 5:
            big[0].plane_add(0)
            big[0].plane_start(1)
        if u == 8:
            big[1].plane_add(0)
            big[1].plane_start(1)
        if u == 10:
            for r in big[2:]:
                r.plane_add(0)
                r.plane_start(1)

    grad_own.wait()
    for h in range(nh):
        for off in range(1, nz):
            grad_copy(h, off).wait_recv()
        key_grad[...] = jnp.zeros_like(key_grad)
        value_grad[...] = jnp.zeros_like(value_grad)

        def block(i, carry):
            start = pl.multiple_of(i * rows, rows)
            own_seg = seg_row[0:1, pl.ds(start, rows)]
            query = qkv[h * HD : (h + 1) * HD, pl.ds(start, rows)] * jnp.bfloat16(0.125)
            back = grad_land[i, h * HD : (h + 1) * HD, :]
            row_term = jnp.sum(
                back.astype(f32) * att[h * HD : (h + 1) * HD, pl.ds(start, rows)],
                axis=0,
                keepdims=True,
            )
            log_total = lse[h : h + 1, pl.ds(start, rows)]
            query_grad = jnp.zeros((HD, rows), f32)
            for c in range(0, seq, kc):
                chunk = slice(c, c + kc)
                lanes = seg_lanes[chunk, :]
                allowed = jnp.concatenate(
                    [lanes == own_seg[:, k : k + 128] for k in range(0, rows, 128)], axis=1
                )
                score = nn(keys[h, chunk, :], query)
                weight = jnp.where(allowed, jnp.exp(score - log_total), 0.0)
                value_grad[chunk, :] += nt(weight.astype(b16), back)
                weight_grad = nn(values[h, chunk, :], back)
                score_grad = (weight * (weight_grad - row_term)).astype(b16)
                key_grad[chunk, :] += nt(score_grad, query)
                query_grad = query_grad + nn(
                    qkv[own_cols + h * HD : own_cols + (h + 1) * HD, chunk], score_grad
                )
            staged[i, 0, h * HD : (h + 1) * HD, :] = (query_grad * 0.125).astype(b16)
            for b in range(nz):
                u = h * nz + b

                @pl.when(i == b)
                def _():
                    chores(u)

            return carry

        lax.fori_loop(0, nz, block, 0)
        for p, source in ((1, key_grad), (2, value_grad)):
            turned[...] = source[...].T
            for j in range(nz):
                staged[j, p, h * HD : (h + 1) * HD, :] = turned[:, j * rows : (j + 1) * rows].astype(b16)
        for off in range(1, nz):
            row_copy(h, off).start()
        rows_land[:, z, h * HD : (h + 1) * HD, :] = staged[z, :, h * HD : (h + 1) * HD, :]
        at = pl.ds(pl.multiple_of(z * own_cols + h * HD, HD), HD)
        for col, p in ((0, 0), (1, 2)):
            total = jnp.zeros((HD, 1), f32)
            for j in range(nz):
                total = total + jnp.sum(
                    staged[j, p, h * HD : (h + 1) * HD, :].astype(f32), axis=1, keepdims=True
                )
            bias_cols[at, col : col + 1] = total

    grad_t = jnp.zeros((3 * own_cols, width), f32)
    for j in range(nz):
        grad_t = grad_t + nn(
            staged[j].reshape(3 * own_cols, rows), normed[j * rows : (j + 1) * rows, :]
        )
    grad_joint = grad_t.T
    own = part_joint.shape[2]
    for d in range(nd):
        for j in range(nz):
            at = (d * nz + j) * own
            part_joint[d, j] = grad_joint[at : at + own, :].astype(b16)
    joint.core_start()
    for t in range(1, steps):
        for r in big:
            r.plane_add(t)
            r.plane_start(t + 1)
    for r in big:
        r.line_start()
    joint.core_add()
    joint.plane_start(0)
    for t in range(steps):
        joint.plane_add(t)
        joint.plane_start(t + 1)
    joint.line_start()

    for h in range(nh):
        for off in range(1, nz):
            row_copy(h, off).wait_recv()
    back_t = nn(joint_full[...], rows_land[...].reshape(3 * width, rows))
    back = back_t.T
    gain = vec_in[0:1, :]
    x = x_own[...].astype(f32)
    centre = x - jnp.mean(x, axis=-1, keepdims=True)
    inverse = lax.rsqrt(jnp.mean(centre * centre, axis=-1, keepdims=True) + EPSILON)
    unit = centre * inverse
    scaled = back * gain
    tokens_grad[...] = base[...] + inverse * (
        scaled
        - jnp.mean(scaled, axis=-1, keepdims=True)
        - unit * jnp.mean(scaled * unit, axis=-1, keepdims=True)
    )
    bias_rows = bias_cols[...].T
    vec_stage[0] = vec_in[...]
    vec_stage[0, 0:1, :] = jnp.sum(back * unit, axis=0, keepdims=True)
    vec_stage[0, 1:2, :] = jnp.sum(back, axis=0, keepdims=True)
    vec_stage[0, 2:4, :] = bias_rows[0:2, :]
    bits = [1] + joint.bits

    def vec_copy(t):
        return pltpu.make_async_remote_copy(
            src_ref=vec_stage.at[t],
            dst_ref=vec_land.at[t],
            send_sem=vec_out.at[t],
            recv_sem=vec_in_sem.at[t],
            device_id=(peer_flip(dp, bits[t]), z),
            device_id_type=MESH,
        )

    def vec_line_copy(off):
        return pltpu.make_async_remote_copy(
            src_ref=vec_stage.at[len(bits)],
            dst_ref=vec_line.at[off],
            send_sem=vec_out.at[len(bits) + off],
            recv_sem=vec_in_sem.at[len(bits) + off],
            device_id=(dp, lax.rem(z + off, nz)),
            device_id_type=MESH,
        )

    for t in range(len(bits)):
        vec_copy(t).start()
        vec_copy(t).wait_recv()
        vec_stage[t + 1] = vec_stage[t] + vec_land[t]
    for off in range(1, nz):
        vec_line_copy(off).start()
    for r, out in zip(big, (out_w2, out_w1, out_wa, out_wo)):
        out[...] = r.line_sum()
    joint.line_wait()
    out_joint[z] = joint.acc[0, z].astype(f32)
    for off in range(1, nz):
        out_joint[lax.rem(z - off + nz, nz)] = joint.line[off].astype(f32)
    total = vec_stage[len(bits)]
    for off in range(1, nz):
        vec_line_copy(off).wait_recv()
        total = total + vec_line[off]
    out_vec[...] = total
    for t in range(len(bits)):
        vec_copy(t).wait_send()
    for off in range(1, nz):
        vec_line_copy(off).wait_send()
        for h in range(nh):
            grad_copy(h, off).wait_send()
            row_copy(h, off).wait_send()
    for r in reduces:
        r.sends_wait()


def backward_call(
    grad_parts, wo, wa, w1, w2, qkv, att, lse, seg_row, normed, joint_full, x_own, base, vec_in, nd, nz, nh, cid
):
    rows, width = x_own.shape
    seq, own_cols = rows * nz, nh * HD
    own = width // (nd * nz)
    f32, b16 = jnp.float32, jnp.bfloat16
    S, D = jax.ShapeDtypeStruct, pltpu.SemaphoreType.DMA
    joint_shape = (nd, nz, own, 3 * own_cols)
    held = []
    for shape, wide in ((w2.shape, True), (w1.shape, True), (wa.shape, False), (wo.shape, False), (joint_shape, False)):
        piece = shape[1:]
        line = (nz, piece[0], piece[1] // nz) if wide else piece
        held += [
            pltpu.VMEM((nd // 2,) + piece, b16),
            pltpu.VMEM((nd // 2,) + piece, b16),
            pltpu.VMEM((max(nd // 2 - 1, 1),) + piece, b16),
            pltpu.VMEM(line, b16),
        ]
    na, nb = 5, nd.bit_length() - 1
    return pl.pallas_call(
        functools.partial(backward_kernel, nd, nz, nh),
        out_shape=(
            S((rows, width), f32),
            S((nz, own, 3 * own_cols), f32),
            S(wo.shape[2:], f32),
            S(wa.shape[2:], f32),
            S((w1.shape[1], w1.shape[2] // nz), f32),
            S((w2.shape[1], w2.shape[2] // nz), f32),
            S(vec_in.shape, f32),
        ),
        in_specs=[ANY] * 5 + [VM] * 9,
        out_specs=(VM,) * 7,
        scratch_shapes=[
            pltpu.VMEM((nz, own_cols, rows), b16),
            pltpu.VMEM((nh, seq, HD), b16),
            pltpu.VMEM((nh, seq, HD), b16),
            pltpu.VMEM((seq, HD), f32),
            pltpu.VMEM((seq, HD), f32),
            pltpu.VMEM((HD, seq), f32),
            pltpu.VMEM((nz, 3, own_cols, rows), b16),
            pltpu.VMEM((3, nz, own_cols, rows), b16),
            pltpu.VMEM(joint_shape, b16),
            pltpu.VMEM((width, 128), f32),
            pltpu.VMEM((seq, 128), jnp.int32),
            pltpu.VMEM((nb + 1,) + vec_in.shape, f32),
            pltpu.VMEM((nb,) + vec_in.shape, f32),
            pltpu.VMEM((nz,) + vec_in.shape, f32),
        ]
        + held
        + [
            D((na, nd // 2)),
            D((na, nd // 2)),
            D((na, nd // 2)),
            D((na, 2, nd // 2)),
            D((na, 2, nd // 2)),
            D((na, nz)),
            D((na, nz)),
            D((nh, nz)),
            D((nh, nz)),
            D((nh, nz)),
            D((nh, nz)),
            D((nb + nz,)),
            D((nb + nz,)),
            D,
        ],
        compiler_params=pltpu.CompilerParams(
            collective_id=cid, has_side_effects=True, vmem_limit_bytes=60 << 20
        ),
    )(grad_parts, wo, wa, w1, w2, qkv, att, lse, seg_row, normed, joint_full, x_own, base, vec_in)


def gelu_pair(u):
    size = jnp.abs(u)
    t = 1.0 / (1.0 + (0.3275911 * 0.7071067811865476) * size)
    poly = ((((1.061405429 * t - 1.453152027) * t + 1.421413741) * t - 0.284496736) * t + 0.254829592) * t
    bell = jnp.exp(-0.5 * u * u)
    tail = 0.5 * poly * bell
    share = jnp.where(u >= 0.0, 1.0 - tail, tail)
    return u * share, share + u * (0.3989422804014327 * bell)


def norm_parts(values):
    centre = values - jnp.mean(values, axis=-1, keepdims=True)
    inverse = lax.rsqrt(jnp.mean(centre * centre, axis=-1, keepdims=True) + EPSILON)
    return centre * inverse, inverse


def norm_back(grad, unit, inverse, gain):
    scaled = grad * gain
    back = inverse * (
        scaled
        - jnp.mean(scaled, axis=-1, keepdims=True)
        - unit * jnp.mean(scaled * unit, axis=-1, keepdims=True)
    )
    return (
        back,
        jnp.sum(grad * unit, axis=0, keepdims=True),
        jnp.sum(grad, axis=0, keepdims=True),
    )


def middle_kernel(
    pieces,
    nz,
    al_in,
    x_in,
    og_in,
    ag_in,
    wo_in,
    wa_in,
    w1_in,
    w2_in,
    vec,
    expand_bias,
    align_bias,
    block_out,
    align_out,
    base,
    grad_parts,
    part_wo,
    part_wa,
    part_w1,
    part_w2,
    sums,
    al,
    x,
    og,
    ag,
    wo,
    wa,
    w1,
    w2,
    act,
    slope,
    block,
    align,
    base_v,
    grads,
    own_wo,
    own_wa,
    own_w1,
    own_w2,
    load_sem,
    store_sem,
):
    f32, b16 = jnp.float32, jnp.bfloat16
    width = x.shape[1]
    hidden = w1.shape[1]
    step = hidden // pieces
    cols = [slice(j * step, (j + 1) * step) for j in range(pieces)]
    loads = {}

    def load(name, source, to):
        loads[name] = pltpu.make_async_copy(source, to, load_sem.at[len(loads)])
        loads[name].start()

    load("wo", wo_in, wo)
    load("al", al_in, al)
    load("x", x_in, x)
    for j in range(pieces):
        load(("w1", j), w1_in.at[:, cols[j]], w1.at[:, cols[j]])
        load(("w2", j), w2_in.at[:, cols[j]], w2.at[:, cols[j]])
    load("wa", wa_in, wa)
    load("ag", ag_in, ag)
    load("og", og_in, og)
    stores = []

    def store(source, to):
        stores.append(pltpu.make_async_copy(source, to, store_sem.at[len(stores)]))
        stores[-1].start()

    def row(i):
        return vec[i : i + 1, :]

    sums[...] = jnp.zeros_like(sums)
    sums[0:1, :] = row(0)
    for name in ("wo", "al", "x"):
        loads[name].wait()
    x1 = x[...].astype(f32) + nn(al[...].T, wo[...]) + row(4)
    unit_two, inverse_two = norm_parts(x1)
    n2 = (unit_two * row(5) + row(6)).astype(b16)
    y = x1 + row(7)
    for j in range(pieces):
        loads["w1", j].wait()
        u = nn(n2, w1[:, cols[j]]) + expand_bias[:, cols[j]]
        value, derivative = gelu_pair(u)
        act[:, cols[j]] = value.astype(b16)
        slope[:, cols[j]] = derivative.astype(b16)
    for j in range(pieces):
        loads["w2", j].wait()
        y = y + nt(act[:, cols[j]], w2[:, cols[j]])
    block[...] = y.astype(b16)
    store(block, block_out)
    unit_three, inverse_three = norm_parts(y)
    n3 = (unit_three * row(8) + row(9)).astype(b16)
    loads["wa"].wait()
    loads["ag"].wait()
    align[...] = (nn(n3, wa[...]) + align_bias[...]).astype(b16)
    store(align, align_out)
    own_wa[...] = nn(n3.T, ag[...]).astype(b16)
    store(own_wa, part_wa)
    aligned = jnp.sum(ag[...].astype(f32), axis=0, keepdims=True)
    done = 0
    at = 10 + hidden // width
    while done < aligned.shape[1]:
        size = min(width, aligned.shape[1] - done)
        sums[at : at + 1, 0:size] = aligned[:, done : done + size]
        done, at = done + size, at + 1
    back, sums[8:9, :], sums[9:10, :] = norm_back(
        nt(ag[...], wa[...]), unit_three, inverse_three, row(8)
    )
    loads["og"].wait()
    gy = og[...].astype(f32) + back
    gm = gy.astype(b16)
    sums[7:8, :] = jnp.sum(gm.astype(f32), axis=0, keepdims=True)
    gm_t, n2_t = gm.T, n2.T
    gn2 = jnp.zeros(gy.shape, f32)
    for j in range(pieces):
        own_w2[:, cols[j]] = nn(gm_t, act[:, cols[j]]).astype(b16)
        store(own_w2.at[:, cols[j]], part_w2.at[:, cols[j]])
        gu = (nn(gm, w2[:, cols[j]]) * slope[:, cols[j]].astype(f32)).astype(b16)
        slope[:, cols[j]] = gu
        total = jnp.sum(gu.astype(f32), axis=0, keepdims=True)
        for k in range(0, step, width):
            at = (j * step + k) // width
            sums[10 + at : 11 + at, (j * step + k) % width : (j * step + k) % width + min(step, width)] = (
                total[:, k : k + width]
            )
        gn2 = gn2 + nt(gu, w1[:, cols[j]])
    back, sums[5:6, :], sums[6:7, :] = norm_back(gn2, unit_two, inverse_two, row(5))
    gx1 = gy + back
    base_v[...] = gx1
    store(base_v, base)
    go = gx1.astype(b16)
    sums[4:5, :] = jnp.sum(go.astype(f32), axis=0, keepdims=True)
    grads[...] = nt(wo[...], go).astype(b16)
    store(grads, grad_parts)
    for j in range(pieces):
        own_w1[:, cols[j]] = nn(n2_t, slope[:, cols[j]]).astype(b16)
        store(own_w1.at[:, cols[j]], part_w1.at[:, cols[j]])
    own_wo[...] = nn(al[...], go).astype(b16)
    store(own_wo, part_wo)
    for s in stores:
        s.wait()


def middle_call(al, x, og, ag, wo, wa, w1, w2, vec, expand_bias, align_bias, nz):
    f32, b16 = jnp.float32, jnp.bfloat16
    S = jax.ShapeDtypeStruct
    rows, width = x.shape
    hidden, wide = w1.shape[1], wa.shape[1]
    pieces = 4
    shapes = [al, x, og, ag, wo, wa, w1, w2]
    return pl.pallas_call(
        functools.partial(middle_kernel, pieces, nz),
        out_shape=(
            S((rows, width), b16),
            S((rows, wide), b16),
            S((rows, width), f32),
            S((width, rows), b16),
            S(wo.shape, b16),
            S(wa.shape, b16),
            S(w1.shape, b16),
            S(w2.shape, b16),
            S(vec.shape, f32),
        ),
        in_specs=[ANY] * 8 + [VM] * 3,
        out_specs=(ANY,) * 8 + (VM,),
        scratch_shapes=[pltpu.VMEM(a.shape, b16) for a in shapes]
        + [
            pltpu.VMEM((rows, hidden), b16),
            pltpu.VMEM((rows, hidden), b16),
            pltpu.VMEM((rows, width), b16),
            pltpu.VMEM((rows, wide), b16),
            pltpu.VMEM((rows, width), f32),
            pltpu.VMEM((width, rows), b16),
            pltpu.VMEM(wo.shape, b16),
            pltpu.VMEM(wa.shape, b16),
            pltpu.VMEM(w1.shape, b16),
            pltpu.VMEM(w2.shape, b16),
            pltpu.SemaphoreType.DMA((6 + 2 * pieces,)),
            pltpu.SemaphoreType.DMA((6 + 2 * pieces,)),
        ],
        compiler_params=pltpu.CompilerParams(vmem_limit_bytes=60 << 20),
    )(al, x, og, ag, wo, wa, w1, w2, vec, expand_bias, align_bias)


def local(
    tokens,
    segments,
    out_grad,
    align_grad,
    first_gain,
    first_shift,
    joint_weight,
    query_bias,
    value_bias,
    output_weight,
    output_bias,
    second_gain,
    second_shift,
    expand_bias,
    reduce_bias,
    head_gain,
    head_shift,
    align_weight,
    align_bias,
    expand_weight,
    reduce_weight,
):
    nd, nz = lax.axis_size("dp"), lax.axis_size("mp")
    n = nd * nz
    z = lax.axis_index("mp")
    rows, width = tokens.shape
    seq = rows * nz
    nh = H // nz
    own_cols = nh * HD
    f32, b16 = jnp.float32, jnp.bfloat16

    own = first_gain.shape[0]

    small = (
        first_gain,
        first_shift,
        query_bias,
        value_bias,
        output_bias,
        second_gain,
        second_shift,
        reduce_bias,
        head_gain,
        head_shift,
        expand_bias,
        align_bias,
    )
    flat, at = 0.0, 0
    for v in small:
        flat = flat + jnp.pad(v, (at, 16 * own - at - v.shape[0]))
        at += v.shape[0]
    vec = jnp.pad(flat.reshape(16, own).T, ((0, 0), (0, 112)))
    seg_row = segments.reshape(1, seq)
    vectors, joint_full, wo, wa, w1, w2, normed_all, qkv, att, lse, attended = forward_call(
        tokens,
        vec,
        joint_weight,
        output_weight,
        align_weight,
        expand_weight,
        reduce_weight.T,
        seg_row,
        nd,
        nz,
        nh,
        1,
    )
    joint_full = joint_full.reshape(width, 3 * width)
    output_full = wo.reshape(width, width)
    align_full = wa.reshape(width, -1)
    expand_full = w1.reshape(width, -1)
    reduce_full = w2.reshape(width, -1)
    attended = attended.reshape(width, rows)
    count = -(-expand_bias.shape[0] // own)
    bias_expand = (
        vectors[10 : 10 + count].reshape(count, n, own).transpose(1, 0, 2).reshape(n, count * own)
    )[:, : expand_bias.shape[0]].reshape(-1)
    count_align = -(-align_bias.shape[0] // own)
    bias_align = (
        vectors[10 + count : 10 + count + count_align]
        .reshape(count_align, n, own)
        .transpose(1, 0, 2)
        .reshape(n, count_align * own)
    )[:, : align_bias.shape[0]].reshape(-1)

    block_out, align_out, base, grad_parts, p_wo, p_wa, p_w1, p_w2, vec_in = middle_call(
        attended,
        tokens,
        out_grad,
        align_grad,
        output_full,
        align_full,
        expand_full,
        reduce_full,
        vectors,
        bias_expand[None],
        bias_align[None],
        nz,
    )
    hidden = expand_full.shape[1]
    tokens_grad, joint_mine, g_wo, g_wa, g_w1, g_w2, sums = backward_call(
        grad_parts.reshape(nz, own_cols, rows),
        p_wo.reshape(nd, nz, own, width),
        p_wa.reshape(nd, nz, own, -1),
        p_w1.reshape(nd, width // nd, hidden),
        p_w2.reshape(nd, width // nd, hidden),
        qkv,
        att,
        lse,
        seg_row,
        normed_all,
        joint_full,
        tokens,
        base,
        vec_in,
        nd,
        nz,
        nh,
        2,
    )
    g_joint = (
        joint_mine.reshape(nz, own, 3, own_cols).transpose(1, 2, 0, 3).reshape(own, 3 * width)
    )
    me = lax.axis_index("dp") * nz + z
    mine = lax.dynamic_slice_in_dim(sums[:10], me * own, own, axis=1)
    flat = sums[10:].reshape(-1)
    size_e, size_a = expand_bias.shape[0], align_bias.shape[0]
    g_expand_b = lax.dynamic_slice_in_dim(flat, me * size_e, size_e)
    g_align_b = lax.dynamic_slice_in_dim(flat, hidden + me * size_a, size_a)
    return (
        block_out,
        align_out,
        tokens_grad,
        mine[0],
        mine[1],
        g_joint,
        mine[2],
        mine[3],
        g_wo,
        mine[4],
        mine[5],
        mine[6],
        g_expand_b,
        mine[7],
        mine[8],
        mine[9],
        g_wa,
        g_align_b,
        g_w1,
        g_w2.T,
    )


def solution(mesh):
    both = P(("dp", "mp"))
    rows = P(("dp", "mp"), None)
    in_specs = (
        (rows, P("dp", None), rows, rows, both, both, rows, both, both, rows)
        + (both,) * 7
        + (rows, both, P("dp", "mp"), P("mp", "dp"))
    )
    out_specs = (
        (rows, rows, rows, both, both, rows, both, both, rows)
        + (both,) * 7
        + (rows, both, P("dp", "mp"), P("mp", "dp"))
    )
    return jax.shard_map(local, mesh=mesh, in_specs=in_specs, out_specs=out_specs, check_vma=False)
```

```python
import functools

import jax
import jax.numpy as jnp
from jax import lax
from jax.experimental import pallas as pl
from jax.experimental.pallas import tpu as pltpu
from jax.sharding import PartitionSpec as P

H = 12
HD = 64
EPSILON = 1e-06
NEG_FILL = -1000000000.0
MESH = pl.DeviceIdType.MESH
VMEM_LIMIT = 56 << 20


def layer_norm(values, gain, shift):
    centre = values - jnp.mean(values, axis=-1, keepdims=True)
    spread = jnp.mean(centre * centre, axis=-1, keepdims=True)
    return centre * lax.rsqrt(spread + EPSILON) * gain + shift


def nn(left, right):
    return lax.dot_general(
        left, right, (((1,), (0,)), ((), ())), preferred_element_type=jnp.float32
    )


def nt(left, right):
    return lax.dot_general(
        left, right, (((1,), (1,)), ((), ())), preferred_element_type=jnp.float32
    )


ANY = pl.BlockSpec(memory_space=pl.ANY)
VM = pl.BlockSpec(memory_space=pltpu.VMEM)


def peer_flip(index, bit):
    return index + bit * (1 - 2 * (index // bit % 2))


def mask_flip(index, mask):
    bit = 1
    while bit <= mask:
        if mask & bit:
            index = peer_flip(index, bit)
        bit *= 2
    return index


def plane_masks(order, step):
    masks = [0]
    for bit in order[:step]:
        masks += [m ^ bit for m in masks]
    return masks


class Spread:
    def __init__(self, slot, own, full, wide, nd, nz, dp, z, sems):
        self.slot, self.own, self.full, self.wide = slot, own, full, wide
        self.nd, self.nz, self.dp, self.z = nd, nz, dp, z
        self.keep_sem, self.right_sem, self.left_sem, self.line_sem, self.send_sem, self.recv_sem = sems
        self.bits = [1 << b for b in range(1, nd.bit_length() - 1)]
        self.cut = nz // 2

    def order(self, half):
        return self.bits if half == 0 else self.bits[::-1]

    def chunk(self, j):
        if self.wide:
            cols = self.own.shape[1]
            return self.full.at[self.dp, :, pl.ds(pl.multiple_of(j * cols, 128), cols)]
        return self.full.at[self.dp, j]

    def block(self, half, mask):
        d = mask_flip(self.dp, mask)
        lo, hi = (0, self.cut) if half == 0 else (self.cut, self.nz)
        if self.wide:
            cols = self.own.shape[1]
            return self.full.at[d, :, pl.ds(lo * cols, (hi - lo) * cols)]
        return self.full.at[d, pl.ds(lo, hi - lo)]

    def keep(self):
        return pltpu.make_async_copy(self.own, self.chunk(self.z), self.keep_sem.at[self.slot])

    def _right(self, step):
        j = jnp.maximum(self.z - step, 0)
        return pltpu.make_async_remote_copy(
            src_ref=self.own if step == 0 else self.chunk(j),
            dst_ref=self.chunk(j),
            send_sem=self.right_sem.at[self.slot, step],
            recv_sem=self.line_sem.at[self.slot, j],
            device_id=(self.dp, jnp.minimum(self.z + 1, self.nz - 1)),
            device_id_type=MESH,
        )

    def _left(self, step):
        j = jnp.minimum(self.z + step, self.nz - 1)
        return pltpu.make_async_remote_copy(
            src_ref=self.own if step == 0 else self.chunk(j),
            dst_ref=self.chunk(j),
            send_sem=self.left_sem.at[self.slot, step],
            recv_sem=self.line_sem.at[self.slot, j],
            device_id=(self.dp, jnp.maximum(self.z - 1, 0)),
            device_id_type=MESH,
        )

    def line_start(self, step):
        if step >= self.nz - 1:
            return

        @pl.when((self.z < self.nz - 1) & (self.z - step >= 0))
        def _():
            self._right(step).start()

        @pl.when((self.z > 0) & (self.z + step <= self.nz - 1))
        def _():
            self._left(step).start()

    def line_wait(self, step):
        @pl.when(self.z - step >= 0)
        def _():
            self._right(step).wait_recv()

        @pl.when(self.z + step <= self.nz - 1)
        def _():
            self._left(step).wait_recv()

    def _plane(self, half, mask, bit):
        return pltpu.make_async_remote_copy(
            src_ref=self.block(half, mask),
            dst_ref=self.block(half, mask),
            send_sem=self.send_sem.at[self.slot, half, mask ^ bit],
            recv_sem=self.recv_sem.at[self.slot, half, mask ^ bit],
            device_id=(peer_flip(self.dp, bit), self.z),
            device_id_type=MESH,
        )

    def _arrival(self, half, mask, bit):
        return pltpu.make_async_remote_copy(
            src_ref=self.block(half, mask),
            dst_ref=self.block(half, mask),
            send_sem=self.send_sem.at[self.slot, half, mask],
            recv_sem=self.recv_sem.at[self.slot, half, mask],
            device_id=(peer_flip(self.dp, bit), self.z),
            device_id_type=MESH,
        )

    def plane_start(self, step):
        if step >= len(self.bits):
            return
        for half in range(2):
            order = self.order(half)
            for mask in plane_masks(order, step):
                self._plane(half, mask, order[step]).start()

    def plane_wait(self, step):
        for half in range(2):
            order = self.order(half)
            for mask in plane_masks(order, step):
                self._arrival(half, mask ^ order[step], order[step]).wait_recv()

    def _new_masks(self, half, step):
        order = self.order(half)
        return [0] if step < 0 else [m ^ order[step] for m in plane_masks(order, step)]

    def core_start(self, step):
        for half in range(2):
            for mask in self._new_masks(half, step):
                self._plane(half, mask, 1).start()

    def core_wait(self):
        for half in range(2):
            for mask in plane_masks(self.bits, len(self.bits)):
                self._arrival(half, mask ^ 1, 1).wait_recv()

    def line_sends_wait(self):
        for step in range(self.nz - 1):

            @pl.when((self.z < self.nz - 1) & (self.z - step >= 0))
            def _():
                self._right(step).wait_send()

            @pl.when((self.z > 0) & (self.z + step <= self.nz - 1))
            def _():
                self._left(step).wait_send()

    def plane_sends_wait(self):
        for half in range(2):
            order = self.order(half)
            for step in range(len(self.bits)):
                for mask in plane_masks(order, step):
                    self._plane(half, mask, order[step]).wait_send()
            for mask in plane_masks(order, len(self.bits)):
                self._plane(half, mask, 1).wait_send()


def greet(nd, nz, dp, z, everyone=False):
    barrier = pltpu.get_barrier_semaphore()
    count = 0
    for off in range(1, nz):
        pl.semaphore_signal(
            barrier, inc=1, device_id=(dp, lax.rem(z + off, nz)), device_id_type=MESH
        )
        count += 1
    bits = [1 << b for b in range(nd.bit_length() - 1)]
    peers = (
        [lax.rem(dp + off, nd) for off in range(1, nd)]
        if everyone
        else [peer_flip(dp, bit) for bit in bits]
    )
    for peer in peers:
        pl.semaphore_signal(barrier, inc=1, device_id=(peer, z), device_id_type=MESH)
        count += 1
    pl.semaphore_wait(barrier, count)


def lane_copies(seg_row):
    return jnp.broadcast_to(seg_row[...], (128, seg_row.shape[1])).T


def gelu_pair(u):
    size = jnp.abs(u)
    t = 1.0 / (1.0 + (0.3275911 * 0.7071067811865476) * size)
    poly = ((((1.061405429 * t - 1.453152027) * t + 1.421413741) * t - 0.284496736) * t + 0.254829592) * t
    bell = jnp.exp(-0.5 * u * u)
    tail = 0.5 * poly * bell
    share = jnp.where(u >= 0.0, 1.0 - tail, tail)
    return u * share, share + u * (0.3989422804014327 * bell)


def norm_parts(values):
    centre = values - jnp.mean(values, axis=-1, keepdims=True)
    inverse = lax.rsqrt(jnp.mean(centre * centre, axis=-1, keepdims=True) + EPSILON)
    return centre * inverse, inverse


def norm_back(grad, unit, inverse, gain):
    scaled = grad * gain
    back = inverse * (
        scaled
        - jnp.mean(scaled, axis=-1, keepdims=True)
        - unit * jnp.mean(scaled * unit, axis=-1, keepdims=True)
    )
    return (
        back,
        jnp.sum(grad * unit, axis=0, keepdims=True),
        jnp.sum(grad, axis=0, keepdims=True),
    )


def forward_kernel(
    nd,
    nz,
    nh,
    size_e,
    size_a,
    x_own,
    og_in,
    ag_in,
    vec_own,
    joint_own,
    wo_own,
    wa_own,
    w1_own,
    w2_own,
    seg_row,
    block_out,
    align_out,
    base_out,
    grads_out,
    part_wo,
    part_wa,
    part_w1,
    part_w2,
    sums,
    joint,
    wo_land,
    wa_land,
    normed_out,
    qkv_out,
    att_out,
    lse,
    al_land,
    x_land,
    vec,
    window,
    w1,
    w2,
    vec_cols,
    vec_rows,
    bias_rows,
    weights,
    weights_t,
    wide,
    normed,
    qkv,
    att,
    keys,
    bias,
    seg_lanes,
    tops,
    totals,
    att_send,
    og,
    ag,
    wo,
    wa,
    act,
    slope,
    block,
    align,
    base,
    grads,
    keep_sem,
    right_sem,
    left_sem,
    line_sem,
    send_sem,
    recv_sem,
    x_sem,
    x_right,
    x_left,
    x_recv,
    win_send,
    win_recv,
    att_send_sem,
    att_recv_sem,
    out_sem,
    load_sem,
    store_sem,
):
    dp, z = lax.axis_index("dp"), lax.axis_index("mp")
    rows, width = x_own.shape
    seq = rows * nz
    own = vec_own.shape[0]
    own_cols = nh * HD
    win_cols = window.shape[-1] // 3
    win = z * own_cols // 128 * 128
    shift = pl.multiple_of(z * own_cols - win, HD)
    win = pl.multiple_of(win, 128)
    hidden, aligned = size_e * nd * nz, size_a * nd * nz
    f32, b16 = jnp.float32, jnp.bfloat16
    sems = (keep_sem, right_sem, left_sem, line_sem, send_sem, recv_sem)
    specs = [
        (vec_own, vec, False),
        (joint_own, joint, False),
        (wo_own, wo_land, False),
        (w1_own, w1, True),
        (w2_own, w2, True),
        (wa_own, wa_land, False),
        (joint_own, window, False),
    ]
    spreads = [Spread(i, *spec, nd, nz, dp, z, sems) for i, spec in enumerate(specs)]
    vecs, joints, early, late, heads = (
        spreads[:1],
        spreads[1:2],
        spreads[2:5],
        spreads[5:6],
        spreads[6:],
    )
    lined = spreads[:6]
    steps = len(spreads[0].bits)

    def line_step(group, step):
        for s in group:
            s.line_wait(step)
            s.line_start(step)

    def plane_open(group):
        for s in group:
            s.keep().wait()
            s.plane_start(0)
            s.core_start(-1)

    def plane_step(group, step):
        for s in group:
            s.plane_wait(step)
            s.plane_start(step + 1)
            s.core_start(step)

    def x_to_right(step):
        j = jnp.maximum(z - step, 0)
        return pltpu.make_async_remote_copy(
            src_ref=x_land.at[j],
            dst_ref=x_land.at[j],
            send_sem=x_right.at[step],
            recv_sem=x_recv.at[j],
            device_id=(dp, jnp.minimum(z + 1, nz - 1)),
            device_id_type=MESH,
        )

    def x_to_left(step):
        j = jnp.minimum(z + step, nz - 1)
        return pltpu.make_async_remote_copy(
            src_ref=x_land.at[j],
            dst_ref=x_land.at[j],
            send_sem=x_left.at[step],
            recv_sem=x_recv.at[j],
            device_id=(dp, jnp.maximum(z - 1, 0)),
            device_id_type=MESH,
        )

    def x_start(step):
        @pl.when((z < nz - 1) & (z - step >= 0))
        def _():
            x_to_right(step).start()

        @pl.when((z > 0) & (z + step <= nz - 1))
        def _():
            x_to_left(step).start()

    def piece(to, p):
        at = to * own_cols // 128 * 128 + p * width
        return joint_own.at[:, pl.ds(pl.multiple_of(at, 128), win_cols)]

    def piece_copy(off, p):
        to = lax.rem(z + off, nz)
        return pltpu.make_async_remote_copy(
            src_ref=piece(to, p),
            dst_ref=window.at[dp, z, :, pl.ds(p * win_cols, win_cols)],
            send_sem=win_send.at[off, p],
            recv_sem=win_recv.at[off, p],
            device_id=(dp, to),
            device_id_type=MESH,
        )

    def piece_keep(p):
        return pltpu.make_async_copy(
            piece(z, p), window.at[dp, z, :, pl.ds(p * win_cols, win_cols)], win_send.at[0, p]
        )

    og_load = pltpu.make_async_copy(og_in, og, load_sem.at[0])
    ag_load = pltpu.make_async_copy(ag_in, ag, load_sem.at[1])
    x_keep = pltpu.make_async_copy(x_own, x_land.at[z], x_sem)
    x_keep.start()
    greet(nd, nz, dp, z)
    for s in lined:
        s.keep().start()
    for s in vecs:
        s.line_start(0)
    for off in range(1, nz):
        for p in range(3):
            piece_copy(off, p).start()
    for p in range(3):
        piece_keep(p).start()
    for s in early:
        s.line_start(0)
    og_load.start()
    ag_load.start()
    for step in range(1, nz - 1):
        line_step(vecs, step)
    seg_lanes[...] = lane_copies(seg_row)
    for p in range(3):
        piece_keep(p).wait()
        for off in range(1, nz):
            piece_copy(off, p).wait_recv()
    for s in heads:
        s.plane_start(0)
        s.core_start(-1)
    line_step(vecs, nz - 1)
    plane_open(vecs)
    line_step(early, 1)
    plane_step(heads + vecs, 0)
    for step in range(2, nz - 1):
        line_step(early, step)
    x_keep.wait()
    x_start(0)
    line_step(early, nz - 1)
    plane_open(early)
    for t in range(1, steps):
        plane_step(heads + vecs, t)
    for s in heads + vecs:
        s.core_wait()

    for d in range(nd):
        for j in range(nz):
            at = (d * nz + j) * own
            vec_cols[at : at + own, :] = vec[d, j].astype(f32)
            weights[at : at + own, :] = window[d, j].astype(f32)
    vec_rows[...] = vec_cols[...].T[: vec_rows.shape[0]]
    for p in range(3):
        cols = slice(p * win_cols, (p + 1) * win_cols)
        weights_t[cols, :] = weights[:, cols].T.astype(b16)

    def row(i):
        return vec_rows[i : i + 1, :]

    bias_q = vec_cols[pl.ds(win, win_cols), 2:3]
    bias_v = vec_cols[pl.ds(win, win_cols), 3:4]

    def flatten(source, to):
        cols = to.shape[1]
        part = cols // -(-cols // window.shape[-1])
        for k in range(0, cols, part):
            load = pltpu.make_async_copy(
                source.at[:, :, :, pl.ds(k, part)], window.at[:, :, :, pl.ds(0, part)], load_sem.at[2]
            )
            load.start()
            load.wait()
            for d in range(nd):
                for j in range(nz):
                    at = (d * nz + j) * own
                    weights[at : at + own, :part] = window[d, j, :, :part].astype(f32)
            to[:, k : k + part] = weights[:, :part].astype(b16)

    def normed_copy(j):
        at = pl.ds(pl.multiple_of(j * rows, rows), rows)
        return pltpu.make_async_copy(normed.at[at], normed_out.at[at], out_sem.at[0, j])

    def qkv_copy(j):
        at = pl.ds(pl.multiple_of(j * rows, rows), rows)
        return pltpu.make_async_copy(qkv.at[:, at], qkv_out.at[:, at], out_sem.at[1, j])

    def att_keep(j):
        at = pl.ds(pl.multiple_of(j * rows, rows), rows)
        return pltpu.make_async_copy(att.at[:, at], att_out.at[:, at], out_sem.at[2, j])

    def att_copy(to):
        return pltpu.make_async_remote_copy(
            src_ref=att_send.at[to],
            dst_ref=al_land.at[z],
            send_sem=att_send_sem.at[lax.rem(to - z + nz, nz)],
            recv_sem=att_recv_sem.at[lax.rem(to - z + nz, nz)],
            device_id=(dp, to),
            device_id_type=MESH,
        )

    def project(j):
        at = pl.ds(pl.multiple_of(j * rows, rows), rows)
        normed[at, :] = layer_norm(x_land[j].astype(f32), row(0), row(1)).astype(b16)
        for p in range(3):
            part = nt(weights_t[p * win_cols : (p + 1) * win_cols, :], normed[at, :])
            if p == 0:
                part = part + bias_q
            if p == 2:
                part = part + bias_v
            wide[p * win_cols : (p + 1) * win_cols, :] = part.astype(b16)
            qkv[p * own_cols : (p + 1) * own_cols, at] = wide[
                pl.ds(p * win_cols + shift, own_cols), :
            ]
        for h in range(nh):
            keys[h, at, :] = wide[pl.ds(win_cols + shift + h * HD, HD), :].T
        tops[:, at] = jnp.full((tops.shape[0], rows), -jnp.inf, f32)
        totals[:, at] = jnp.zeros((totals.shape[0], rows), f32)
        att[:, at] = jnp.zeros((own_cols, rows), f32)
        normed_copy(j).start()
        qkv_copy(j).start()

    def pair(i, j):
        to = pl.ds(pl.multiple_of(i * rows, rows), rows)
        of = pl.ds(pl.multiple_of(j * rows, rows), rows)
        own_seg, lanes = seg_row[0:1, to], seg_lanes[of, :]
        bias[...] = jnp.concatenate(
            [
                jnp.where(lanes == own_seg[:, k : k + 128], 0.0, NEG_FILL)
                for k in range(0, rows, 128)
            ],
            axis=1,
        )
        for h in range(nh):
            query = qkv[h * HD : (h + 1) * HD, to] * jnp.bfloat16(0.125)
            score = nn(keys[h, of, :], query) + bias[...]
            top = tops[h : h + 1, to]
            new_top = jnp.maximum(top, jnp.max(score, axis=0, keepdims=True))
            weight = jnp.exp(score - new_top)
            fade = jnp.exp(top - new_top)
            tops[h : h + 1, to] = new_top
            totals[h : h + 1, to] = totals[h : h + 1, to] * fade + jnp.sum(
                weight, axis=0, keepdims=True
            )
            value = qkv[2 * own_cols + h * HD : 2 * own_cols + (h + 1) * HD, of]
            att[h * HD : (h + 1) * HD, to] = att[h * HD : (h + 1) * HD, to] * fade + nn(
                value, weight.astype(b16)
            )

    def finish(i):
        to = pl.ds(pl.multiple_of(i * rows, rows), rows)
        for h in range(nh):
            total = totals[h : h + 1, to]
            result = att[h * HD : (h + 1) * HD, to] / total
            att[h * HD : (h + 1) * HD, to] = result
            att_send[i, h * HD : (h + 1) * HD, :] = result.astype(b16)
            lse[h : h + 1, to] = tops[h : h + 1, to] + jnp.log(total)
        att_keep(i).start()

        @pl.when(i != z)
        def _():
            att_copy(i).start()

    def take(c, low, high, last):
        project(c)

        def old_queries(f, carry):
            pair(f, c)

            @pl.when(last)
            def _():
                finish(f)

            return carry

        def new_queries(f, carry):
            pair(c, f)
            return carry

        lax.fori_loop(low, high, old_queries, 0)
        lax.fori_loop(low, high, new_queries, 0)
        pair(c, c)

        @pl.when(last)
        def _():
            finish(c)

    project(z)
    pair(z, z)
    plane_step(early, 0)
    final = jnp.maximum(z, nz - 1 - z)

    def arrivals(step, carry):
        @pl.when(z - step >= 0)
        def _():
            x_to_right(step).wait_recv()

        @pl.when(z + step <= nz - 1)
        def _():
            x_to_left(step).wait_recv()

        @pl.when(step < nz - 1)
        def _():
            x_start(step)

        @pl.when(step == nz - 2)
        def _():
            for s in late:
                s.line_start(0)

        high = jnp.minimum(z + step, nz)

        @pl.when(z - step >= 0)
        def _():
            take(z - step, z - step + 1, high, (step == final) & (z + step > nz - 1))

        @pl.when(z + step <= nz - 1)
        def _():
            take(z + step, jnp.maximum(z - step, 0), high, step == final)

        @pl.when(step == nz - 2)
        def _():
            for t in range(1, steps):
                plane_step(early, t)
            for s in early:
                s.core_wait()
            for s in heads:
                s.plane_sends_wait()
            flatten(wo_land, wo)
            for k in range(nd * nz):
                bias_rows[0:1, k * size_e : (k + 1) * size_e] = vec_cols[
                    k * own : k * own + 1, 16 : 16 + size_e
                ]
                bias_rows[1:2, k * size_a : (k + 1) * size_a] = vec_cols[
                    k * own + 1 : k * own + 2, 16 : 16 + size_a
                ]

        return carry

    lax.fori_loop(1, nz, arrivals, 0)
    for step in range(1, nz):
        line_step(late, step)
    plane_open(late)
    for s in joints:
        s.line_start(0)
    al_land[z] = att_send[z]
    for off in range(1, nz):
        att_copy(lax.rem(z + off, nz)).wait()

    stores = []

    def store(source, to):
        stores.append(pltpu.make_async_copy(source, to, store_sem.at[len(stores)]))
        stores[-1].start()

    step = hidden // nz
    cols = [slice(j * step, (j + 1) * step) for j in range(nz)]

    def weight(full, j):
        return full[:, :, cols[j]].reshape(width, step)

    sums[...] = jnp.zeros_like(sums)
    sums[0:1, :] = row(0)
    al = al_land[...].reshape(width, rows)
    x1 = x_land[z].astype(f32) + nn(al.T, wo[...]) + row(4)
    unit_two, inverse_two = norm_parts(x1)
    n2 = (unit_two * row(5) + row(6)).astype(b16)
    y = x1 + row(7)
    plane_step(late, 0)
    line_step(joints, 1)
    for t in range(1, steps):
        plane_step(late, t)
    for j in range(nz):
        u = nn(n2, weight(w1, j)) + bias_rows[0:1, cols[j]]
        value, derivative = gelu_pair(u)
        act[:, cols[j]] = value.astype(b16)
        slope[:, cols[j]] = derivative.astype(b16)
        if j == 1:
            for t in range(2, nz):
                line_step(joints, t)
            plane_open(joints)
    for j in range(nz):
        y = y + nt(act[:, cols[j]], weight(w2, j))
    block[...] = y.astype(b16)
    store(block, block_out)
    unit_three, inverse_three = norm_parts(y)
    n3 = (unit_three * row(8) + row(9)).astype(b16)
    for s in late:
        s.core_wait()
    flatten(wa_land, wa)
    plane_step(joints, 0)
    align[...] = (nn(n3, wa[...]) + bias_rows[1:2, :aligned]).astype(b16)
    store(align, align_out)
    ag_load.wait()
    back = nt(ag[...], wa[...])
    total = jnp.sum(ag[...].astype(f32), axis=0, keepdims=True)
    at = 10 + hidden // width
    for k in range(0, aligned, width):
        size = min(width, aligned - k)
        sums[at : at + 1, 0:size] = total[:, k : k + size]
        at += 1
    wa[...] = nn(n3.T, ag[...]).astype(b16)
    store(wa, part_wa)
    back, sums[8:9, :], sums[9:10, :] = norm_back(back, unit_three, inverse_three, row(8))
    og_load.wait()
    gy = og[...].astype(f32) + back
    gm = gy.astype(b16)
    sums[7:8, :] = jnp.sum(gm.astype(f32), axis=0, keepdims=True)
    gm_t, n2_t = gm.T, n2.T
    for s in spreads[3:5]:
        s.line_sends_wait()
        s.plane_sends_wait()
    gn2 = jnp.zeros(gy.shape, f32)
    for j in range(nz):
        back = nn(gm, weight(w2, j))
        w2[:, :, cols[j]] = nn(gm_t, act[:, cols[j]]).astype(b16).reshape(nd, width // nd, step)
        store(w2.at[:, :, cols[j]], part_w2.at[:, :, cols[j]])
        gu = (back * slope[:, cols[j]].astype(f32)).astype(b16)
        slope[:, cols[j]] = gu
        total = jnp.sum(gu.astype(f32), axis=0, keepdims=True)
        for k in range(0, step, width):
            at = (j * step + k) // width
            sums[10 + at : 11 + at, 0:width] = total[:, k : k + width]
        gn2 = gn2 + nt(gu, weight(w1, j))
        if j == 1:
            for t in range(1, steps):
                plane_step(joints, t)
    back, sums[5:6, :], sums[6:7, :] = norm_back(gn2, unit_two, inverse_two, row(5))
    gx1 = gy + back
    base[...] = gx1
    store(base, base_out)
    go = gx1.astype(b16)
    sums[4:5, :] = jnp.sum(go.astype(f32), axis=0, keepdims=True)
    grads[...] = nt(wo[...], go).astype(b16)
    store(grads, grads_out)
    for j in range(nz):
        w1[:, :, cols[j]] = (
            nn(n2_t, slope[:, cols[j]]).astype(b16).reshape(nd, width // nd, step)
        )
        store(w1.at[:, :, cols[j]], part_w1.at[:, :, cols[j]])
    wo[...] = nn(al, go).astype(b16)
    store(wo, part_wo)
    for s in joints:
        s.core_wait()
    for j in range(nz):
        normed_copy(j).wait()
        qkv_copy(j).wait()
        att_keep(j).wait()
    for t in range(nz - 1):

        @pl.when((z < nz - 1) & (z - t >= 0))
        def _():
            x_to_right(t).wait_send()

        @pl.when((z > 0) & (z + t <= nz - 1))
        def _():
            x_to_left(t).wait_send()

    for off in range(1, nz):
        for p in range(3):
            piece_copy(off, p).wait_send()
    for s in spreads[:3] + spreads[5:6]:
        s.line_sends_wait()
    for s in spreads[:3] + spreads[5:6]:
        s.plane_sends_wait()
    for copy in stores:
        copy.wait()


def forward_call(
    x, og, ag, vec, joint, wo, wa, w1, w2, seg_row, nd, nz, nh, size_e, size_a, cid
):
    rows, width = x.shape
    seq, own_cols = rows * nz, nh * HD
    win_cols = -(-(own_cols + HD) // 128) * 128
    own = joint.shape[0]
    hidden, aligned = size_e * nd * nz, ag.shape[1]
    lines = 10 + hidden // width + -(-aligned // width)
    f32, b16 = jnp.float32, jnp.bfloat16
    S, D = jax.ShapeDtypeStruct, pltpu.SemaphoreType.DMA
    na = 7
    wide_shape = (nd, w1.shape[0], nz * w1.shape[1])
    return pl.pallas_call(
        functools.partial(forward_kernel, nd, nz, nh, size_e, size_a),
        out_shape=(
            S((rows, width), b16),
            S((rows, aligned), b16),
            S((rows, width), f32),
            S((width, rows), b16),
            S((width, width), b16),
            S((width, aligned), b16),
            S(wide_shape, b16),
            S(wide_shape, b16),
            S((lines, width), f32),
            S((nd, nz) + joint.shape, b16),
            S((nd, nz) + wo.shape, b16),
            S((nd, nz) + wa.shape, b16),
            S((seq, width), b16),
            S((3 * own_cols, seq), b16),
            S((own_cols, seq), f32),
            S((8, seq), f32),
        ),
        in_specs=[ANY] * 3 + [VM] * 7,
        out_specs=(ANY,) * 8 + (VM,) + (ANY,) * 6 + (VM,),
        scratch_shapes=[
            pltpu.VMEM((nz, own_cols, rows), b16),
            pltpu.VMEM((nz, rows, width), b16),
            pltpu.VMEM((nd, nz) + vec.shape, b16),
            pltpu.VMEM((nd, nz, own, 3 * win_cols), b16),
            pltpu.VMEM(wide_shape, b16),
            pltpu.VMEM(wide_shape, b16),
            pltpu.VMEM((width, vec.shape[1]), f32),
            pltpu.VMEM((16, width), f32),
            pltpu.VMEM((8, max(hidden, aligned)), f32),
            pltpu.VMEM((width, max(width, 3 * win_cols)), f32),
            pltpu.VMEM((3 * win_cols, width), b16),
            pltpu.VMEM((3 * win_cols, rows), b16),
            pltpu.VMEM((seq, width), b16),
            pltpu.VMEM((3 * own_cols, seq), b16),
            pltpu.VMEM((own_cols, seq), f32),
            pltpu.VMEM((nh, seq, HD), b16),
            pltpu.VMEM((rows, rows), f32),
            pltpu.VMEM((seq, 128), jnp.int32),
            pltpu.VMEM((8, seq), f32),
            pltpu.VMEM((8, seq), f32),
            pltpu.VMEM((nz, own_cols, rows), b16),
            pltpu.VMEM((rows, width), b16),
            pltpu.VMEM((rows, aligned), b16),
            pltpu.VMEM((width, width), b16),
            pltpu.VMEM((width, aligned), b16),
            pltpu.VMEM((rows, hidden), b16),
            pltpu.VMEM((rows, hidden), b16),
            pltpu.VMEM((rows, width), b16),
            pltpu.VMEM((rows, aligned), b16),
            pltpu.VMEM((rows, width), f32),
            pltpu.VMEM((width, rows), b16),
            D((na,)),
            D((na, nz)),
            D((na, nz)),
            D((na, nz)),
            D((na, 2, nd)),
            D((na, 2, nd)),
            D,
            D((nz,)),
            D((nz,)),
            D((nz,)),
            D((nz, 3)),
            D((nz, 3)),
            D((nz,)),
            D((nz,)),
            D((3, nz)),
            D((3,)),
            D((6 + 2 * nz,)),
        ],
        compiler_params=pltpu.CompilerParams(
            collective_id=cid, has_side_effects=True, vmem_limit_bytes=62 << 20
        ),
    )(x, og, ag, vec, joint, wo, wa, w1, w2, seg_row)


class Reduce:
    def __init__(self, slot, part, acc, land, plane, line, wide, nd, nz, dp, z, sems):
        self.slot, self.part, self.acc, self.land, self.plane, self.line = slot, part, acc, land, plane, line
        self.wide, self.nd, self.nz, self.dp, self.z = wide, nd, nz, dp, z
        self.load_sem, self.core_out, self.core_in, self.plane_out, self.plane_in, self.line_out, self.line_in = sems
        self.bits = [1 << b for b in range(1, nd.bit_length() - 1)]
        self.masks = plane_masks(self.bits, len(self.bits))
        self.cut = nz // 2
        self.cols = acc.shape[-1] // nz if wide else acc.shape[-1]

    def order(self, half):
        return self.bits if half == 0 else self.bits[::-1]

    def span(self, half):
        return (0, self.cut) if half == 0 else (self.cut, self.nz)

    def region(self, ref, i, half):
        lo, hi = self.span(half)
        if self.wide:
            return ref.at[i, :, pl.ds(lo * self.cols, (hi - lo) * self.cols)]
        return ref.at[i, pl.ds(lo, hi - lo)]

    def chunk(self, ref, i, j):
        if self.wide:
            at = j * self.cols
            at = at if isinstance(at, int) else pl.multiple_of(at, 128)
            return ref.at[i, :, pl.ds(at, self.cols)]
        return ref.at[i, j]

    def slots(self, half, step):
        order, base = self.order(half), 0
        for t in range(step):
            base += 1 << (len(order) - 1 - t)
        rest = plane_masks(order[step + 1 :], len(order) - step - 1)
        return [(m, base + k) for k, m in enumerate(rest)]

    def _load(self, m):
        return pltpu.make_async_copy(
            self.part.at[mask_flip(self.dp, m)], self.acc.at[m >> 1], self.load_sem.at[self.slot, m >> 1]
        )

    def _core(self, m):
        return pltpu.make_async_remote_copy(
            src_ref=self.part.at[mask_flip(self.dp, m ^ 1)],
            dst_ref=self.land.at[m >> 1],
            send_sem=self.core_out.at[self.slot, m >> 1],
            recv_sem=self.core_in.at[self.slot, m >> 1],
            device_id=(peer_flip(self.dp, 1), self.z),
            device_id_type=MESH,
        )

    def core_start(self):
        for m in self.masks:
            self._core(m).start()
        for m in self.masks:
            self._load(m).start()

    def _add(self, i, source, k, half):
        lo, hi = self.span(half)

        def step(j, carry):
            to, more = self.chunk(self.acc, i, j), self.chunk(source, k, j)
            to[...] = (to[...].astype(jnp.float32) + more[...].astype(jnp.float32)).astype(to.dtype)
            return carry

        lax.fori_loop(lo, hi, step, 0)

    def core_add(self):
        for m in self.masks:
            self._load(m).wait()
            self._core(m).wait_recv()
            for half in range(2):
                self._add(m >> 1, self.land, m >> 1, half)

    def _plane(self, half, step, m, place):
        bit = self.order(half)[step]
        return pltpu.make_async_remote_copy(
            src_ref=self.region(self.acc, (m ^ bit) >> 1, half),
            dst_ref=self.region(self.plane, place, half),
            send_sem=self.plane_out.at[self.slot, half, place],
            recv_sem=self.plane_in.at[self.slot, half, place],
            device_id=(peer_flip(self.dp, bit), self.z),
            device_id_type=MESH,
        )

    def plane_start(self, step):
        if step < len(self.bits):
            for half in range(2):
                for m, place in self.slots(half, step):
                    self._plane(half, step, m, place).start()

    def plane_add(self, step):
        for half in range(2):
            for m, place in self.slots(half, step):
                self._plane(half, step, m, place).wait_recv()
                self._add(m >> 1, self.plane, place, half)

    def _line(self, off):
        to = lax.rem(self.z + off, self.nz)
        return pltpu.make_async_remote_copy(
            src_ref=self.chunk(self.acc, 0, to),
            dst_ref=self.line.at[off],
            send_sem=self.line_out.at[self.slot, off],
            recv_sem=self.line_in.at[self.slot, off],
            device_id=(self.dp, to),
            device_id_type=MESH,
        )

    def line_start(self):
        for off in range(1, self.nz):
            self._line(off).start()

    def line_wait(self):
        for off in range(1, self.nz):
            self._line(off).wait_recv()

    def _hop(self, j, way):
        to = jnp.clip(self.z + way, 0, self.nz - 1)
        place = j if way < 0 else jnp.where(j == to, self.nz, j)
        return pltpu.make_async_remote_copy(
            src_ref=self.chunk(self.acc, 0, j),
            dst_ref=self.line.at[place],
            send_sem=self.line_out.at[self.slot, j],
            recv_sem=self.line_in.at[self.slot, place],
            device_id=(self.dp, to),
            device_id_type=MESH,
        )

    def _landed(self, place):
        return pltpu.make_async_remote_copy(
            src_ref=self.line.at[place],
            dst_ref=self.line.at[place],
            send_sem=self.line_out.at[self.slot, 0],
            recv_sem=self.line_in.at[self.slot, place],
            device_id=(self.dp, self.z),
            device_id_type=MESH,
        )

    def hop(self, j, way, first):
        @pl.when(jnp.logical_not(first))
        def _():
            self._landed(j).wait_recv()
            to = self.chunk(self.acc, 0, j)
            to[...] = (to[...].astype(jnp.float32) + self.line[j].astype(jnp.float32)).astype(to.dtype)

        self._hop(j, way).start()

    def home(self):
        total = self.chunk(self.acc, 0, self.z)
        self.total[...] = total[...].astype(jnp.float32)

        @pl.when(self.z < self.nz - 1)
        def _():
            self._landed(self.z).wait_recv()
            self.total[...] += self.line[self.z].astype(jnp.float32)

        @pl.when(self.z > 0)
        def _():
            self._landed(self.nz).wait_recv()
            self.total[...] += self.line[self.nz].astype(jnp.float32)

    def hops_wait(self):
        def step(j, carry):
            @pl.when(j != self.z)
            def _():
                self._hop(j, -1).wait_send()

            return carry

        lax.fori_loop(0, self.nz, step, 0)

    def sends_wait(self):
        for m in self.masks:
            self._core(m).wait_send()
        for half in range(2):
            for step in range(len(self.bits)):
                for m, place in self.slots(half, step):
                    self._plane(half, step, m, place).wait_send()


def backward_kernel(
    nd,
    nz,
    nh,
    grad_parts,
    part_wo,
    part_wa,
    part_w1,
    part_w2,
    qkv_in,
    att_in,
    normed_in,
    joint_in,
    x_in,
    base_in,
    lse,
    seg_row,
    vec_in,
    tokens_grad,
    out_joint,
    out_wo,
    out_wa,
    out_w1,
    out_w2,
    out_vec,
    grad_land,
    keys,
    values,
    key_grad,
    value_grad,
    turned,
    staged,
    rows_land,
    part_joint,
    bias_cols,
    seg_lanes,
    vec_stage,
    vec_land,
    vec_line,
    qkv,
    att,
    normed,
    joint_full,
    x_own,
    base,
    in_sem,
    *rest,
):
    na = 5
    buffers = [rest[4 * a : 4 * a + 4] for a in range(na)]
    (
        load_sem,
        core_out,
        core_in,
        plane_out,
        plane_in,
        line_out,
        line_in,
        grad_out,
        grad_in,
        row_out,
        row_in,
        vec_out,
        vec_in_sem,
        vec_line_out,
        vec_line_in,
        own_sem,
    ) = rest[4 * na :]
    dp, z = lax.axis_index("dp"), lax.axis_index("mp")
    rows, width = x_own.shape
    seq = rows * nz
    own_cols = nh * HD
    f32, b16 = jnp.float32, jnp.bfloat16
    sems = (load_sem, core_out, core_in, plane_out, plane_in, line_out, line_in)
    parts = [(part_w2, True), (part_w1, True), (part_wa, False), (part_wo, False), (part_joint, False)]
    reduces = [
        Reduce(a, part, *buffers[a], wide, nd, nz, dp, z, sems) for a, (part, wide) in enumerate(parts)
    ]
    big, joint = reduces[:4], reduces[4]
    for r, out in zip(big, (out_w2, out_w1, out_wa, out_wo)):
        r.total = out
    steps = len(joint.bits)

    loads = [
        pltpu.make_async_copy(source, to, in_sem.at[i])
        for i, (source, to) in enumerate(
            zip(
                (qkv_in, att_in, normed_in, joint_in, x_in, base_in),
                (qkv, att, normed, joint_full, x_own, base),
            )
        )
    ]
    for copy in loads:
        copy.start()
    greet(nd, nz, dp, z, everyone=True)

    def grad_copy(h, off):
        to = lax.rem(z + off, nz)
        return pltpu.make_async_remote_copy(
            src_ref=grad_parts.at[to, pl.ds(h * HD, HD)],
            dst_ref=grad_land.at[z, pl.ds(h * HD, HD)],
            send_sem=grad_out.at[h, off],
            recv_sem=grad_in.at[h, off],
            device_id=(dp, to),
            device_id_type=MESH,
        )

    grad_own = pltpu.make_async_copy(grad_parts.at[z], grad_land.at[z], own_sem)
    grad_own.start()
    for off in range(1, nz):
        grad_copy(0, off).start()
    for r in big:
        r.core_start()
    loads[0].wait()
    for h in range(nh):
        keys[h] = qkv[own_cols + h * HD : own_cols + (h + 1) * HD, :].T
        values[h] = qkv[2 * own_cols + h * HD : 2 * own_cols + (h + 1) * HD, :].T
    bias_cols[...] = jnp.zeros_like(bias_cols)
    seg_lanes[...] = lane_copies(seg_row)
    kc = min(512, seq)

    def row_copy(h, off):
        to = lax.rem(z + off, nz)
        return pltpu.make_async_remote_copy(
            src_ref=staged.at[to, :, pl.ds(h * HD, HD)],
            dst_ref=rows_land.at[:, z, pl.ds(h * HD, HD)],
            send_sem=row_out.at[h, off],
            recv_sem=row_in.at[h, off],
            device_id=(dp, to),
            device_id_type=MESH,
        )

    def chores(u):
        if u == 0:
            big[1].core_add()
            big[1].plane_start(0)
        if u == 1:
            for r in big[2:]:
                r.core_add()
                r.plane_start(0)
        if u == 4:
            big[0].plane_add(0)
            big[0].plane_start(1)
        if u == 6:
            vec_sum(1)
        if u == 7:
            big[1].plane_add(0)
            big[1].plane_start(1)
        if u == 9:
            for r in big[2:]:
                r.plane_add(0)
                r.plane_start(1)

    def vec_copy(part, off):
        span = pl.ds(8 * part, 8)
        return pltpu.make_async_remote_copy(
            src_ref=vec_stage.at[0, span],
            dst_ref=vec_land.at[off, span],
            send_sem=vec_out.at[part, off],
            recv_sem=vec_in_sem.at[part, off],
            device_id=(lax.rem(dp + off, nd), z),
            device_id_type=MESH,
        )

    def vec_line_copy(part, off):
        span = pl.ds(8 * part, 8)
        return pltpu.make_async_remote_copy(
            src_ref=vec_stage.at[1, span],
            dst_ref=vec_line.at[off, span],
            send_sem=vec_line_out.at[part, off],
            recv_sem=vec_line_in.at[part, off],
            device_id=(dp, lax.rem(z + off, nz)),
            device_id_type=MESH,
        )

    def vec_sum(part):
        span = slice(8 * part, 8 * part + 8)
        total = vec_stage[0, span, :]
        for off in range(1, nd):
            vec_copy(part, off).wait_recv()
            total = total + vec_land[off, span, :]
        vec_stage[1, span, :] = total
        for off in range(1, nz):
            vec_line_copy(part, off).start()

    vec_stage[0] = vec_in[...]
    for off in range(1, nd):
        vec_copy(1, off).start()
    big[0].core_add()
    big[0].plane_start(0)
    grad_own.wait()
    loads[1].wait()
    for h in range(nh):
        for off in range(1, nz):
            grad_copy(h, off).wait_recv()
        if h == 0:
            for later in range(1, nh):
                for off in range(1, nz):
                    grad_copy(later, off).start()
        key_grad[...] = jnp.zeros_like(key_grad)
        value_grad[...] = jnp.zeros_like(value_grad)

        def block(i, carry):
            start = pl.multiple_of(i * rows, rows)
            own_seg = seg_row[0:1, pl.ds(start, rows)]
            query = qkv[h * HD : (h + 1) * HD, pl.ds(start, rows)] * jnp.bfloat16(0.125)
            back = grad_land[i, h * HD : (h + 1) * HD, :]
            row_term = jnp.sum(
                back.astype(f32) * att[h * HD : (h + 1) * HD, pl.ds(start, rows)],
                axis=0,
                keepdims=True,
            )
            log_total = lse[h : h + 1, pl.ds(start, rows)]
            query_grad = jnp.zeros((HD, rows), f32)
            for c in range(0, seq, kc):
                chunk = slice(c, c + kc)
                lanes = seg_lanes[chunk, :]
                allowed = jnp.concatenate(
                    [lanes == own_seg[:, k : k + 128] for k in range(0, rows, 128)], axis=1
                )
                score = nn(keys[h, chunk, :], query)
                weight = jnp.where(allowed, jnp.exp(score - log_total), 0.0)
                value_grad[chunk, :] += nt(weight.astype(b16), back)
                weight_grad = nn(values[h, chunk, :], back)
                score_grad = (weight * (weight_grad - row_term)).astype(b16)
                key_grad[chunk, :] += nt(score_grad, query)
                query_grad = query_grad + nn(
                    qkv[own_cols + h * HD : own_cols + (h + 1) * HD, chunk], score_grad
                )
            staged[i, 0, h * HD : (h + 1) * HD, :] = (query_grad * 0.125).astype(b16)
            for b in range(nz):
                u = h * nz + b

                @pl.when(i == b)
                def _():
                    chores(u)

            return carry

        lax.fori_loop(0, nz, block, 0)
        for p, source in ((1, key_grad), (2, value_grad)):
            turned[...] = source[...].T
            for j in range(nz):
                staged[j, p, h * HD : (h + 1) * HD, :] = turned[:, j * rows : (j + 1) * rows].astype(b16)
        for off in range(1, nz):
            row_copy(h, off).start()
        rows_land[:, z, h * HD : (h + 1) * HD, :] = staged[z, :, h * HD : (h + 1) * HD, :]
        at = pl.ds(pl.multiple_of(z * own_cols + h * HD, HD), HD)
        for col, p in ((0, 0), (1, 2)):
            total = jnp.zeros((HD, 1), f32)
            for j in range(nz):
                total = total + jnp.sum(
                    staged[j, p, h * HD : (h + 1) * HD, :].astype(f32), axis=1, keepdims=True
                )
            bias_cols[at, col : col + 1] = total

    def stream(r, way):
        def left(j, carry):
            r.hop(j, -1, z == nz - 1)
            return carry

        def right(k, carry):
            r.hop(nz - 1 - k, 1, z == 0)
            return carry

        if way < 0:
            lax.fori_loop(0, z, left, 0)
        else:
            lax.fori_loop(0, nz - 1 - z, right, 0)

    for r in big:
        for t in range(1, steps):
            r.plane_add(t)
            r.plane_start(t + 1)

        @pl.when(z == nz - 1)
        def _():
            stream(r, -1)

        @pl.when(z == 0)
        def _():
            stream(r, 1)

    for copy in loads[2:]:
        copy.wait()
    grad_t = jnp.zeros((3 * own_cols, width), f32)
    for j in range(nz):
        grad_t = grad_t + nn(
            staged[j].reshape(3 * own_cols, rows), normed[j * rows : (j + 1) * rows, :]
        )
    grad_joint = grad_t.T
    own = part_joint.shape[2]
    for d in range(nd):
        for j in range(nz):
            at = (d * nz + j) * own
            part_joint[d, j] = grad_joint[at : at + own, :].astype(b16)
    joint.core_start()
    joint.core_add()
    joint.plane_start(0)
    for t in range(steps):
        joint.plane_add(t)
        joint.plane_start(t + 1)
    joint.line_start()

    @pl.when((z > 0) & (z < nz // 2))
    def _():
        for r in big:
            stream(r, 1)

    @pl.when((z >= nz // 2) & (z < nz - 1))
    def _():
        for r in big:
            stream(r, -1)

    for h in range(nh):
        for off in range(1, nz):
            row_copy(h, off).wait_recv()
    back_t = nn(joint_full[...], rows_land[...].reshape(3 * width, rows))
    back = back_t.T
    gain = vec_in[0:1, :]
    x = x_own[...].astype(f32)
    centre = x - jnp.mean(x, axis=-1, keepdims=True)
    inverse = lax.rsqrt(jnp.mean(centre * centre, axis=-1, keepdims=True) + EPSILON)
    unit = centre * inverse
    scaled = back * gain
    tokens_grad[...] = base[...] + inverse * (
        scaled
        - jnp.mean(scaled, axis=-1, keepdims=True)
        - unit * jnp.mean(scaled * unit, axis=-1, keepdims=True)
    )
    bias_rows = bias_cols[...].T
    vec_stage[0, 0:1, :] = jnp.sum(back * unit, axis=0, keepdims=True)
    vec_stage[0, 1:2, :] = jnp.sum(back, axis=0, keepdims=True)
    vec_stage[0, 2:4, :] = bias_rows[0:2, :]
    for off in range(1, nd):
        vec_copy(0, off).start()

    @pl.when((z > 0) & (z < nz // 2))
    def _():
        for r in big:
            stream(r, -1)

    @pl.when((z >= nz // 2) & (z < nz - 1))
    def _():
        for r in big:
            stream(r, 1)

    vec_sum(0)

    for r in big:
        r.home()
    joint.line_wait()
    joint.line[0] = joint.acc[0, z]
    for j in range(nz):
        piece = joint.line[lax.rem(z - j + nz, nz)].astype(f32)
        for p in range(3):
            out_joint[:, p * width + j * own_cols : p * width + (j + 1) * own_cols] = piece[
                :, p * own_cols : (p + 1) * own_cols
            ]
    total = vec_stage[1]
    for off in range(1, nz):
        for part in range(2):
            vec_line_copy(part, off).wait_recv()
        total = total + vec_line[off]
    out_vec[...] = total
    for part in range(2):
        for off in range(1, nd):
            vec_copy(part, off).wait_send()
        for off in range(1, nz):
            vec_line_copy(part, off).wait_send()
    for off in range(1, nz):
        for h in range(nh):
            grad_copy(h, off).wait_send()
            row_copy(h, off).wait_send()
        joint._line(off).wait_send()
    for r in reduces:
        r.sends_wait()
    for r in big:
        r.hops_wait()


def backward_call(
    grad_parts, wo, wa, w1, w2, qkv, att, normed, joint_full, x_own, base, lse, seg_row, vec_in, nd, nz, nh, cid
):
    rows, width = x_own.shape
    seq, own_cols = rows * nz, nh * HD
    own = width // (nd * nz)
    f32, b16 = jnp.float32, jnp.bfloat16
    S, D = jax.ShapeDtypeStruct, pltpu.SemaphoreType.DMA
    joint_shape = (nd, nz, own, 3 * own_cols)
    held = []
    for shape, wide in ((w2.shape, True), (w1.shape, True), (wa.shape, False), (wo.shape, False), (joint_shape, False)):
        piece = shape[1:]
        line = (nz + 1, piece[0], piece[1] // nz) if wide else (nz + 1,) + piece[1:]
        held += [
            pltpu.VMEM((nd // 2,) + piece, b16),
            pltpu.VMEM((nd // 2,) + piece, b16),
            pltpu.VMEM((max(nd // 2 - 1, 1),) + piece, b16),
            pltpu.VMEM(line, b16),
        ]
    na = 5
    return pl.pallas_call(
        functools.partial(backward_kernel, nd, nz, nh),
        out_shape=(
            S((rows, width), f32),
            S((own, 3 * width), f32),
            S(wo.shape[2:], f32),
            S(wa.shape[2:], f32),
            S((w1.shape[1], w1.shape[2] // nz), f32),
            S((w2.shape[1], w2.shape[2] // nz), f32),
            S(vec_in.shape, f32),
        ),
        in_specs=[ANY] * 11 + [VM] * 3,
        out_specs=(VM,) * 7,
        scratch_shapes=[
            pltpu.VMEM((nz, own_cols, rows), b16),
            pltpu.VMEM((nh, seq, HD), b16),
            pltpu.VMEM((nh, seq, HD), b16),
            pltpu.VMEM((seq, HD), f32),
            pltpu.VMEM((seq, HD), f32),
            pltpu.VMEM((HD, seq), f32),
            pltpu.VMEM((nz, 3, own_cols, rows), b16),
            pltpu.VMEM((3, nz, own_cols, rows), b16),
            pltpu.VMEM(joint_shape, b16),
            pltpu.VMEM((width, 128), f32),
            pltpu.VMEM((seq, 128), jnp.int32),
            pltpu.VMEM((2,) + vec_in.shape, f32),
            pltpu.VMEM((nd,) + vec_in.shape, f32),
            pltpu.VMEM((nz,) + vec_in.shape, f32),
            pltpu.VMEM(qkv.shape, b16),
            pltpu.VMEM(att.shape, f32),
            pltpu.VMEM(normed.shape, b16),
            pltpu.VMEM(joint_full.shape, b16),
            pltpu.VMEM(x_own.shape, b16),
            pltpu.VMEM(base.shape, f32),
            D((6,)),
        ]
        + held
        + [
            D((na, nd // 2)),
            D((na, nd // 2)),
            D((na, nd // 2)),
            D((na, 2, nd // 2)),
            D((na, 2, nd // 2)),
            D((na, nz + 1)),
            D((na, nz + 1)),
            D((nh, nz)),
            D((nh, nz)),
            D((nh, nz)),
            D((nh, nz)),
            D((2, nd)),
            D((2, nd)),
            D((2, nz)),
            D((2, nz)),
            D,
        ],
        compiler_params=pltpu.CompilerParams(
            collective_id=cid, has_side_effects=True, vmem_limit_bytes=63 << 20
        ),
    )(grad_parts, wo, wa, w1, w2, qkv, att, normed, joint_full, x_own, base, lse, seg_row, vec_in)


def local(
    tokens,
    segments,
    out_grad,
    align_grad,
    first_gain,
    first_shift,
    joint_weight,
    query_bias,
    value_bias,
    output_weight,
    output_bias,
    second_gain,
    second_shift,
    expand_bias,
    reduce_bias,
    head_gain,
    head_shift,
    align_weight,
    align_bias,
    expand_weight,
    reduce_weight,
):
    nd, nz = lax.axis_size("dp"), lax.axis_size("mp")
    n = nd * nz
    z = lax.axis_index("mp")
    rows, width = tokens.shape
    seq = rows * nz
    nh = H // nz
    own_cols = nh * HD
    f32, b16 = jnp.float32, jnp.bfloat16

    own = first_gain.shape[0]

    small = (
        first_gain,
        first_shift,
        query_bias,
        value_bias,
        output_bias,
        second_gain,
        second_shift,
        reduce_bias,
        head_gain,
        head_shift,
    )
    flat = 0.0
    for i, v in enumerate(small):
        flat = flat + jnp.pad(v, (i * own, (15 - i) * own))
    size_e, size_a = expand_bias.shape[0], align_bias.shape[0]
    vec = (
        jnp.pad(flat.reshape(16, own).T, ((0, 0), (0, 112)))
        + jnp.pad(expand_bias[None], ((0, own - 1), (16, 112 - size_e)))
        + jnp.pad(align_bias[None], ((1, own - 2), (16, 112 - size_a)))
    )
    seg_row = segments.reshape(1, seq)
    (
        block_out,
        align_out,
        base,
        grad_parts,
        p_wo,
        p_wa,
        p_w1,
        p_w2,
        vec_in,
        joint_full,
        _,
        _,
        normed_all,
        qkv,
        att,
        lse,
    ) = forward_call(
        tokens,
        out_grad,
        align_grad,
        vec,
        joint_weight,
        output_weight,
        align_weight,
        expand_weight,
        reduce_weight.T,
        seg_row,
        nd,
        nz,
        nh,
        size_e,
        size_a,
        1,
    )
    joint_full = joint_full.reshape(width, 3 * width)
    hidden = size_e * n
    tokens_grad, g_joint, g_wo, g_wa, g_w1, g_w2, sums = backward_call(
        grad_parts.reshape(nz, own_cols, rows),
        p_wo.reshape(nd, nz, own, width),
        p_wa.reshape(nd, nz, own, -1),
        p_w1,
        p_w2,
        qkv,
        att,
        normed_all,
        joint_full,
        tokens,
        base,
        lse,
        seg_row,
        vec_in,
        nd,
        nz,
        nh,
        2,
    )
    me = lax.axis_index("dp") * nz + z
    mine = lax.dynamic_slice_in_dim(sums[:10], me * own, own, axis=1)
    flat = sums[10:].reshape(-1)
    g_expand_b = lax.dynamic_slice_in_dim(flat, me * size_e, size_e)
    g_align_b = lax.dynamic_slice_in_dim(flat, hidden + me * size_a, size_a)
    return (
        block_out,
        align_out,
        tokens_grad,
        mine[0],
        mine[1],
        g_joint,
        mine[2],
        mine[3],
        g_wo,
        mine[4],
        mine[5],
        mine[6],
        g_expand_b,
        mine[7],
        mine[8],
        mine[9],
        g_wa,
        g_align_b,
        g_w1,
        g_w2.T,
    )


def solution(mesh):
    both = P(("dp", "mp"))
    rows = P(("dp", "mp"), None)
    in_specs = (
        (rows, P("dp", None), rows, rows, both, both, rows, both, both, rows)
        + (both,) * 7
        + (rows, both, P("dp", "mp"), P("mp", "dp"))
    )
    out_specs = (
        (rows, rows, rows, both, both, rows, both, both, rows)
        + (both,) * 7
        + (rows, both, P("dp", "mp"), P("mp", "dp"))
    )
    return jax.shard_map(local, mesh=mesh, in_specs=in_specs, out_specs=out_specs, check_vma=False)
```

```python
import functools

import jax
import jax.numpy as jnp
from jax import lax
from jax.experimental import pallas as pl
from jax.experimental.pallas import tpu as pltpu
from jax.sharding import PartitionSpec as P

H = 12
HD = 64
EPSILON = 1e-06
NEG_FILL = -1000000000.0
MESH = pl.DeviceIdType.MESH
VMEM_LIMIT = 56 << 20


def layer_norm(values, gain, shift):
    centre = values - jnp.mean(values, axis=-1, keepdims=True)
    spread = jnp.mean(centre * centre, axis=-1, keepdims=True)
    return centre * lax.rsqrt(spread + EPSILON) * gain + shift


def nn(left, right):
    return lax.dot_general(
        left, right, (((1,), (0,)), ((), ())), preferred_element_type=jnp.float32
    )


def nt(left, right):
    return lax.dot_general(
        left, right, (((1,), (1,)), ((), ())), preferred_element_type=jnp.float32
    )


ANY = pl.BlockSpec(memory_space=pl.ANY)
VM = pl.BlockSpec(memory_space=pltpu.VMEM)


def peer_flip(index, bit):
    return index + bit * (1 - 2 * (index // bit % 2))


def mask_flip(index, mask):
    bit = 1
    while bit <= mask:
        if mask & bit:
            index = peer_flip(index, bit)
        bit *= 2
    return index


def plane_masks(order, step):
    masks = [0]
    for bit in order[:step]:
        masks += [m ^ bit for m in masks]
    return masks


class Spread:
    def __init__(self, slot, own, full, wide, nd, nz, dp, z, sems):
        self.slot, self.own, self.full, self.wide = slot, own, full, wide
        self.nd, self.nz, self.dp, self.z = nd, nz, dp, z
        self.keep_sem, self.right_sem, self.left_sem, self.line_sem, self.send_sem, self.recv_sem = sems
        self.bits = [1 << b for b in range(1, nd.bit_length() - 1)]
        self.cut = nz // 2

    def order(self, half):
        return self.bits if half == 0 else self.bits[::-1]

    def chunk(self, j):
        if self.wide:
            cols = self.own.shape[1]
            return self.full.at[self.dp, :, pl.ds(pl.multiple_of(j * cols, 128), cols)]
        return self.full.at[self.dp, j]

    def block(self, half, mask):
        d = mask_flip(self.dp, mask)
        lo, hi = (0, self.cut) if half == 0 else (self.cut, self.nz)
        if self.wide:
            cols = self.own.shape[1]
            return self.full.at[d, :, pl.ds(lo * cols, (hi - lo) * cols)]
        return self.full.at[d, pl.ds(lo, hi - lo)]

    def keep(self):
        return pltpu.make_async_copy(self.own, self.chunk(self.z), self.keep_sem.at[self.slot])

    def _right(self, step):
        j = jnp.maximum(self.z - step, 0)
        return pltpu.make_async_remote_copy(
            src_ref=self.own if step == 0 else self.chunk(j),
            dst_ref=self.chunk(j),
            send_sem=self.right_sem.at[self.slot, step],
            recv_sem=self.line_sem.at[self.slot, j],
            device_id=(self.dp, jnp.minimum(self.z + 1, self.nz - 1)),
            device_id_type=MESH,
        )

    def _left(self, step):
        j = jnp.minimum(self.z + step, self.nz - 1)
        return pltpu.make_async_remote_copy(
            src_ref=self.own if step == 0 else self.chunk(j),
            dst_ref=self.chunk(j),
            send_sem=self.left_sem.at[self.slot, step],
            recv_sem=self.line_sem.at[self.slot, j],
            device_id=(self.dp, jnp.maximum(self.z - 1, 0)),
            device_id_type=MESH,
        )

    def line_start(self, step):
        if step >= self.nz - 1:
            return

        @pl.when((self.z < self.nz - 1) & (self.z - step >= 0))
        def _():
            self._right(step).start()

        @pl.when((self.z > 0) & (self.z + step <= self.nz - 1))
        def _():
            self._left(step).start()

    def line_wait(self, step):
        @pl.when(self.z - step >= 0)
        def _():
            self._right(step).wait_recv()

        @pl.when(self.z + step <= self.nz - 1)
        def _():
            self._left(step).wait_recv()

    def _plane(self, half, mask, bit):
        return pltpu.make_async_remote_copy(
            src_ref=self.block(half, mask),
            dst_ref=self.block(half, mask),
            send_sem=self.send_sem.at[self.slot, half, mask ^ bit],
            recv_sem=self.recv_sem.at[self.slot, half, mask ^ bit],
            device_id=(peer_flip(self.dp, bit), self.z),
            device_id_type=MESH,
        )

    def _arrival(self, half, mask, bit):
        return pltpu.make_async_remote_copy(
            src_ref=self.block(half, mask),
            dst_ref=self.block(half, mask),
            send_sem=self.send_sem.at[self.slot, half, mask],
            recv_sem=self.recv_sem.at[self.slot, half, mask],
            device_id=(peer_flip(self.dp, bit), self.z),
            device_id_type=MESH,
        )

    def plane_start(self, step):
        if step >= len(self.bits):
            return
        for half in range(2):
            order = self.order(half)
            for mask in plane_masks(order, step):
                self._plane(half, mask, order[step]).start()

    def plane_wait(self, step):
        for half in range(2):
            order = self.order(half)
            for mask in plane_masks(order, step):
                self._arrival(half, mask ^ order[step], order[step]).wait_recv()

    def _new_masks(self, half, step):
        order = self.order(half)
        return [0] if step < 0 else [m ^ order[step] for m in plane_masks(order, step)]

    def core_start(self, step):
        for half in range(2):
            for mask in self._new_masks(half, step):
                self._plane(half, mask, 1).start()

    def core_wait(self):
        for half in range(2):
            for mask in plane_masks(self.bits, len(self.bits)):
                self._arrival(half, mask ^ 1, 1).wait_recv()

    def line_sends_wait(self):
        for step in range(self.nz - 1):

            @pl.when((self.z < self.nz - 1) & (self.z - step >= 0))
            def _():
                self._right(step).wait_send()

            @pl.when((self.z > 0) & (self.z + step <= self.nz - 1))
            def _():
                self._left(step).wait_send()

    def plane_sends_wait(self):
        for half in range(2):
            order = self.order(half)
            for step in range(len(self.bits)):
                for mask in plane_masks(order, step):
                    self._plane(half, mask, order[step]).wait_send()
            for mask in plane_masks(order, len(self.bits)):
                self._plane(half, mask, 1).wait_send()


def greet(nd, nz, dp, z, everyone=False):
    barrier = pltpu.get_barrier_semaphore()
    count = 0
    for off in range(1, nz):
        pl.semaphore_signal(
            barrier, inc=1, device_id=(dp, lax.rem(z + off, nz)), device_id_type=MESH
        )
        count += 1
    bits = [1 << b for b in range(nd.bit_length() - 1)]
    peers = (
        [lax.rem(dp + off, nd) for off in range(1, nd)]
        if everyone
        else [peer_flip(dp, bit) for bit in bits]
    )
    for peer in peers:
        pl.semaphore_signal(barrier, inc=1, device_id=(peer, z), device_id_type=MESH)
        count += 1
    pl.semaphore_wait(barrier, count)


def lane_copies(seg_row):
    return jnp.broadcast_to(seg_row[...], (128, seg_row.shape[1])).T


def gelu_pair(u):
    size = jnp.abs(u)
    t = 1.0 / (1.0 + (0.3275911 * 0.7071067811865476) * size)
    poly = ((((1.061405429 * t - 1.453152027) * t + 1.421413741) * t - 0.284496736) * t + 0.254829592) * t
    bell = jnp.exp(-0.5 * u * u)
    tail = 0.5 * poly * bell
    share = jnp.where(u >= 0.0, 1.0 - tail, tail)
    return u * share, share + u * (0.3989422804014327 * bell)


def norm_parts(values):
    centre = values - jnp.mean(values, axis=-1, keepdims=True)
    inverse = lax.rsqrt(jnp.mean(centre * centre, axis=-1, keepdims=True) + EPSILON)
    return centre * inverse, inverse


def norm_back(grad, unit, inverse, gain):
    scaled = grad * gain
    back = inverse * (
        scaled
        - jnp.mean(scaled, axis=-1, keepdims=True)
        - unit * jnp.mean(scaled * unit, axis=-1, keepdims=True)
    )
    return (
        back,
        jnp.sum(grad * unit, axis=0, keepdims=True),
        jnp.sum(grad, axis=0, keepdims=True),
    )


def forward_kernel(
    nd,
    nz,
    nh,
    size_e,
    size_a,
    x_own,
    og_in,
    ag_in,
    vec_own,
    joint_own,
    wo_own,
    wa_own,
    w1_own,
    w2_own,
    seg_row,
    block_out,
    align_out,
    base_out,
    grads_out,
    part_wo,
    part_wa,
    part_w1,
    part_w2,
    sums,
    joint,
    wo_land,
    wa_land,
    normed_out,
    qkv_out,
    att_out,
    lse,
    al_land,
    x_land,
    vec,
    window,
    w1,
    w2,
    vec_cols,
    vec_rows,
    bias_rows,
    weights,
    weights_t,
    wide,
    normed,
    qkv,
    att,
    keys,
    bias,
    seg_lanes,
    tops,
    totals,
    att_send,
    og,
    ag,
    wo,
    wa,
    act,
    slope,
    block,
    align,
    base,
    grads,
    keep_sem,
    right_sem,
    left_sem,
    line_sem,
    send_sem,
    recv_sem,
    x_sem,
    x_right,
    x_left,
    x_recv,
    win_send,
    win_recv,
    att_send_sem,
    att_recv_sem,
    out_sem,
    load_sem,
    store_sem,
):
    dp, z = lax.axis_index("dp"), lax.axis_index("mp")
    rows, width = x_own.shape
    seq = rows * nz
    own = vec_own.shape[0]
    own_cols = nh * HD
    win_cols = window.shape[-1] // 3
    win = z * own_cols // 128 * 128
    shift = pl.multiple_of(z * own_cols - win, HD)
    win = pl.multiple_of(win, 128)
    hidden, aligned = size_e * nd * nz, size_a * nd * nz
    f32, b16 = jnp.float32, jnp.bfloat16
    sems = (keep_sem, right_sem, left_sem, line_sem, send_sem, recv_sem)
    specs = [
        (vec_own, vec, False),
        (joint_own, joint, False),
        (wo_own, wo_land, False),
        (w1_own, w1, True),
        (w2_own, w2, True),
        (wa_own, wa_land, False),
        (joint_own, window, False),
    ]
    spreads = [Spread(i, *spec, nd, nz, dp, z, sems) for i, spec in enumerate(specs)]
    vecs, joints, early, late, heads = (
        spreads[:1],
        spreads[1:2],
        spreads[2:5],
        spreads[5:6],
        spreads[6:],
    )
    lined = spreads[:6]
    steps = len(spreads[0].bits)

    def line_step(group, step):
        for s in group:
            s.line_wait(step)
            s.line_start(step)

    def plane_open(group):
        for s in group:
            s.keep().wait()
            s.plane_start(0)
            s.core_start(-1)

    def plane_step(group, step):
        for s in group:
            s.plane_wait(step)
            s.plane_start(step + 1)
            s.core_start(step)

    def x_to_right(step):
        j = jnp.maximum(z - step, 0)
        return pltpu.make_async_remote_copy(
            src_ref=x_land.at[j],
            dst_ref=x_land.at[j],
            send_sem=x_right.at[step],
            recv_sem=x_recv.at[j],
            device_id=(dp, jnp.minimum(z + 1, nz - 1)),
            device_id_type=MESH,
        )

    def x_to_left(step):
        j = jnp.minimum(z + step, nz - 1)
        return pltpu.make_async_remote_copy(
            src_ref=x_land.at[j],
            dst_ref=x_land.at[j],
            send_sem=x_left.at[step],
            recv_sem=x_recv.at[j],
            device_id=(dp, jnp.maximum(z - 1, 0)),
            device_id_type=MESH,
        )

    def x_start(step):
        @pl.when((z < nz - 1) & (z - step >= 0))
        def _():
            x_to_right(step).start()

        @pl.when((z > 0) & (z + step <= nz - 1))
        def _():
            x_to_left(step).start()

    def piece(to, p):
        at = to * own_cols // 128 * 128 + p * width
        return joint_own.at[:, pl.ds(pl.multiple_of(at, 128), win_cols)]

    def piece_copy(off, p):
        to = lax.rem(z + off, nz)
        return pltpu.make_async_remote_copy(
            src_ref=piece(to, p),
            dst_ref=window.at[dp, z, :, pl.ds(p * win_cols, win_cols)],
            send_sem=win_send.at[off, p],
            recv_sem=win_recv.at[off, p],
            device_id=(dp, to),
            device_id_type=MESH,
        )

    def piece_keep(p):
        return pltpu.make_async_copy(
            piece(z, p), window.at[dp, z, :, pl.ds(p * win_cols, win_cols)], win_send.at[0, p]
        )

    og_load = pltpu.make_async_copy(og_in, og, load_sem.at[0])
    ag_load = pltpu.make_async_copy(ag_in, ag, load_sem.at[1])
    x_keep = pltpu.make_async_copy(x_own, x_land.at[z], x_sem)
    x_keep.start()
    greet(nd, nz, dp, z)
    for s in lined:
        s.keep().start()
    for s in vecs:
        s.line_start(0)
    for off in range(1, nz):
        for p in range(3):
            piece_copy(off, p).start()
    for p in range(3):
        piece_keep(p).start()
    for s in early:
        s.line_start(0)
    og_load.start()
    ag_load.start()
    for step in range(1, nz - 1):
        line_step(vecs, step)
    seg_lanes[...] = lane_copies(seg_row)
    for p in range(3):
        piece_keep(p).wait()
        for off in range(1, nz):
            piece_copy(off, p).wait_recv()
    for s in heads:
        s.plane_start(0)
        s.core_start(-1)
    line_step(vecs, nz - 1)
    plane_open(vecs)
    line_step(early, 1)
    plane_step(heads + vecs, 0)
    for step in range(2, nz - 1):
        line_step(early, step)
    x_keep.wait()
    x_start(0)
    line_step(early, nz - 1)
    plane_open(early)
    for t in range(1, steps):
        plane_step(heads + vecs, t)
    for s in heads + vecs:
        s.core_wait()

    for d in range(nd):
        for j in range(nz):
            at = (d * nz + j) * own
            vec_cols[at : at + own, :] = vec[d, j].astype(f32)
            weights[at : at + own, :] = window[d, j].astype(f32)
    vec_rows[...] = vec_cols[...].T[: vec_rows.shape[0]]
    for p in range(3):
        cols = slice(p * win_cols, (p + 1) * win_cols)
        weights_t[cols, :] = weights[:, cols].T.astype(b16)

    def row(i):
        return vec_rows[i : i + 1, :]

    bias_q = vec_cols[pl.ds(win, win_cols), 2:3]
    bias_v = vec_cols[pl.ds(win, win_cols), 3:4]

    slots = 3
    part = window.shape[-1] // slots

    def flatten_load(source, k):
        return pltpu.make_async_copy(
            source.at[:, :, :, pl.ds(k * part, part)],
            window.at[:, :, :, pl.ds(k % slots * part, part)],
            load_sem.at[2 + k % slots],
        )

    def flatten_start(source, to):
        for k in range(min(slots, to.shape[1] // part)):
            flatten_load(source, k).start()

    def flatten_finish(source, to):
        count = to.shape[1] // part
        for k in range(count):
            flatten_load(source, k).wait()
            lanes = slice(k % slots * part, (k % slots + 1) * part)
            for d in range(nd):
                for j in range(nz):
                    at = (d * nz + j) * own
                    weights[at : at + own, lanes] = window[d, j, :, lanes].astype(f32)
            to[:, k * part : (k + 1) * part] = weights[:, lanes].astype(b16)
            if k + slots < count:
                flatten_load(source, k + slots).start()

    def normed_copy(j):
        at = pl.ds(pl.multiple_of(j * rows, rows), rows)
        return pltpu.make_async_copy(normed.at[at], normed_out.at[at], out_sem.at[0, j])

    def qkv_copy(j):
        at = pl.ds(pl.multiple_of(j * rows, rows), rows)
        return pltpu.make_async_copy(qkv.at[:, at], qkv_out.at[:, at], out_sem.at[1, j])

    def att_keep(j):
        at = pl.ds(pl.multiple_of(j * rows, rows), rows)
        return pltpu.make_async_copy(att.at[:, at], att_out.at[:, at], out_sem.at[2, j])

    def att_copy(to):
        return pltpu.make_async_remote_copy(
            src_ref=att_send.at[to],
            dst_ref=al_land.at[z],
            send_sem=att_send_sem.at[lax.rem(to - z + nz, nz)],
            recv_sem=att_recv_sem.at[lax.rem(to - z + nz, nz)],
            device_id=(dp, to),
            device_id_type=MESH,
        )

    def project(j):
        at = pl.ds(pl.multiple_of(j * rows, rows), rows)
        normed[at, :] = layer_norm(x_land[j].astype(f32), row(0), row(1)).astype(b16)
        for p in range(3):
            part = nt(weights_t[p * win_cols : (p + 1) * win_cols, :], normed[at, :])
            if p == 0:
                part = part + bias_q
            if p == 2:
                part = part + bias_v
            wide[p * win_cols : (p + 1) * win_cols, :] = part.astype(b16)
            qkv[p * own_cols : (p + 1) * own_cols, at] = wide[
                pl.ds(p * win_cols + shift, own_cols), :
            ]
        for h in range(nh):
            keys[h, at, :] = wide[pl.ds(win_cols + shift + h * HD, HD), :].T
        tops[:, at] = jnp.full((tops.shape[0], rows), -jnp.inf, f32)
        totals[:, at] = jnp.zeros((totals.shape[0], rows), f32)
        att[:, at] = jnp.zeros((own_cols, rows), f32)
        normed_copy(j).start()
        qkv_copy(j).start()

    def pair(i, j):
        to = pl.ds(pl.multiple_of(i * rows, rows), rows)
        of = pl.ds(pl.multiple_of(j * rows, rows), rows)
        own_seg, lanes = seg_row[0:1, to], seg_lanes[of, :]
        bias[...] = jnp.concatenate(
            [
                jnp.where(lanes == own_seg[:, k : k + 128], 0.0, NEG_FILL)
                for k in range(0, rows, 128)
            ],
            axis=1,
        )
        for h in range(nh):
            query = qkv[h * HD : (h + 1) * HD, to] * jnp.bfloat16(0.125)
            score = nn(keys[h, of, :], query) + bias[...]
            top = tops[h : h + 1, to]
            new_top = jnp.maximum(top, jnp.max(score, axis=0, keepdims=True))
            weight = jnp.exp(score - new_top)
            fade = jnp.exp(top - new_top)
            tops[h : h + 1, to] = new_top
            totals[h : h + 1, to] = totals[h : h + 1, to] * fade + jnp.sum(
                weight, axis=0, keepdims=True
            )
            value = qkv[2 * own_cols + h * HD : 2 * own_cols + (h + 1) * HD, of]
            att[h * HD : (h + 1) * HD, to] = att[h * HD : (h + 1) * HD, to] * fade + nn(
                value, weight.astype(b16)
            )

    def finish(i):
        to = pl.ds(pl.multiple_of(i * rows, rows), rows)
        for h in range(nh):
            total = totals[h : h + 1, to]
            result = att[h * HD : (h + 1) * HD, to] / total
            att[h * HD : (h + 1) * HD, to] = result
            att_send[i, h * HD : (h + 1) * HD, :] = result.astype(b16)
            lse[h : h + 1, to] = tops[h : h + 1, to] + jnp.log(total)
        att_keep(i).start()

        @pl.when(i != z)
        def _():
            att_copy(i).start()

    def take(c, low, high, last):
        project(c)

        def old_queries(f, carry):
            pair(f, c)

            @pl.when(last)
            def _():
                finish(f)

            return carry

        def new_queries(f, carry):
            pair(c, f)
            return carry

        lax.fori_loop(low, high, old_queries, 0)
        lax.fori_loop(low, high, new_queries, 0)
        pair(c, c)

        @pl.when(last)
        def _():
            finish(c)

    project(z)
    pair(z, z)
    plane_step(early, 0)
    for k in range(nd * nz):
        bias_rows[0:1, k * size_e : (k + 1) * size_e] = vec_cols[
            k * own : k * own + 1, 16 : 16 + size_e
        ]
        bias_rows[1:2, k * size_a : (k + 1) * size_a] = vec_cols[
            k * own + 1 : k * own + 2, 16 : 16 + size_a
        ]
    for s in heads:
        s.plane_sends_wait()
    final = jnp.maximum(z, nz - 1 - z)

    def arrivals(step, carry):
        @pl.when(z - step >= 0)
        def _():
            x_to_right(step).wait_recv()

        @pl.when(z + step <= nz - 1)
        def _():
            x_to_left(step).wait_recv()

        @pl.when(step < nz - 1)
        def _():
            x_start(step)

        @pl.when(step == nz - 2)
        def _():
            for s in late:
                s.line_start(0)

        @pl.when(step == nz - 1)
        def _():
            for t in range(1, steps):
                plane_step(early[:2], t)

        high = jnp.minimum(z + step, nz)

        @pl.when(z - step >= 0)
        def _():
            take(z - step, z - step + 1, high, (step == final) & (z + step > nz - 1))

        @pl.when(z + step <= nz - 1)
        def _():
            take(z + step, jnp.maximum(z - step, 0), high, step == final)

        return carry

    lax.fori_loop(1, nz, arrivals, 0)
    for step in range(1, nz):
        line_step(late, step)
    plane_open(late)
    for s in joints:
        s.line_start(0)
    early[0].core_wait()
    flatten_start(wo_land, wo)
    for t in range(1, steps):
        plane_step(early[2:], t)
    flatten_finish(wo_land, wo)
    al_land[z] = att_send[z]
    for off in range(1, nz):
        att_copy(lax.rem(z + off, nz)).wait()

    stores = []

    def store(source, to):
        stores.append(pltpu.make_async_copy(source, to, store_sem.at[len(stores)]))
        stores[-1].start()

    step = hidden // nz
    cols = [slice(j * step, (j + 1) * step) for j in range(nz)]

    def weight(full, j):
        return full[:, :, cols[j]].reshape(width, step)

    sums[...] = jnp.zeros_like(sums)
    sums[0:1, :] = row(0)
    al = al_land[...].reshape(width, rows)
    x1 = x_land[z].astype(f32) + nn(al.T, wo[...]) + row(4)
    unit_two, inverse_two = norm_parts(x1)
    n2 = (unit_two * row(5) + row(6)).astype(b16)
    y = x1 + row(7)
    plane_step(late, 0)
    line_step(joints, 1)
    for t in range(1, steps):
        plane_step(late, t)
    early[1].core_wait()
    for j in range(nz):
        u = nn(n2, weight(w1, j)) + bias_rows[0:1, cols[j]]
        value, derivative = gelu_pair(u)
        act[:, cols[j]] = value.astype(b16)
        slope[:, cols[j]] = derivative.astype(b16)
        if j == 1:
            for t in range(2, nz):
                line_step(joints, t)
            plane_open(joints)
    for s in late:
        s.core_wait()
    flatten_start(wa_land, wa)
    early[2].core_wait()
    for j in range(nz):
        y = y + nt(act[:, cols[j]], weight(w2, j))
    block[...] = y.astype(b16)
    store(block, block_out)
    unit_three, inverse_three = norm_parts(y)
    n3 = (unit_three * row(8) + row(9)).astype(b16)
    flatten_finish(wa_land, wa)
    plane_step(joints, 0)
    align[...] = (nn(n3, wa[...]) + bias_rows[1:2, :aligned]).astype(b16)
    store(align, align_out)
    ag_load.wait()
    back = nt(ag[...], wa[...])
    total = jnp.sum(ag[...].astype(f32), axis=0, keepdims=True)
    at = 10 + hidden // width
    for k in range(0, aligned, width):
        size = min(width, aligned - k)
        sums[at : at + 1, 0:size] = total[:, k : k + size]
        at += 1
    wa[...] = nn(n3.T, ag[...]).astype(b16)
    store(wa, part_wa)
    back, sums[8:9, :], sums[9:10, :] = norm_back(back, unit_three, inverse_three, row(8))
    og_load.wait()
    gy = og[...].astype(f32) + back
    gm = gy.astype(b16)
    sums[7:8, :] = jnp.sum(gm.astype(f32), axis=0, keepdims=True)
    gm_t, n2_t = gm.T, n2.T
    for s in spreads[3:5]:
        s.line_sends_wait()
        s.plane_sends_wait()
    gn2 = jnp.zeros(gy.shape, f32)
    for j in range(nz):
        back = nn(gm, weight(w2, j))
        w2[:, :, cols[j]] = nn(gm_t, act[:, cols[j]]).astype(b16).reshape(nd, width // nd, step)
        store(w2.at[:, :, cols[j]], part_w2.at[:, :, cols[j]])
        gu = (back * slope[:, cols[j]].astype(f32)).astype(b16)
        slope[:, cols[j]] = gu
        total = jnp.sum(gu.astype(f32), axis=0, keepdims=True)
        for k in range(0, step, width):
            at = (j * step + k) // width
            sums[10 + at : 11 + at, 0:width] = total[:, k : k + width]
        gn2 = gn2 + nt(gu, weight(w1, j))
        if j == 1:
            for t in range(1, steps):
                plane_step(joints, t)
    back, sums[5:6, :], sums[6:7, :] = norm_back(gn2, unit_two, inverse_two, row(5))
    gx1 = gy + back
    base[...] = gx1
    store(base, base_out)
    go = gx1.astype(b16)
    sums[4:5, :] = jnp.sum(go.astype(f32), axis=0, keepdims=True)
    grads[...] = nt(wo[...], go).astype(b16)
    store(grads, grads_out)
    for j in range(nz):
        w1[:, :, cols[j]] = (
            nn(n2_t, slope[:, cols[j]]).astype(b16).reshape(nd, width // nd, step)
        )
        store(w1.at[:, :, cols[j]], part_w1.at[:, :, cols[j]])
    wo[...] = nn(al, go).astype(b16)
    store(wo, part_wo)
    for s in joints:
        s.core_wait()
    for j in range(nz):
        normed_copy(j).wait()
        qkv_copy(j).wait()
        att_keep(j).wait()
    for t in range(nz - 1):

        @pl.when((z < nz - 1) & (z - t >= 0))
        def _():
            x_to_right(t).wait_send()

        @pl.when((z > 0) & (z + t <= nz - 1))
        def _():
            x_to_left(t).wait_send()

    for off in range(1, nz):
        for p in range(3):
            piece_copy(off, p).wait_send()
    for s in spreads[:3] + spreads[5:6]:
        s.line_sends_wait()
    for s in spreads[:3] + spreads[5:6]:
        s.plane_sends_wait()
    for copy in stores:
        copy.wait()


def forward_call(
    x, og, ag, vec, joint, wo, wa, w1, w2, seg_row, nd, nz, nh, size_e, size_a, cid
):
    rows, width = x.shape
    seq, own_cols = rows * nz, nh * HD
    win_cols = -(-(own_cols + HD) // 128) * 128
    own = joint.shape[0]
    hidden, aligned = size_e * nd * nz, ag.shape[1]
    lines = 10 + hidden // width + -(-aligned // width)
    f32, b16 = jnp.float32, jnp.bfloat16
    S, D = jax.ShapeDtypeStruct, pltpu.SemaphoreType.DMA
    na = 7
    wide_shape = (nd, w1.shape[0], nz * w1.shape[1])
    return pl.pallas_call(
        functools.partial(forward_kernel, nd, nz, nh, size_e, size_a),
        out_shape=(
            S((rows, width), b16),
            S((rows, aligned), b16),
            S((rows, width), f32),
            S((width, rows), b16),
            S((width, width), b16),
            S((width, aligned), b16),
            S(wide_shape, b16),
            S(wide_shape, b16),
            S((lines, width), f32),
            S((nd, nz) + joint.shape, b16),
            S((nd, nz) + wo.shape, b16),
            S((nd, nz) + wa.shape, b16),
            S((seq, width), b16),
            S((3 * own_cols, seq), b16),
            S((own_cols, seq), f32),
            S((8, seq), f32),
        ),
        in_specs=[ANY] * 3 + [VM] * 7,
        out_specs=(ANY,) * 8 + (VM,) + (ANY,) * 6 + (VM,),
        scratch_shapes=[
            pltpu.VMEM((nz, own_cols, rows), b16),
            pltpu.VMEM((nz, rows, width), b16),
            pltpu.VMEM((nd, nz) + vec.shape, b16),
            pltpu.VMEM((nd, nz, own, 3 * win_cols), b16),
            pltpu.VMEM(wide_shape, b16),
            pltpu.VMEM(wide_shape, b16),
            pltpu.VMEM((width, vec.shape[1]), f32),
            pltpu.VMEM((16, width), f32),
            pltpu.VMEM((8, max(hidden, aligned)), f32),
            pltpu.VMEM((width, max(width, 3 * win_cols)), f32),
            pltpu.VMEM((3 * win_cols, width), b16),
            pltpu.VMEM((3 * win_cols, rows), b16),
            pltpu.VMEM((seq, width), b16),
            pltpu.VMEM((3 * own_cols, seq), b16),
            pltpu.VMEM((own_cols, seq), f32),
            pltpu.VMEM((nh, seq, HD), b16),
            pltpu.VMEM((rows, rows), f32),
            pltpu.VMEM((seq, 128), jnp.int32),
            pltpu.VMEM((8, seq), f32),
            pltpu.VMEM((8, seq), f32),
            pltpu.VMEM((nz, own_cols, rows), b16),
            pltpu.VMEM((rows, width), b16),
            pltpu.VMEM((rows, aligned), b16),
            pltpu.VMEM((width, width), b16),
            pltpu.VMEM((width, aligned), b16),
            pltpu.VMEM((rows, hidden), b16),
            pltpu.VMEM((rows, hidden), b16),
            pltpu.VMEM((rows, width), b16),
            pltpu.VMEM((rows, aligned), b16),
            pltpu.VMEM((rows, width), f32),
            pltpu.VMEM((width, rows), b16),
            D((na,)),
            D((na, nz)),
            D((na, nz)),
            D((na, nz)),
            D((na, 2, nd)),
            D((na, 2, nd)),
            D,
            D((nz,)),
            D((nz,)),
            D((nz,)),
            D((nz, 3)),
            D((nz, 3)),
            D((nz,)),
            D((nz,)),
            D((3, nz)),
            D((5,)),
            D((6 + 2 * nz,)),
        ],
        compiler_params=pltpu.CompilerParams(
            collective_id=cid, has_side_effects=True, vmem_limit_bytes=62 << 20
        ),
    )(x, og, ag, vec, joint, wo, wa, w1, w2, seg_row)


class Reduce:
    def __init__(self, slot, part, acc, land, plane, line, wide, nd, nz, dp, z, sems):
        self.slot, self.part, self.acc, self.land, self.plane, self.line = slot, part, acc, land, plane, line
        self.wide, self.nd, self.nz, self.dp, self.z = wide, nd, nz, dp, z
        self.load_sem, self.core_out, self.core_in, self.plane_out, self.plane_in, self.line_out, self.line_in = sems
        self.bits = [1 << b for b in range(1, nd.bit_length() - 1)]
        self.masks = plane_masks(self.bits, len(self.bits))
        self.cut = nz // 2
        self.cols = acc.shape[-1] // nz if wide else acc.shape[-1]

    def order(self, half):
        return self.bits if half == 0 else self.bits[::-1]

    def span(self, half):
        return (0, self.cut) if half == 0 else (self.cut, self.nz)

    def region(self, ref, i, half):
        lo, hi = self.span(half)
        if self.wide:
            return ref.at[i, :, pl.ds(lo * self.cols, (hi - lo) * self.cols)]
        return ref.at[i, pl.ds(lo, hi - lo)]

    def chunk(self, ref, i, j):
        if self.wide:
            at = j * self.cols
            at = at if isinstance(at, int) else pl.multiple_of(at, 128)
            return ref.at[i, :, pl.ds(at, self.cols)]
        return ref.at[i, j]

    def slots(self, half, step):
        order, base = self.order(half), 0
        for t in range(step):
            base += 1 << (len(order) - 1 - t)
        rest = plane_masks(order[step + 1 :], len(order) - step - 1)
        return [(m, base + k) for k, m in enumerate(rest)]

    def _load(self, m):
        return pltpu.make_async_copy(
            self.part.at[mask_flip(self.dp, m)], self.acc.at[m >> 1], self.load_sem.at[self.slot, m >> 1]
        )

    def _core(self, m):
        return pltpu.make_async_remote_copy(
            src_ref=self.part.at[mask_flip(self.dp, m ^ 1)],
            dst_ref=self.land.at[m >> 1],
            send_sem=self.core_out.at[self.slot, m >> 1],
            recv_sem=self.core_in.at[self.slot, m >> 1],
            device_id=(peer_flip(self.dp, 1), self.z),
            device_id_type=MESH,
        )

    def core_start(self):
        for m in self.masks:
            self._core(m).start()
        for m in self.masks:
            self._load(m).start()

    def _add(self, i, source, k, half):
        lo, hi = self.span(half)

        def step(j, carry):
            to, more = self.chunk(self.acc, i, j), self.chunk(source, k, j)
            to[...] = (to[...].astype(jnp.float32) + more[...].astype(jnp.float32)).astype(to.dtype)
            return carry

        lax.fori_loop(lo, hi, step, 0)

    def core_add(self):
        for m in self.masks:
            self._load(m).wait()
            self._core(m).wait_recv()
            for half in range(2):
                self._add(m >> 1, self.land, m >> 1, half)

    def _plane(self, half, step, m, place):
        bit = self.order(half)[step]
        return pltpu.make_async_remote_copy(
            src_ref=self.region(self.acc, (m ^ bit) >> 1, half),
            dst_ref=self.region(self.plane, place, half),
            send_sem=self.plane_out.at[self.slot, half, place],
            recv_sem=self.plane_in.at[self.slot, half, place],
            device_id=(peer_flip(self.dp, bit), self.z),
            device_id_type=MESH,
        )

    def plane_start(self, step):
        if step < len(self.bits):
            for half in range(2):
                for m, place in self.slots(half, step):
                    self._plane(half, step, m, place).start()

    def plane_add(self, step):
        for half in range(2):
            for m, place in self.slots(half, step):
                self._plane(half, step, m, place).wait_recv()
                self._add(m >> 1, self.plane, place, half)

    def _line(self, off):
        to = lax.rem(self.z + off, self.nz)
        return pltpu.make_async_remote_copy(
            src_ref=self.chunk(self.acc, 0, to),
            dst_ref=self.line.at[off],
            send_sem=self.line_out.at[self.slot, off],
            recv_sem=self.line_in.at[self.slot, off],
            device_id=(self.dp, to),
            device_id_type=MESH,
        )

    def line_start(self):
        for off in range(1, self.nz):
            self._line(off).start()

    def line_wait(self):
        for off in range(1, self.nz):
            self._line(off).wait_recv()

    def _hop(self, j, way):
        to = jnp.clip(self.z + way, 0, self.nz - 1)
        place = j if way < 0 else jnp.where(j == to, self.nz, j)
        return pltpu.make_async_remote_copy(
            src_ref=self.chunk(self.acc, 0, j),
            dst_ref=self.line.at[place],
            send_sem=self.line_out.at[self.slot, j],
            recv_sem=self.line_in.at[self.slot, place],
            device_id=(self.dp, to),
            device_id_type=MESH,
        )

    def _landed(self, place):
        return pltpu.make_async_remote_copy(
            src_ref=self.line.at[place],
            dst_ref=self.line.at[place],
            send_sem=self.line_out.at[self.slot, 0],
            recv_sem=self.line_in.at[self.slot, place],
            device_id=(self.dp, self.z),
            device_id_type=MESH,
        )

    def hop(self, j, way, first):
        @pl.when(jnp.logical_not(first))
        def _():
            self._landed(j).wait_recv()
            to = self.chunk(self.acc, 0, j)
            to[...] = (to[...].astype(jnp.float32) + self.line[j].astype(jnp.float32)).astype(to.dtype)

        self._hop(j, way).start()

    def home(self):
        total = self.chunk(self.acc, 0, self.z)
        self.total[...] = total[...].astype(jnp.float32)

        @pl.when(self.z < self.nz - 1)
        def _():
            self._landed(self.z).wait_recv()
            self.total[...] += self.line[self.z].astype(jnp.float32)

        @pl.when(self.z > 0)
        def _():
            self._landed(self.nz).wait_recv()
            self.total[...] += self.line[self.nz].astype(jnp.float32)

    def hops_wait(self):
        def step(j, carry):
            @pl.when(j != self.z)
            def _():
                self._hop(j, -1).wait_send()

            return carry

        lax.fori_loop(0, self.nz, step, 0)

    def sends_wait(self):
        for m in self.masks:
            self._core(m).wait_send()
        for half in range(2):
            for step in range(len(self.bits)):
                for m, place in self.slots(half, step):
                    self._plane(half, step, m, place).wait_send()


def backward_kernel(
    nd,
    nz,
    nh,
    grad_parts,
    part_wo,
    part_wa,
    part_w1,
    part_w2,
    qkv_in,
    att_in,
    normed_in,
    joint_in,
    x_in,
    base_in,
    lse,
    seg_row,
    vec_in,
    tokens_grad,
    out_joint,
    out_wo,
    out_wa,
    out_w1,
    out_w2,
    out_vec,
    grad_land,
    keys,
    values,
    key_grad,
    value_grad,
    turned,
    staged,
    rows_land,
    part_joint,
    bias_cols,
    seg_lanes,
    vec_stage,
    vec_land,
    vec_line,
    qkv,
    att,
    normed,
    joint_full,
    x_own,
    base,
    in_sem,
    *rest,
):
    na = 5
    buffers = [rest[4 * a : 4 * a + 4] for a in range(na)]
    (
        load_sem,
        core_out,
        core_in,
        plane_out,
        plane_in,
        line_out,
        line_in,
        grad_out,
        grad_in,
        row_out,
        row_in,
        vec_out,
        vec_in_sem,
        vec_line_out,
        vec_line_in,
        own_sem,
    ) = rest[4 * na :]
    dp, z = lax.axis_index("dp"), lax.axis_index("mp")
    rows, width = x_own.shape
    seq = rows * nz
    own_cols = nh * HD
    f32, b16 = jnp.float32, jnp.bfloat16
    sems = (load_sem, core_out, core_in, plane_out, plane_in, line_out, line_in)
    parts = [(part_w2, True), (part_w1, True), (part_wa, False), (part_wo, False), (part_joint, False)]
    reduces = [
        Reduce(a, part, *buffers[a], wide, nd, nz, dp, z, sems) for a, (part, wide) in enumerate(parts)
    ]
    big, joint = reduces[:4], reduces[4]
    for r, out in zip(big, (out_w2, out_w1, out_wa, out_wo)):
        r.total = out
    steps = len(joint.bits)

    loads = [
        pltpu.make_async_copy(source, to, in_sem.at[i])
        for i, (source, to) in enumerate(
            zip(
                (qkv_in, att_in, normed_in, joint_in, x_in, base_in),
                (qkv, att, normed, joint_full, x_own, base),
            )
        )
    ]
    for copy in loads:
        copy.start()
    greet(nd, nz, dp, z, everyone=True)

    def grad_copy(h, off):
        to = lax.rem(z + off, nz)
        return pltpu.make_async_remote_copy(
            src_ref=grad_parts.at[to, pl.ds(h * HD, HD)],
            dst_ref=grad_land.at[z, pl.ds(h * HD, HD)],
            send_sem=grad_out.at[h, off],
            recv_sem=grad_in.at[h, off],
            device_id=(dp, to),
            device_id_type=MESH,
        )

    grad_own = pltpu.make_async_copy(grad_parts.at[z], grad_land.at[z], own_sem)
    grad_own.start()
    for off in range(1, nz):
        grad_copy(0, off).start()
    for r in big:
        r.core_start()
    loads[0].wait()
    for h in range(nh):
        keys[h] = qkv[own_cols + h * HD : own_cols + (h + 1) * HD, :].T
        values[h] = qkv[2 * own_cols + h * HD : 2 * own_cols + (h + 1) * HD, :].T
    bias_cols[...] = jnp.zeros_like(bias_cols)
    seg_lanes[...] = lane_copies(seg_row)
    kc = min(512, seq)

    def row_copy(h, off):
        to = lax.rem(z + off, nz)
        return pltpu.make_async_remote_copy(
            src_ref=staged.at[to, :, pl.ds(h * HD, HD)],
            dst_ref=rows_land.at[:, z, pl.ds(h * HD, HD)],
            send_sem=row_out.at[h, off],
            recv_sem=row_in.at[h, off],
            device_id=(dp, to),
            device_id_type=MESH,
        )

    def chores(u):
        if u == 0:
            big[1].core_add()
            big[1].plane_start(0)
        if u == 1:
            for r in big[2:]:
                r.core_add()
                r.plane_start(0)
        if u == 4:
            big[0].plane_add(0)
            big[0].plane_start(1)
        if u == 6:
            vec_sum(1)
        if u == 7:
            big[1].plane_add(0)
            big[1].plane_start(1)
        if u == 9:
            for r in big[2:]:
                r.plane_add(0)
                r.plane_start(1)

    def vec_copy(part, off):
        span = pl.ds(8 * part, 8)
        return pltpu.make_async_remote_copy(
            src_ref=vec_stage.at[0, span],
            dst_ref=vec_land.at[off, span],
            send_sem=vec_out.at[part, off],
            recv_sem=vec_in_sem.at[part, off],
            device_id=(lax.rem(dp + off, nd), z),
            device_id_type=MESH,
        )

    def vec_line_copy(part, off):
        span = pl.ds(8 * part, 8)
        return pltpu.make_async_remote_copy(
            src_ref=vec_stage.at[1, span],
            dst_ref=vec_line.at[off, span],
            send_sem=vec_line_out.at[part, off],
            recv_sem=vec_line_in.at[part, off],
            device_id=(dp, lax.rem(z + off, nz)),
            device_id_type=MESH,
        )

    def vec_sum(part):
        span = slice(8 * part, 8 * part + 8)
        total = vec_stage[0, span, :]
        for off in range(1, nd):
            vec_copy(part, off).wait_recv()
            total = total + vec_land[off, span, :]
        vec_stage[1, span, :] = total
        for off in range(1, nz):
            vec_line_copy(part, off).start()

    vec_stage[0] = vec_in[...]
    for off in range(1, nd):
        vec_copy(1, off).start()
    big[0].core_add()
    big[0].plane_start(0)
    grad_own.wait()
    loads[1].wait()
    for h in range(nh):
        for off in range(1, nz):
            grad_copy(h, off).wait_recv()
        if h == 0:
            for later in range(1, nh):
                for off in range(1, nz):
                    grad_copy(later, off).start()
        key_grad[...] = jnp.zeros_like(key_grad)
        value_grad[...] = jnp.zeros_like(value_grad)

        def block(i, carry):
            start = pl.multiple_of(i * rows, rows)
            own_seg = seg_row[0:1, pl.ds(start, rows)]
            query = qkv[h * HD : (h + 1) * HD, pl.ds(start, rows)] * jnp.bfloat16(0.125)
            back = grad_land[i, h * HD : (h + 1) * HD, :]
            row_term = jnp.sum(
                back.astype(f32) * att[h * HD : (h + 1) * HD, pl.ds(start, rows)],
                axis=0,
                keepdims=True,
            )
            log_total = lse[h : h + 1, pl.ds(start, rows)]
            query_grad = jnp.zeros((HD, rows), f32)
            for c in range(0, seq, kc):
                chunk = slice(c, c + kc)
                lanes = seg_lanes[chunk, :]
                allowed = jnp.concatenate(
                    [lanes == own_seg[:, k : k + 128] for k in range(0, rows, 128)], axis=1
                )
                score = nn(keys[h, chunk, :], query)
                weight = jnp.where(allowed, jnp.exp(score - log_total), 0.0)
                value_grad[chunk, :] += nt(weight.astype(b16), back)
                weight_grad = nn(values[h, chunk, :], back)
                score_grad = (weight * (weight_grad - row_term)).astype(b16)
                key_grad[chunk, :] += nt(score_grad, query)
                query_grad = query_grad + nn(
                    qkv[own_cols + h * HD : own_cols + (h + 1) * HD, chunk], score_grad
                )
            staged[i, 0, h * HD : (h + 1) * HD, :] = (query_grad * 0.125).astype(b16)
            for b in range(nz):
                u = h * nz + b

                @pl.when(i == b)
                def _():
                    chores(u)

            return carry

        lax.fori_loop(0, nz, block, 0)
        for p, source in ((1, key_grad), (2, value_grad)):
            turned[...] = source[...].T
            for j in range(nz):
                staged[j, p, h * HD : (h + 1) * HD, :] = turned[:, j * rows : (j + 1) * rows].astype(b16)
        for off in range(1, nz):
            row_copy(h, off).start()
        rows_land[:, z, h * HD : (h + 1) * HD, :] = staged[z, :, h * HD : (h + 1) * HD, :]
        at = pl.ds(pl.multiple_of(z * own_cols + h * HD, HD), HD)
        for col, p in ((0, 0), (1, 2)):
            total = jnp.zeros((HD, 1), f32)
            for j in range(nz):
                total = total + jnp.sum(
                    staged[j, p, h * HD : (h + 1) * HD, :].astype(f32), axis=1, keepdims=True
                )
            bias_cols[at, col : col + 1] = total

    def stream(r, way):
        def left(j, carry):
            r.hop(j, -1, z == nz - 1)
            return carry

        def right(k, carry):
            r.hop(nz - 1 - k, 1, z == 0)
            return carry

        if way < 0:
            lax.fori_loop(0, z, left, 0)
        else:
            lax.fori_loop(0, nz - 1 - z, right, 0)

    for r in big:
        for t in range(1, steps):
            r.plane_add(t)
            r.plane_start(t + 1)

        @pl.when(z == nz - 1)
        def _():
            stream(r, -1)

        @pl.when(z == 0)
        def _():
            stream(r, 1)

    for copy in loads[2:]:
        copy.wait()
    grad_t = jnp.zeros((3 * own_cols, width), f32)
    for j in range(nz):
        grad_t = grad_t + nn(
            staged[j].reshape(3 * own_cols, rows), normed[j * rows : (j + 1) * rows, :]
        )
    grad_joint = grad_t.T
    own = part_joint.shape[2]
    for d in range(nd):
        for j in range(nz):
            at = (d * nz + j) * own
            part_joint[d, j] = grad_joint[at : at + own, :].astype(b16)
    joint.core_start()
    joint.core_add()
    joint.plane_start(0)
    for t in range(steps):
        joint.plane_add(t)
        joint.plane_start(t + 1)
    joint.line_start()

    @pl.when((z > 0) & (z < nz // 2))
    def _():
        for r in big:
            stream(r, 1)

    @pl.when((z >= nz // 2) & (z < nz - 1))
    def _():
        for r in big:
            stream(r, -1)

    for h in range(nh):
        for off in range(1, nz):
            row_copy(h, off).wait_recv()
    back_t = nn(joint_full[...], rows_land[...].reshape(3 * width, rows))
    back = back_t.T
    gain = vec_in[0:1, :]
    x = x_own[...].astype(f32)
    centre = x - jnp.mean(x, axis=-1, keepdims=True)
    inverse = lax.rsqrt(jnp.mean(centre * centre, axis=-1, keepdims=True) + EPSILON)
    unit = centre * inverse
    scaled = back * gain
    tokens_grad[...] = base[...] + inverse * (
        scaled
        - jnp.mean(scaled, axis=-1, keepdims=True)
        - unit * jnp.mean(scaled * unit, axis=-1, keepdims=True)
    )
    bias_rows = bias_cols[...].T
    vec_stage[0, 0:1, :] = jnp.sum(back * unit, axis=0, keepdims=True)
    vec_stage[0, 1:2, :] = jnp.sum(back, axis=0, keepdims=True)
    vec_stage[0, 2:4, :] = bias_rows[0:2, :]
    for off in range(1, nd):
        vec_copy(0, off).start()

    @pl.when((z > 0) & (z < nz // 2))
    def _():
        for r in big:
            stream(r, -1)

    @pl.when((z >= nz // 2) & (z < nz - 1))
    def _():
        for r in big:
            stream(r, 1)

    vec_sum(0)

    for r in big:
        r.home()
    joint.line_wait()
    joint.line[0] = joint.acc[0, z]
    for j in range(nz):
        piece = joint.line[lax.rem(z - j + nz, nz)].astype(f32)
        for p in range(3):
            out_joint[:, p * width + j * own_cols : p * width + (j + 1) * own_cols] = piece[
                :, p * own_cols : (p + 1) * own_cols
            ]
    total = vec_stage[1]
    for off in range(1, nz):
        for part in range(2):
            vec_line_copy(part, off).wait_recv()
        total = total + vec_line[off]
    out_vec[...] = total
    for part in range(2):
        for off in range(1, nd):
            vec_copy(part, off).wait_send()
        for off in range(1, nz):
            vec_line_copy(part, off).wait_send()
    for off in range(1, nz):
        for h in range(nh):
            grad_copy(h, off).wait_send()
            row_copy(h, off).wait_send()
        joint._line(off).wait_send()
    for r in reduces:
        r.sends_wait()
    for r in big:
        r.hops_wait()


def backward_call(
    grad_parts, wo, wa, w1, w2, qkv, att, normed, joint_full, x_own, base, lse, seg_row, vec_in, nd, nz, nh, cid
):
    rows, width = x_own.shape
    seq, own_cols = rows * nz, nh * HD
    own = width // (nd * nz)
    f32, b16 = jnp.float32, jnp.bfloat16
    S, D = jax.ShapeDtypeStruct, pltpu.SemaphoreType.DMA
    joint_shape = (nd, nz, own, 3 * own_cols)
    held = []
    for shape, wide in ((w2.shape, True), (w1.shape, True), (wa.shape, False), (wo.shape, False), (joint_shape, False)):
        piece = shape[1:]
        line = (nz + 1, piece[0], piece[1] // nz) if wide else (nz + 1,) + piece[1:]
        held += [
            pltpu.VMEM((nd // 2,) + piece, b16),
            pltpu.VMEM((nd // 2,) + piece, b16),
            pltpu.VMEM((max(nd // 2 - 1, 1),) + piece, b16),
            pltpu.VMEM(line, b16),
        ]
    na = 5
    return pl.pallas_call(
        functools.partial(backward_kernel, nd, nz, nh),
        out_shape=(
            S((rows, width), f32),
            S((own, 3 * width), f32),
            S(wo.shape[2:], f32),
            S(wa.shape[2:], f32),
            S((w1.shape[1], w1.shape[2] // nz), f32),
            S((w2.shape[1], w2.shape[2] // nz), f32),
            S(vec_in.shape, f32),
        ),
        in_specs=[ANY] * 11 + [VM] * 3,
        out_specs=(VM,) * 7,
        scratch_shapes=[
            pltpu.VMEM((nz, own_cols, rows), b16),
            pltpu.VMEM((nh, seq, HD), b16),
            pltpu.VMEM((nh, seq, HD), b16),
            pltpu.VMEM((seq, HD), f32),
            pltpu.VMEM((seq, HD), f32),
            pltpu.VMEM((HD, seq), f32),
            pltpu.VMEM((nz, 3, own_cols, rows), b16),
            pltpu.VMEM((3, nz, own_cols, rows), b16),
            pltpu.VMEM(joint_shape, b16),
            pltpu.VMEM((width, 128), f32),
            pltpu.VMEM((seq, 128), jnp.int32),
            pltpu.VMEM((2,) + vec_in.shape, f32),
            pltpu.VMEM((nd,) + vec_in.shape, f32),
            pltpu.VMEM((nz,) + vec_in.shape, f32),
            pltpu.VMEM(qkv.shape, b16),
            pltpu.VMEM(att.shape, f32),
            pltpu.VMEM(normed.shape, b16),
            pltpu.VMEM(joint_full.shape, b16),
            pltpu.VMEM(x_own.shape, b16),
            pltpu.VMEM(base.shape, f32),
            D((6,)),
        ]
        + held
        + [
            D((na, nd // 2)),
            D((na, nd // 2)),
            D((na, nd // 2)),
            D((na, 2, nd // 2)),
            D((na, 2, nd // 2)),
            D((na, nz + 1)),
            D((na, nz + 1)),
            D((nh, nz)),
            D((nh, nz)),
            D((nh, nz)),
            D((nh, nz)),
            D((2, nd)),
            D((2, nd)),
            D((2, nz)),
            D((2, nz)),
            D,
        ],
        compiler_params=pltpu.CompilerParams(
            collective_id=cid, has_side_effects=True, vmem_limit_bytes=63 << 20
        ),
    )(grad_parts, wo, wa, w1, w2, qkv, att, normed, joint_full, x_own, base, lse, seg_row, vec_in)


def finish_kernel(n, own, size_e, size_a, sums, *refs):
    count = (len(refs) - 12) // 2
    for source, to in zip(refs[:count], refs[count : 2 * count]):
        to[...] = source[...]
    mine = refs[-12:]
    me = lax.axis_index("dp") * lax.axis_size("mp") + lax.axis_index("mp")
    width = sums.shape[1]
    hidden = size_e * n
    for k in range(n):

        @pl.when(me == k)
        def _():
            for i in range(10):
                mine[i][...] = sums[i : i + 1, k * own : (k + 1) * own]
            at = k * size_e
            line = 10 + at // width
            mine[10][...] = sums[line : line + 1, at % width : at % width + size_e]
            at = k * size_a
            line = 10 + hidden // width + at // width
            mine[11][...] = sums[line : line + 1, at % width : at % width + size_a]


def finish_call(sums, results, n, own, size_e, size_a):
    S = jax.ShapeDtypeStruct
    return pl.pallas_call(
        functools.partial(finish_kernel, n, own, size_e, size_a),
        out_shape=tuple(S(r.shape, r.dtype) for r in results)
        + tuple(S((1, size), jnp.float32) for size in (own,) * 10 + (size_e, size_a)),
        in_specs=[VM] * (1 + len(results)),
        out_specs=(VM,) * (len(results) + 12),
        compiler_params=pltpu.CompilerParams(vmem_limit_bytes=VMEM_LIMIT),
    )(sums, *results)


def local(
    tokens,
    segments,
    out_grad,
    align_grad,
    first_gain,
    first_shift,
    joint_weight,
    query_bias,
    value_bias,
    output_weight,
    output_bias,
    second_gain,
    second_shift,
    expand_bias,
    reduce_bias,
    head_gain,
    head_shift,
    align_weight,
    align_bias,
    expand_weight,
    reduce_weight,
):
    nd, nz = lax.axis_size("dp"), lax.axis_size("mp")
    n = nd * nz
    z = lax.axis_index("mp")
    rows, width = tokens.shape
    seq = rows * nz
    nh = H // nz
    own_cols = nh * HD
    f32, b16 = jnp.float32, jnp.bfloat16

    own = first_gain.shape[0]

    small = (
        first_gain,
        first_shift,
        query_bias,
        value_bias,
        output_bias,
        second_gain,
        second_shift,
        reduce_bias,
        head_gain,
        head_shift,
    )
    flat = 0.0
    for i, v in enumerate(small):
        flat = flat + jnp.pad(v, (i * own, (15 - i) * own))
    size_e, size_a = expand_bias.shape[0], align_bias.shape[0]
    vec = (
        jnp.pad(flat.reshape(16, own).T, ((0, 0), (0, 112)))
        + jnp.pad(expand_bias[None], ((0, own - 1), (16, 112 - size_e)))
        + jnp.pad(align_bias[None], ((1, own - 2), (16, 112 - size_a)))
    )
    seg_row = segments.reshape(1, seq)
    (
        block_out,
        align_out,
        base,
        grad_parts,
        p_wo,
        p_wa,
        p_w1,
        p_w2,
        vec_in,
        joint_full,
        _,
        _,
        normed_all,
        qkv,
        att,
        lse,
    ) = forward_call(
        tokens,
        out_grad,
        align_grad,
        vec,
        joint_weight,
        output_weight,
        align_weight,
        expand_weight,
        reduce_weight.T,
        seg_row,
        nd,
        nz,
        nh,
        size_e,
        size_a,
        1,
    )
    joint_full = joint_full.reshape(width, 3 * width)
    hidden = size_e * n
    tokens_grad, g_joint, g_wo, g_wa, g_w1, g_w2, sums = backward_call(
        grad_parts.reshape(nz, own_cols, rows),
        p_wo.reshape(nd, nz, own, width),
        p_wa.reshape(nd, nz, own, -1),
        p_w1,
        p_w2,
        qkv,
        att,
        normed_all,
        joint_full,
        tokens,
        base,
        lse,
        seg_row,
        vec_in,
        nd,
        nz,
        nh,
        2,
    )
    block_out, align_out, tokens_grad, g_joint, g_wo, g_wa, g_w1, g_w2, *mine = finish_call(
        sums,
        (block_out, align_out, tokens_grad, g_joint, g_wo, g_wa, g_w1, g_w2),
        n,
        own,
        size_e,
        size_a,
    )
    mine = [v.reshape(-1) for v in mine]
    return (
        block_out,
        align_out,
        tokens_grad,
        mine[0],
        mine[1],
        g_joint,
        mine[2],
        mine[3],
        g_wo,
        mine[4],
        mine[5],
        mine[6],
        mine[10],
        mine[7],
        mine[8],
        mine[9],
        g_wa,
        mine[11],
        g_w1,
        g_w2.T,
    )


def solution(mesh):
    both = P(("dp", "mp"))
    rows = P(("dp", "mp"), None)
    in_specs = (
        (rows, P("dp", None), rows, rows, both, both, rows, both, both, rows)
        + (both,) * 7
        + (rows, both, P("dp", "mp"), P("mp", "dp"))
    )
    out_specs = (
        (rows, rows, rows, both, both, rows, both, both, rows)
        + (both,) * 7
        + (rows, both, P("dp", "mp"), P("mp", "dp"))
    )
    return jax.shard_map(local, mesh=mesh, in_specs=in_specs, out_specs=out_specs, check_vma=False)
```
